256 devices in a mesh: space: 64 (over x, z, core), dp: 4 (over y).
Axes of the slice: x: 4, y: 4, z: 8, core: 2. Of those that a mesh axis runs over, the one named last changes fastest.
Arguments:
- volume: bfloat16 [4, 64, 32, 8, 256], P('dp', 'space'), may hold values from -6 to 6
- tissue_kept: int32 [4, 64, 4], P('dp', 'space'), may hold values from 0 to 1, as said below
- filter_one: bfloat16 [864, 32], P('dp'), may hold values from -0.21875 to 0.21875
- filter_two: bfloat16 [864, 32], P('dp'), may hold values from -0.21875 to 0.21875
- cotangent: bfloat16 [4, 64, 32, 8, 256], P('dp', 'space'), may hold values from -6 to 6
Outputs:
- activations: bfloat16 [4, 64, 32, 8, 256], P('dp', 'space')
- input_grad: bfloat16 [4, 64, 32, 8, 256], P('dp', 'space')
- filter_grad_one: float32 [864, 32], P('dp')
- filter_grad_two: float32 [864, 32], P('dp')
The draws below stay inside these ranges and needn't reach their ends.
Inputs may be any that keep to these rules, and one draw needn't show every extreme that they name: tissue_kept[s, d, b] is 1 exactly when the block at x = d // 4 lies below the tissue height of its column, the column of y block 2 * ((d // 2) % 2) + b // 2 and z block 2 * (d % 2) + b % 2; each slab has 16 columns with heights of 1 to 16 blocks, the column of y block 3 and z block 3 of height 16, at least one other column under 16.
All inputs are finite; a program needn't handle non-finite values.
Results may differ from the reference program's by a relative error of at most 0.014.
Values may be sent and summed in bfloat16 or wider, within the bound.
A program may use at most 64 MiB of HBM per device.

```python
import math
import jax
import jax.numpy as jnp
from jax import lax

C = 32
BLOCK = 8
SLABS = 4
REGIONS = 64
XBLOCKS = 16
NX = 128
NY = 32


def draw_tissue_kept(key, part):
    key = jax.random.fold_in(key, 11)
    first, second = jax.random.split(key)
    heights = jax.random.randint(first, (SLABS, 16), 1, XBLOCKS + 1)
    shorter = jax.random.randint(second, (SLABS,), 0, 15)
    column = jnp.arange(16)[None, :]
    heights = jnp.where(column == shorter[:, None], max(XBLOCKS // 2, 1), heights)
    heights = jnp.where(column == 15, XBLOCKS, heights)
    heights = heights.reshape(SLABS, 4, 4)
    region = jnp.arange(REGIONS)
    region_x = region // 4
    region_y = region // 2 % 2
    region_z = region % 2
    local = jnp.arange(4)
    column_y = region_y[:, None] * 2 + local[None, :] // 2
    column_z = region_z[:, None] * 2 + local[None, :] % 2
    column_height = heights[:, column_y, column_z]
    return (region_x[None, :, None] < column_height).astype(jnp.int32)


def level_of(rng, dims, cuts, smallest, high):
    gain, own = 1.0, jax.random.fold_in(rng, 6)
    for axis_at, shards_of in cuts:
        draws = jnp.exp(jax.random.uniform(jax.random.fold_in(own, axis_at), (shards_of,), jnp.float32, smallest / len(cuts), high / len(cuts)))
        gain = gain * jnp.repeat(draws, dims[axis_at] // shards_of).reshape([-1 if axis == axis_at else 1 for axis in range(len(dims))])
    return gain


def centred(own_key, extent, scale, most, cuts=(), held_as=jnp.bfloat16):
    result = scale * jax.random.normal(own_key, extent, jnp.float32)
    if cuts:
        result = result * level_of(own_key, extent, cuts, -0.22, 0.18)
    return jnp.clip(result, -most, most).astype(held_as)


def setup_inputs(seed: int = 0) -> dict:
    streams_of = jax.random.split(jax.random.key(seed), 6)
    return {
        "volume": centred(streams_of[0], (SLABS, REGIONS, C, BLOCK, 4 * BLOCK * BLOCK), 1.0, 6.0, ((0, 4), (1, 64))),
        "tissue_kept": draw_tissue_kept(jax.random.fold_in(streams_of[5], 71), 0),
        "filter_one": centred(streams_of[2], (27 * C, C), (27 * C) ** -0.5, 0.21875, ((0, 4),)),
        "filter_two": centred(streams_of[3], (27 * C, C), (27 * C) ** -0.5, 0.21875, ((0, 4),)),
        "cotangent": centred(streams_of[4], (SLABS, REGIONS, C, BLOCK, 4 * BLOCK * BLOCK), 1.0, 6.0, ((0, 4), (1, 64))),
    }


NUMBERS = ('NCDHW', 'DHWIO', 'NCDHW')

def to_slab(blocks):
    grid_x = REGIONS // 4
    shaped = blocks.reshape(SLABS, grid_x, 2, 2, C, BLOCK, 2 * BLOCK, 2 * BLOCK)
    shaped = shaped.transpose(0, 4, 1, 5, 2, 6, 3, 7)
    return shaped.reshape(SLABS, C, NX, NY, NY)

def from_slab(whole_slab):
    grid_x = REGIONS // 4
    shaped = whole_slab.reshape(SLABS, C, grid_x, BLOCK, 2, 2 * BLOCK, 2, 2 * BLOCK)
    shaped = shaped.transpose(0, 2, 4, 6, 1, 3, 5, 7)
    return shaped.reshape(SLABS, REGIONS, C, BLOCK, 4 * BLOCK * BLOCK)

def cell_keep(tissue_kept):
    grid_x = REGIONS // 4
    shaped = tissue_kept.reshape(SLABS, grid_x, 2, 2, 2, 2).astype(jnp.float32)
    shaped = shaped.transpose(0, 1, 2, 4, 3, 5).reshape(SLABS, grid_x, 4, 4)
    cell_grid = jnp.broadcast_to(shaped[:, :, None, :, None, :, None], (SLABS, grid_x, BLOCK, 4, BLOCK, 4, BLOCK))
    return cell_grid.reshape(SLABS, NX, NY, NY)

def correlate(tensor, kernel):
    return lax.conv_general_dilated(tensor[None].astype(jnp.float32), kernel.astype(jnp.float32), (1, 1, 1), 'SAME', dimension_numbers=NUMBERS, precision=lax.Precision.HIGHEST)[0]

def flip_kernel(kernel):
    return kernel[::-1, ::-1, ::-1].transpose(0, 1, 2, 4, 3)

def silu_slope(values):
    logistic = jax.nn.sigmoid(values)
    return logistic + values * logistic * (1.0 - logistic)

def weight_grad(tensor, gradient):
    padded = jnp.pad(tensor.astype(jnp.float32), ((0, 0), (1, 1), (1, 1), (1, 1)))
    flat_grad = gradient.astype(jnp.float32).reshape(C, -1)
    tap_rows = []
    for shift_x in range(3):
        for shift_y in range(3):
            for shift_z in range(3):
                window = padded[:, shift_x:shift_x + NX, shift_y:shift_y + NY, shift_z:shift_z + NY].reshape(C, -1)
                tap_rows.append(jnp.dot(window, flat_grad.T, precision=lax.Precision.HIGHEST))
    return jnp.concatenate(tap_rows, axis=0)

def reference(volume, tissue_kept, filter_one, filter_two, cotangent):
    kernel_one = filter_one.reshape(3, 3, 3, C, C)
    kernel_two = filter_two.reshape(3, 3, 3, C, C)

    def one_slab(operands):
        tensor, keep_mask, upstream = operands
        source = (tensor.astype(jnp.float32) * keep_mask).astype(jnp.bfloat16)
        pre_one = correlate(source, kernel_one)
        act_one = (jax.nn.silu(pre_one) * keep_mask).astype(jnp.bfloat16)
        pre_two = correlate(act_one, kernel_two)
        output = (jax.nn.silu(pre_two) * keep_mask).astype(jnp.bfloat16)
        grad_two = (upstream.astype(jnp.float32) * keep_mask * silu_slope(pre_two)).astype(jnp.bfloat16)
        back_one = correlate(grad_two, flip_kernel(kernel_two))
        grad_one = (back_one * keep_mask * silu_slope(pre_one)).astype(jnp.bfloat16)
        back_input = (correlate(grad_one, flip_kernel(kernel_one)) * keep_mask).astype(jnp.bfloat16)
        return (output, back_input, weight_grad(source, grad_one), weight_grad(act_one, grad_two))
    output, back_input, stacked_one, stacked_two = lax.map(one_slab, (to_slab(volume), cell_keep(tissue_kept), to_slab(cotangent)))
    grad_scale = 1.0 / math.sqrt(SLABS * NX * NY * NY)
    filter_grad_one = lax.optimization_barrier(jnp.sum(stacked_one, axis=0)) * grad_scale
    filter_grad_two = lax.optimization_barrier(jnp.sum(stacked_two, axis=0)) * grad_scale
    return (from_slab(output), from_slab(back_input), filter_grad_one, filter_grad_two)
```

```python
import functools
import math

import jax
import jax.numpy as jnp
from jax import lax
from jax.experimental import pallas as pl
from jax.experimental.pallas import tpu as pltpu
from jax.sharding import PartitionSpec as P

MESH = pl.DeviceIdType.MESH
F32 = jnp.float32
BF16 = jnp.bfloat16

C = 32
CELLS = 256
ROWS = 256
EXT = 320
DEPTH = 9 * EXT
PAD = 2944
GROUP = 16

NN = (((1,), (0,)), ((), ()))
NT = (((1,), (1,)), ((), ()))


def dot(a, b, dims=NN):
    return lax.dot_general(a, b, dims, preferred_element_type=F32)


def iota(shape, axis):
    return lax.broadcasted_iota(jnp.int32, shape, axis)


def spread(cond):
    return jnp.where(cond, 1.0, 0.0).astype(BF16)


def pick(lane_group, parts):
    value = parts[-1]
    for g in range(len(parts) - 2, -1, -1):
        value = jnp.where(lane_group == g, parts[g], value)
    return value


def kernel(
    kept, filter_one, filter_two, volume, cotangent,
    act_out, gin_out, grad_one_out, grad_two_out,
    vin, cin, vout, own, faces, faces_in, edges_in, ext, beside, halo, shifted, banded,
    wsend, wrecv, wrows, wback, product, pile, scattered, summed, crossed, final, gathered,
    sel, expand, perm, perm_back,
    local_sem, out_sem, halo_send, halo_recv, filt_send, filt_recv,
    rs_send, rs_recv, xy_send, xy_recv, ag_send, ag_recv,
):
    space = lax.axis_index("space")
    dp = lax.axis_index("dp")
    count = lax.axis_size("space")
    rx, ry, rz = space // 4, (space // 2) % 2, space % 2
    block, zc = space // GROUP, space % GROUP
    xy = block * 4 + dp
    has_below, has_above = rx > 0, rx < count // 4 - 1

    loads = [
        pltpu.make_async_copy(volume.at[0, 0], vin, local_sem.at[0]),
        pltpu.make_async_copy(cotangent.at[0, 0], cin, local_sem.at[1]),
    ]
    for load in loads:
        load.start()

    base = space - 2 * ry - rz
    flips = (base + 2 * (1 - ry) + rz, base + 2 * ry + (1 - rz), base + 2 * (1 - ry) + (1 - rz))
    below = [lax.rem(d - 4 + count, count) for d in (space,) + flips]
    above = [lax.rem(d + 4, count) for d in (space,) + flips]
    zc_peers = [block * GROUP + lax.rem(zc + k, GROUP) for k in range(1, GROUP)]
    xy_slots = [lax.rem(xy + k, GROUP) for k in range(1, GROUP)]
    xy_peers = [((s // 4) * GROUP + zc, s % 4) for s in xy_slots]

    barrier = pltpu.get_barrier_semaphore()
    greeted = [(d, dp) for d in zc_peers] + xy_peers + [(d, dp) for d in below + above]
    for peer in greeted:
        pl.semaphore_signal(barrier, inc=1, device_id=peer, device_id_type=MESH)

    group = iota((1, 128), 1) // C
    within = iota((1, 128), 1) % C
    row = iota((CELLS, 128), 0)
    k = iota((CELLS, 128), 1) % C
    yb, zb = 15 * (1 - ry), 15 * (1 - rz)
    sel[...] = spread(((k < 16) & (row == yb * 16 + k)) | ((k >= 16) & (row == (k - 16) * 16 + zb)))

    row = iota((256, 256), 0)
    col = iota((256, 256), 1)
    perm[...] = spread(col == 8 * (row % C) + row // C)
    perm_back[...] = spread(row == 8 * (col % C) + col // C)
    k = row % C
    expand[:, :256] = spread(
        (row < 128) & (k >= 16) & (k - 16 == col // 16) & (col % 16 == 15 * (1 - rz))
    )
    row = iota((256, 128), 0)
    k = row % C
    z = iota((256, 128), 1) - 112 * (1 - ry)
    corner, beyond = 15 * rz, 16 - 17 * rz
    for oz in (-1, 0, 1):
        expand[:, 384 + 128 * oz : 512 + 128 * oz] = spread(
            (z >= 0) & (z < 16)
            & (((row < 128) & (k < 16) & (k == z + oz)) | ((row >= 128) & (k == corner) & (z + oz == beyond)))
        )
    zero = jnp.zeros((256, PAD), BF16)
    for f in range(4):
        banded[f] = zero
        shifted[f, DEPTH:PAD] = zero[: PAD - DEPTH, :CELLS]
    wrows[...] = jnp.zeros(wrows.shape, F32)

    repeat = spread(iota((C, 128), 1) % C == iota((C, 128), 0))
    for f, rows in enumerate((filter_one, filter_two)):
        wide = dot(rows[...], repeat)
        wide = jnp.concatenate([wide, jnp.zeros((8, 128), F32)], axis=0)
        packed = pick(group, [wide[56 * g : 56 * g + 56] for g in range(4)])
        packed = jnp.concatenate([packed, jnp.zeros((8, 128), F32)], axis=0).astype(BF16)
        wsend[f] = packed
        wrecv[f, dp] = packed

    cell = iota((1, CELLS), 1)
    tile = 2 * (cell // 128) + (cell % 16) // 8
    keep = jnp.zeros((1, CELLS), F32)
    for b in range(4):
        keep = jnp.where(tile == b, kept[0, 0, b].astype(F32), keep)

    def arrive(staged):
        return dot(perm[...], staged[...].astype(F32).reshape(ROWS, CELLS).astype(BF16))

    def halo_copies(r):
        peer = lambda d: (d, dp)
        copies = []

        def add(src, dst, d):
            i = len(copies)
            copies.append(
                pltpu.make_async_remote_copy(
                    src_ref=src, dst_ref=dst, send_sem=halo_send.at[r, i], recv_sem=halo_recv.at[r, i],
                    device_id=peer(d), device_id_type=MESH,
                )
            )

        add(own.at[r, 0:C], ext.at[r, EXT - C : EXT], below[0])
        add(own.at[r, ROWS - C : ROWS], ext.at[r, 0:C], above[0])
        for p in range(3):
            add(faces.at[r, 0], edges_in.at[r, 1, p], below[1 + p])
            add(faces.at[r, 1], edges_in.at[r, 0, p], above[1 + p])
        for p in range(3):
            add(faces.at[r], faces_in.at[r, p], flips[p])
        return copies

    def give(r, field):
        own[r] = field
        border = dot(field, sel[...])
        for v in range(2):
            faces[r, v] = pick(group, [border[128 * v + C * g : 128 * v + C * g + C] for g in range(4)]).astype(BF16)
        copies = halo_copies(r)
        for copy in copies:
            copy.start()
        ext[r, C : EXT - C] = field
        return copies

    def take(r, copies):
        for copy in copies:
            copy.wait_recv()
        none = jnp.zeros((C, 128), F32)
        for side, there, g, lo in ((0, has_below, 3, 0), (1, has_above, 0, EXT - C)):
            ext[r, lo : lo + C] = jnp.where(there, ext[r, lo : lo + C].astype(F32), 0.0).astype(BF16)
            by_y, by_z, by_yz = (edges_in[r, side, p].astype(F32) for p in range(3))
            here = there & (group == g)
            beside[lo : lo + C, :128] = jnp.where(here, jnp.where(within < 16, by_y, by_z), none).astype(BF16)
            beside[lo : lo + C, 128:] = jnp.where(here, by_yz, none).astype(BF16)
        for v in range(2):
            by_y, by_z, by_yz = (faces_in[r, p, v].astype(F32) for p in range(3))
            by_yz_ = by_yz
            both = jnp.where(within < 16, by_y, by_z)
            for g in range(4):
                lo = C * (1 + 4 * v + g)
                beside[lo : lo + C, :128] = jnp.where(group == g, both, none).astype(BF16)
                beside[lo : lo + C, 128:] = jnp.where(group == g, by_yz_, none).astype(BF16)
        halo[...] = dot(beside[...], expand[...])
        lane = iota((1, 128), 1)

        def rows_of(i, carry):
            rows = pl.ds(pl.multiple_of(i * C, C), C)
            u = [ext[r, rows, 128 * v : 128 * v + 128].astype(F32) for v in range(2)]
            for oz in (-1, 0, 1):
                if oz == 0:
                    s = u
                else:
                    edge = lane % 16 == (15 if oz == 1 else 0)
                    s = [
                        jnp.where(edge, halo[rows, 128 * v : 128 * v + 128], pltpu.roll(u[v], (-oz) % 128, 1))
                        for v in range(2)
                    ]
                beyond_y = halo[rows, 384 + 128 * oz : 512 + 128 * oz]
                up = [pltpu.roll(s[v], 112, 1) for v in range(2)]
                down = [pltpu.roll(s[v], 16, 1) for v in range(2)]
                results = (
                    (jnp.where(lane < 16, beyond_y, down[0]), jnp.where(lane < 16, down[0], down[1])),
                    s,
                    (jnp.where(lane >= 112, up[1], up[0]), jnp.where(lane >= 112, beyond_y, up[1])),
                )
                for oy in range(3):
                    at = pl.ds(pl.multiple_of((oy * 3 + oz + 1) * EXT + i * C, C), C)
                    for v in range(2):
                        shifted[r, at, 128 * v : 128 * v + 128] = results[oy][v].astype(BF16)
            return carry

        lax.fori_loop(0, 10, rows_of, 0)

    def filter_rows(f):
        for g8 in range(108):
            tap, b = g8 // 4, g8 % 4
            src, rr = g8 // 27, g8 % 27
            g, r = rr // 7, rr % 7
            ox, t = tap // 9, tap % 9
            part = wrecv[f, src, 16 * (r // 2) : 16 * (r // 2) + 16].astype(F32)[8 * (r % 2) : 8 * (r % 2) + 8]
            wrows[t * 128 + ox * C + 8 * b : t * 128 + ox * C + 8 * b + 8] = jnp.where(group == g, part, 0.0)

    def band(slot, t, value):
        lane = iota((1, 128), 1)
        for turn in (0, 32, 64, 96):
            turned = value if turn == 0 else pltpu.roll(value, turn, 1)
            for xo in range(8):
                at = t * EXT + C * xo
                if at % 128 != turn:
                    continue
                v = at // 128
                rows = slice(C * xo, C * xo + C)
                if turn <= 32:
                    banded[slot, rows, 128 * v : 128 * v + 128] = turned.astype(BF16)
                else:
                    banded[slot, rows, 128 * v : 128 * v + 128] = jnp.where(lane >= turn, turned, 0.0).astype(BF16)
                    banded[slot, rows, 128 * v + 128 : 128 * v + 256] = jnp.where(lane < turn, turned, 0.0).astype(BF16)

    def band_forward(f):
        eye = spread(iota((C, 128), 1) % C == iota((C, 128), 0))
        turned = dot(eye, wrows[...].astype(BF16), NT)
        for t in range(9):
            band(f, t, turned[:, 128 * t : 128 * t + 128])

    def band_back(f):
        lanes = iota((128, 128), 1)
        ins = iota((128, 128), 0) % C
        for t in range(9):
            value = None
            for ox in range(3):
                place = spread(lanes == C * (2 - ox) + ins)
                part = dot(wrows[t * 128 + ox * C : t * 128 + ox * C + C].astype(BF16), place)
                value = part if value is None else value + part
            band(2 + f, 8 - t, value)

    def conv(slot, r):
        return dot(banded[slot], shifted[r])

    def logistic(v):
        return 1.0 / (1.0 + jnp.exp(-v))

    def depart(slot, field, out):
        vout[slot] = dot(perm_back[...], field).reshape(C, 8, CELLS).astype(BF16)
        copy = pltpu.make_async_copy(vout.at[slot], out.at[0, 0], out_sem.at[slot])
        copy.start()
        return copy

    def filter_gradient(f, r, gradient):
        product[...] = dot(shifted[r, 0:DEPTH], gradient, NT)

        def term(g8):
            tap, b = g8 // 4, g8 % 4
            ox, t = tap // 9, tap % 9
            halves = []
            for v in range(2):
                parts = []
                for g in range(4):
                    at = t * EXT + (4 * v + g + ox) * C + 8 * b
                    parts.append(product[at : at + 8, 128 * v : 128 * v + 128])
                halves.append(pick(group, parts))
            return halves[0] + halves[1]

        odd, high = group % 2 == 1, group >= 2
        tiles = []
        for rr in range(27):
            a = [term(27 * y + rr) for y in range(4)]
            pairs = [
                jnp.where(odd, a[i + 1], a[i]) + pltpu.roll(jnp.where(odd, a[i], a[i + 1]), 32, 1) for i in (0, 2)
            ]
            tiles.append(
                jnp.where(high, pairs[1], pairs[0]) + pltpu.roll(jnp.where(high, pairs[0], pairs[1]), 64, 1)
            )
        tiles.append(jnp.zeros((8, 128), F32))
        for j in range(14):
            pile[f, j] = jnp.concatenate(tiles[2 * j : 2 * j + 2], axis=0).astype(BF16)
        for j in range(14, GROUP):
            pile[f, j] = jnp.zeros((16, 128), BF16)

    def scatter(f):
        copies = []
        for i, d in enumerate(zc_peers):
            copies.append(
                pltpu.make_async_remote_copy(
                    src_ref=pile.at[f, lax.rem(zc + i + 1, GROUP)], dst_ref=scattered.at[f, i],
                    send_sem=rs_send.at[f, i], recv_sem=rs_recv.at[f, i], device_id=(d, dp), device_id_type=MESH,
                )
            )
            copies[-1].start()
        return copies

    def collect(f, copies):
        total = pile[f, zc].astype(F32)
        for i, copy in enumerate(copies):
            copy.wait_recv()
            total = total + scattered[f, i].astype(F32)
        return total

    dp_peers = [(space, lax.rem(dp + i, 4)) for i in range(1, 4)]
    loads[0].wait()
    source = (arrive(vin) * keep).astype(BF16)

    pl.semaphore_wait(barrier, len(greeted))

    moves = []
    for f in range(2):
        row_moves = []
        for i, peer in enumerate(dp_peers):
            row_moves.append(
                pltpu.make_async_remote_copy(
                    src_ref=wsend.at[f], dst_ref=wrecv.at[f, dp], send_sem=filt_send.at[f, i],
                    recv_sem=filt_recv.at[f, i], device_id=peer, device_id_type=MESH,
                )
            )
        moves.append(row_moves)
    for move in moves[0]:
        move.start()
    sent = give(0, source)
    for move in moves[1]:
        move.start()
    halos = [sent]

    loads[1].wait()
    upstream = arrive(cin) * keep

    for move in moves[0]:
        move.wait_recv()
    filter_rows(0)
    band_forward(0)
    take(0, halos[0])
    pre_one = conv(0, 0)
    gate_one = logistic(pre_one)
    halos.append(give(1, (pre_one * gate_one * keep).astype(BF16)))
    slope_one = (gate_one + pre_one * gate_one * (1.0 - gate_one)) * keep

    band_back(0)
    for move in moves[1]:
        move.wait_recv()
    filter_rows(1)
    band_forward(1)
    take(1, halos[1])
    pre_two = conv(1, 1)
    gate_two = logistic(pre_two)
    grad_two = (upstream * (gate_two + pre_two * gate_two * (1.0 - gate_two))).astype(BF16)
    halos.append(give(2, grad_two))
    outs = [depart(0, (pre_two * gate_two * keep).astype(BF16), act_out)]
    band_back(1)
    filter_gradient(1, 1, grad_two)
    piles_two = scatter(1)
    take(2, halos[2])
    grad_one = (conv(3, 2) * slope_one).astype(BF16)
    halos.append(give(3, grad_one))
    filter_gradient(0, 0, grad_one)
    piles_one = scatter(0)
    total_two = collect(1, piles_two)
    take(3, halos[3])
    outs.append(depart(1, (conv(2, 3) * keep).astype(BF16), gin_out))
    total_one = collect(0, piles_one)

    parts = [total_one[:8], total_one[8:], total_two[:8], total_two[8:]]
    odd, high = group % 2 == 1, group >= 2
    one_up = lambda v: pltpu.roll(v, 32, 1)
    one_down = lambda v: pltpu.roll(v, 96, 1)
    half = []
    for i in (0, 2):
        half.append(
            (jnp.where(odd, one_up(parts[i + 1]), parts[i]), jnp.where(odd, parts[i + 1], one_down(parts[i])))
        )
    for i in range(2):
        lo, hi = half[0][i], half[1][i]
        summed[i] = jnp.where(high, pltpu.roll(hi, 64, 1), lo)
        summed[2 + i] = jnp.where(high, hi, pltpu.roll(lo, 64, 1))

    crossing = []
    for i, ((d, y), _) in enumerate(zip(xy_peers, xy_slots)):
        crossing.append(
            pltpu.make_async_remote_copy(
                src_ref=summed.at[y], dst_ref=crossed.at[i], send_sem=xy_send.at[i], recv_sem=xy_recv.at[i],
                device_id=(d, y), device_id_type=MESH,
            )
        )
        crossing[-1].start()
    total = summed[dp]
    for i, copy in enumerate(crossing):
        copy.wait_recv()
        total = total + crossed[i]
    total = total * (1.0 / math.sqrt(4 * count * 2048))
    final[...] = total
    gathered[zc] = total
    spreading = []
    for i, d in enumerate(zc_peers):
        spreading.append(
            pltpu.make_async_remote_copy(
                src_ref=final, dst_ref=gathered.at[zc], send_sem=ag_send.at[i], recv_sem=ag_recv.at[i],
                device_id=(d, dp), device_id_type=MESH,
            )
        )
        spreading[-1].start()
    for copy in spreading:
        copy.wait_recv()
    for j in range(14):
        value = gathered[j]
        for h in range(2):
            if j == 13 and h == 1:
                continue
            at = 16 * j + 8 * h
            lo = value if h == 0 else pltpu.roll(value, 96, 1)
            grad_one_out[at : at + 8, :] = lo[:, :C]
            grad_two_out[at : at + 8, :] = pltpu.roll(value, 64 - 32 * h, 1)[:, :C]

    for copy in outs:
        copy.wait()
    for copies in halos + moves + [piles_one, piles_two, crossing, spreading]:
        for copy in copies:
            copy.wait_send()


def on_device(volume, tissue_kept, filter_one, filter_two, cotangent):
    vmem, anywhere = pl.BlockSpec(memory_space=pltpu.VMEM), pl.BlockSpec(memory_space=pl.ANY)
    dma = pltpu.SemaphoreType.DMA
    field = jax.ShapeDtypeStruct(volume.shape, BF16)
    grad = jax.ShapeDtypeStruct(filter_one.shape, F32)
    return pl.pallas_call(
        kernel,
        out_shape=(field, field, grad, grad),
        in_specs=[pl.BlockSpec(memory_space=pltpu.SMEM), vmem, vmem, anywhere, anywhere],
        out_specs=(anywhere, anywhere, vmem, vmem),
        scratch_shapes=[
            pltpu.VMEM((C, 8, CELLS), BF16),
            pltpu.VMEM((C, 8, CELLS), BF16),
            pltpu.VMEM((2, C, 8, CELLS), BF16),
            pltpu.VMEM((4, ROWS, CELLS), BF16),
            pltpu.VMEM((4, 2, C, 128), BF16),
            pltpu.VMEM((4, 3, 2, C, 128), BF16),
            pltpu.VMEM((4, 2, 3, C, 128), BF16),
            pltpu.VMEM((4, EXT, CELLS), BF16),
            pltpu.VMEM((EXT, 256), BF16),
            pltpu.VMEM((EXT, 640), F32),
            pltpu.VMEM((4, PAD, CELLS), BF16),
            pltpu.VMEM((4, ROWS, PAD), BF16),
            pltpu.VMEM((2, 64, 128), BF16),
            pltpu.VMEM((2, 4, 64, 128), BF16),
            pltpu.VMEM((9 * 128, 128), F32),
            pltpu.VMEM((8, 128), F32),
            pltpu.VMEM((DEPTH, CELLS), F32),
            pltpu.VMEM((2, GROUP, 16, 128), BF16),
            pltpu.VMEM((2, GROUP - 1, 16, 128), BF16),
            pltpu.VMEM((4, 8, 128), F32),
            pltpu.VMEM((GROUP - 1, 8, 128), F32),
            pltpu.VMEM((8, 128), F32),
            pltpu.VMEM((GROUP, 8, 128), F32),
            pltpu.VMEM((CELLS, 128), BF16),
            pltpu.VMEM((256, 640), BF16),
            pltpu.VMEM((256, 256), BF16),
            pltpu.VMEM((256, 256), BF16),
            dma((2,)), dma((2,)), dma((4, 11)), dma((4, 11)), dma((2, 3)), dma((2, 3)),
            dma((2, GROUP - 1)), dma((2, GROUP - 1)), dma((GROUP - 1,)), dma((GROUP - 1,)),
            dma((GROUP - 1,)), dma((GROUP - 1,)),
        ],
        compiler_params=pltpu.CompilerParams(
            collective_id=0, has_side_effects=True, vmem_limit_bytes=48 * 1024 * 1024
        ),
    )(tissue_kept, filter_one, filter_two, volume, cotangent)


def solution(mesh):
    field, rows = P("dp", "space", None, None, None), P("dp", None)
    return jax.shard_map(
        on_device,
        mesh=mesh,
        in_specs=(field, P("dp", "space", None), rows, rows, field),
        out_specs=(field, field, rows, rows),
        check_vma=False,
    )
```

```python
import math

import jax
import jax.numpy as jnp
from jax import lax
from jax.experimental import pallas as pl
from jax.experimental.pallas import tpu as pltpu
from jax.sharding import PartitionSpec as P

MESH = pl.DeviceIdType.MESH
F32 = jnp.float32
BF16 = jnp.bfloat16
NN = (((1,), (0,)), ((), ()))
NT = (((1,), (1,)), ((), ()))
TN = (((0,), (0,)), ((), ()))

C = 32
GONE = 64.0
STARTS = (0, 6, 13, 20)


def dot(a, b, dims=NN):
    return lax.dot_general(a, b, dims, preferred_element_type=F32)


def iota(shape, axis):
    return lax.broadcasted_iota(jnp.int32, shape, axis)


def ones_at(cond):
    return jnp.where(cond, 1.0, 0.0).astype(BF16)


def pick(group, parts):
    value = None
    for g in range(len(parts) - 1, -1, -1):
        part = 0.0 if parts[g] is None else parts[g]
        if value is None:
            value = part
        elif not (parts[g] is None and isinstance(value, float)):
            value = jnp.where(group == g, part, value)
    return value


def logistic(v):
    return 1.0 / (1.0 + jnp.exp(-v))


def tiles(count, body, unroll=3):
    def step(i, carry):
        for u in range(unroll):
            body(pl.multiple_of((i * unroll + u) * 16, 16))
        return carry

    lax.fori_loop(0, count // unroll, step, 0)
    for i in range(count // unroll * unroll, count):
        body(i * 16)


def layout(h):
    yrows = 32 if h == 3 else 16
    low, high, beyond = 128, 128 + 16 * h, 128 + 32 * h
    return yrows, low, high, beyond, beyond + yrows, beyond + yrows + 16, beyond + yrows + 32


def kernel(
    kept, filter_one, filter_two, volume, cotangent,
    act_out, gin_out, grad_one_out, grad_two_out,
    vin, cin, vout, spread, nat, nat_main, nat_z, face_main, face_z, stack_main, stack_z,
    blk, cot, keep, slope, pre, shifted, bands, leaving, owned, wide,
    wsend, wrecv, wrows, rep, product, tap_tile, pile, pair_in, crossing, xy_in, z_in, xc_in, final,
    turn, copies8, sel3, sel1, rows3, rows1, place0, place1, place2, pack, unplace, inside,
    local_sem, out_sem, halo_send, halo_recv, filt_send, filt_recv,
    pair_send, pair_recv, xy_send, xy_recv, z_send, z_recv, xc_send, xc_recv,
):
    space = lax.axis_index("space")
    dp = lax.axis_index("dp")
    count = lax.axis_size("space")
    rx, ry, rz = space // 4, (space // 2) % 2, space % 2
    bx, pz = space // 16, (space // 2) % 8
    has_below, has_above = rx > 0, rx < count // 4 - 1
    started = []

    loads = [
        pltpu.make_async_copy(volume.at[0, 0], vin, local_sem.at[0]),
        pltpu.make_async_copy(cotangent.at[0, 0], cin, local_sem.at[1]),
    ]
    for load in loads:
        load.start()

    def send(src, dst, sems, at, peer):
        copy = pltpu.make_async_remote_copy(
            src_ref=src, dst_ref=dst, send_sem=sems[0].at[at], recv_sem=sems[1].at[at],
            device_id=peer, device_id_type=MESH,
        )
        copy.start()
        started.append(copy)
        return copy

    base = space - 2 * ry - rz
    column = (space, base + 2 * (1 - ry) + rz, base + 2 * ry + (1 - rz), base + 2 * (1 - ry) + (1 - rz))
    below = [lax.rem(d - 4 + count, count) for d in column]
    above = [lax.rem(d + 4, count) for d in column]
    xy = bx * 4 + dp
    xy_slots = [lax.rem(xy + k, 16) for k in range(1, 16)]
    xy_peers = [((s // 4) * 16 + lax.rem(space, 16), s % 4) for s in xy_slots]
    z_peers = [(bx * 16 + 2 * lax.rem(pz + k, 8) + rz, dp) for k in range(1, 8)]
    xc = rz * 4 + bx
    xc_slots = [lax.rem(xc + k, 8) for k in range(1, 8)]
    xc_peers = [((s % 4) * 16 + 2 * pz + s // 4, dp) for s in xc_slots]
    dp_peers = [(space, lax.rem(dp + k, 4)) for k in range(1, 4)]

    barrier = pltpu.get_barrier_semaphore()
    greeted = [(d, dp) for d in column[1:]] + [(d, dp) for d in below + above] + xy_peers + z_peers + xc_peers
    for peer in greeted:
        pl.semaphore_signal(barrier, inc=1, device_id=peer, device_id_type=MESH)

    group = iota((1, 128), 1) // C

    row, col = iota((256, 256), 0), iota((256, 256), 1)
    y, z = row % 16, row // 16
    turn[...] = ones_at(col == 16 * jnp.where(ry == 0, y, 15 - y) + jnp.where(rz == 0, z, 15 - z))
    row, col = iota((256, 128), 0), iota((256, 128), 1)
    for x in range(8):
        copies8[:, 128 * x : 128 * x + 128] = ones_at(row == 8 * (col % C) + x)

    def faces_of(h):
        row, col = iota((32 * h, 128), 0), iota((32 * h, 128), 1)
        y, x = col // 8, col % 8
        return ones_at(
            ((x < h) & (row == h * y + x)) | ((x >= 8 - h) & (row == 16 * h + h * y + x - (8 - h)))
        )

    sel3[...] = faces_of(3)

    cell = iota((1, 256), 1)
    tile = 2 * (cell // 128) + (cell % 16) // 8
    kept_cells = jnp.zeros((1, 256), F32)
    for b in range(4):
        kept_cells = jnp.where(tile == b, kept[0, 0, b].astype(F32), kept_cells)

    def turn_in(f, field):
        cells = dot(turn[...], field.astype(BF16), NT).astype(BF16)
        spread[...] = dot(cells, copies8[...])
        for x in range(8):
            for w in range(5):
                layers = [4 * w + g for g in range(4)] if w < 4 else [None, 15, 14, 13]
                parts = [None if l is None else spread[16 * l : 16 * l + 16, 128 * x : 128 * x + 128] for l in layers]
                nat[w, pl.ds(x, 16, stride=8), :] = pick(group, parts)
        return jnp.concatenate([nat[w] for w in range(5)], axis=1).astype(BF16)

    def give(f, h, sel, field):
        yrows, low, high, beyond, corner_low, corner_high, _ = layout(h)
        main, last = field[:, :512], field[:, 512:]
        nat_main[f] = main
        nat_z[f] = last
        faces = dot(sel, field).astype(BF16)
        for side in range(2):
            face_main[f, side, 0 : 16 * h] = faces[16 * h * side : 16 * h * side + 16 * h, :512]
            face_z[f, side, 0 : 16 * h] = faces[16 * h * side : 16 * h * side + 16 * h, 512:]
        moves = []

        def add(src, dst, d):
            moves.append(send(src, dst, (halo_send, halo_recv), (f, len(moves)), (d, dp)))

        ends = ((1, low, corner_low, above), (0, high, corner_high, below))
        for side, at, _, to in ends:
            add(face_main.at[f, side, 0 : 16 * h], stack_main.at[f, at : at + 16 * h], to[0])
        for side, at, corner, to in ends:
            add(face_z.at[f, side, 0 : 16 * h], stack_z.at[f, at : at + 16 * h], to[2])
            add(face_main.at[f, side, 16 * h - 16 : 16 * h], stack_main.at[f, corner : corner + 16], to[1])
            add(face_z.at[f, side, 16 * h - 16 : 16 * h], stack_z.at[f, corner : corner + 16], to[3])
        add(nat_main.at[f, 128 - yrows : 128], stack_main.at[f, beyond : beyond + yrows], column[1])
        add(nat_z.at[f, 128 - yrows : 128], stack_z.at[f, beyond : beyond + yrows], column[3])
        add(nat_z.at[f], stack_z.at[f, 0:128], column[2])
        stack_main[f, 0:128] = main
        return moves

    def assemble(h):
        yrows, low, high, beyond, corner_low, corner_high, total = layout(h)
        row, col = iota((304, total), 0), iota((304, total), 1)
        y, x = row // 16, row % 16 - 4
        mid, lo, hi = (x >= 0) & (x < 8), (x < 0) & (x >= -h), (x >= 8) & (x < 8 + h)
        own, far = y < 16, (y >= 16) & (y < 16 + h)
        first, there = 16 - yrows // 8, 31 - y
        skip = 16 * h - 16
        at = jnp.where(own & mid, 8 * y + x, -1)
        at = jnp.where(own & lo, low + h * y + x + h, at)
        at = jnp.where(own & hi, high + h * y + x - 8, at)
        at = jnp.where(far & mid, beyond + 8 * (there - first) + x, at)
        at = jnp.where(far & lo, corner_low + h * there + x + h - skip, at)
        at = jnp.where(far & hi, corner_high + h * there + x - 8 - skip, at)
        return ones_at(at == col)

    def take(f, h, rows, moves):
        for move in moves:
            move.wait_recv()
        total = layout(h)[-1]
        pieces = jnp.concatenate([stack_main[f, 0:total], stack_z[f, 0:total]], axis=1)
        whole = dot(rows, pieces).astype(BF16)
        return (
            dot(whole[:, 0:256], place0[...]), dot(whole[:, 128:512], place1[...]), dot(whole[:, 256:640], place2[...])
        )

    def put(f, b, v, r0, value):
        lanes = slice(128 * v, 128 * v + 128)
        at = pl.ds(r0 + 16, 16)
        shifted[f, 1, b, at, lanes] = value.astype(BF16)
        shifted[f, 0, b, at, lanes] = pltpu.roll(value, 1, 0).astype(BF16)
        shifted[f, 2, b, at, lanes] = pltpu.roll(value, 15, 0).astype(BF16)

    def put_all(f, r0, parts):
        for b in range(3):
            lo, hi = parts[b]
            lo = jnp.where(group == 0, pltpu.roll(parts[b - 1][1], 64, 1) if b > 0 else 0.0, lo)
            hi = jnp.where(group == 3, pltpu.roll(parts[b + 1][0], 64, 1) if b < 2 else 0.0, hi)
            put(f, b, 0, r0, lo)
            put(f, b, 1, r0, hi)

    def inputs_of(f, ox, oy, ny):
        return shifted[f, ox, :, 16 * oy : 16 * oy + 16 * ny].reshape(48 * ny, 256)

    def conv(f, slot, ny, back):
        lhs = jnp.concatenate([inputs_of(f, ox, oy, ny) for ox in range(3) for oy in range(3)], axis=1)
        if back:
            rhs, dims = jnp.concatenate([bands[slot, t] for t in range(9)], axis=1), NT
        else:
            rhs, dims = bands[slot].reshape(9 * 256, 256), NN
        pre[:, 0 : 16 * ny] = dot(lhs, rhs, dims).reshape(3, 16 * ny, 256)

    def send_rows(f, rows):
        square = ones_at(iota((216, 216), 0) == iota((216, 216), 1))
        four = jnp.concatenate([rows[...]] * 4, axis=0)
        full = jnp.concatenate([dot(square, four, NT), jnp.zeros((8, 128), F32)], axis=0)
        packed = pick(group, [full[56 * g : 56 * g + 56] for g in range(4)])
        packed = jnp.concatenate([packed, jnp.zeros((8, 128), F32)], axis=0).astype(BF16)
        wsend[f] = packed
        wrecv[f, dp] = packed

    def share_rows(f):
        return [
            send(wsend.at[f], wrecv.at[f, dp], (filt_send, filt_recv), (f, i), peer) for i, peer in enumerate(dp_peers)
        ]

    def filter_rows(f):
        for g8 in range(108):
            src, rr = g8 // 27, g8 % 27
            g, r = rr // 7, rr % 7
            part = wrecv[f, src, 16 * (r // 2) : 16 * (r // 2) + 16].astype(F32)[8 * (r % 2) : 8 * (r % 2) + 8]
            wrows[8 * g8 : 8 * g8 + 8] = jnp.where(group == g, part, 0.0)
        again = ones_at(iota((128, 128), 0) % C == iota((128, 128), 1) % C)
        rep[f] = dot(wrows[...].astype(BF16), again).reshape(27, C, 128)

    def tap(ox, oy, oz):
        ty = oy if oy == 1 else jnp.where(ry == 0, oy, 2 - oy)
        tz = oz if oz == 1 else jnp.where(rz == 0, oz, 2 - oz)
        return 9 * ox + 3 * ty + tz

    def band(f):
        for ox in range(3):
            for oy in range(3):
                taps = [rep[f, tap(ox, oy, oz)] for oz in range(3)]
                for v in range(2):
                    for zi in range(8):
                        parts = []
                        for g in range(4):
                            zo = 4 * v + g
                            parts.append(taps[zi - zo + 1] if 1 <= zo <= 6 and abs(zi - zo) <= 1 else None)
                        if any(p is not None for p in parts):
                            value = pick(group, parts).astype(BF16)
                        else:
                            value = jnp.zeros((C, 128), BF16)
                        bands[f, 3 * ox + oy, C * zi : C * zi + C, 128 * v : 128 * v + 128] = value

    def band_back(f):
        for sx in range(3):
            for sy in range(3):
                taps = [rep[f, tap(2 - sx, 2 - sy, oz)] for oz in range(3)]
                for v in range(2):
                    for zo in range(8):
                        parts = []
                        for g in range(4):
                            zi = 4 * v + g
                            parts.append(taps[zo - zi + 1] if 1 <= zo <= 6 and abs(zi - zo) <= 1 else None)
                        if any(p is not None for p in parts):
                            value = pick(group, parts).astype(BF16)
                        else:
                            value = jnp.zeros((C, 128), BF16)
                        bands[2 + f, 3 * sx + sy, C * zo : C * zo + C, 128 * v : 128 * v + 128] = value

    def natural(blocked):
        rows = jnp.concatenate([dot(pack[...], blocked[b]) for b in range(3)], axis=1).astype(BF16)
        return dot(rows, unplace[...])

    def depart(slot, field, out):
        for w in range(4):
            nat[w] = field[:, 128 * w : 128 * w + 128]
        for x in range(8):
            for w in range(4):
                value = nat[w, pl.ds(x, 16, stride=8), :]
                for g in range(4):
                    at = 16 * (4 * w + g)
                    wide[at : at + 16, 128 * x : 128 * x + 128] = jnp.where(group == g, value, 0.0).astype(BF16)
        cells = dot(copies8[...], wide[...], NT).astype(BF16)
        vout[slot] = dot(cells, turn[...]).reshape(C, 8, 256).astype(BF16)
        copy = pltpu.make_async_copy(vout.at[slot], out.at[0, 0], out_sem.at[slot])
        copy.start()
        return copy

    def filter_gradient(f, r):
        gradient = owned[f].reshape(768, 256)
        odd, high = group % 2 == 1, group >= 2
        for t in range(9):
            product[t] = dot(gradient, inputs_of(r, t // 3, t % 3, 16), TN)
        for t in range(9):
            for oz in range(3):
                a = []
                for j in range(4):
                    halves = []
                    for v in range(2):
                        parts = []
                        for g in range(4):
                            zo = 4 * v + g - (oz - 1)
                            at = zo * C + 8 * j
                            parts.append(product[t, at : at + 8, 128 * v : 128 * v + 128] if 1 <= zo <= 6 else None)
                        halves.append(pick(group, parts))
                    a.append(halves[0] + halves[1])
                pairs = [
                    jnp.where(odd, a[i + 1], a[i]) + pltpu.roll(jnp.where(odd, a[i], a[i + 1]), 32, 1) for i in (0, 2)
                ]
                tap_tile[f, tap(t // 3, t % 3, oz)] = jnp.where(high, pairs[1], pairs[0]) + pltpu.roll(
                    jnp.where(high, pairs[0], pairs[1]), 64, 1
                )
        for q in range(4):
            for k in range(8):
                source = STARTS[q] + k
                pile[f, k // 4, 4 * (k % 4) + q] = (
                    tap_tile[f, source] if source < 27 else jnp.zeros((8, 128), F32)
                )
        return send(pile.at[f, 1 - rz], pair_in.at[f], (pair_send, pair_recv), f, (column[2], dp))

    loads[0].wait()
    field = jnp.where(kept_cells > 0.5, vin[...].astype(F32).reshape(256, 256), GONE)
    field = turn_in(0, field)
    pl.semaphore_wait(barrier, len(greeted))
    volume_moves = give(0, 3, sel3[...], field)

    send_rows(0, filter_one)
    row_moves = [share_rows(0)]
    send_rows(1, filter_two)
    row_moves.append(share_rows(1))

    sel1[...] = faces_of(1)
    loads[1].wait()
    cot_moves = give(1, 1, sel1[...], turn_in(1, cin[...].astype(F32).reshape(256, 256)))

    rows3[...] = assemble(3)
    rows1[...] = assemble(1)
    k, n = iota((256, 256), 0), iota((256, 256), 1)
    place0[...] = ones_at(n - k == C)
    k, n = iota((384, 256), 0), iota((384, 256), 1)
    place1[...] = ones_at(k - n == C)
    place2[...] = ones_at(k - n == jnp.where(n < 160, 96, 128))
    row, col = iota((128, 256), 0), iota((128, 256), 1)
    pack[...] = ones_at(col == 16 * (row // 8) + row % 8 + 4)
    for b in range(3):
        k, n = iota((256, 640), 0), iota((256, 640), 1)
        zi, z = k // C, 6 * b + k // C - 1
        good = (zi >= 1) & (zi <= 6) & (z < 16) & (k % C == n % C)
        unplace[256 * b : 256 * b + 256] = ones_at(
            good & (((n < 512) & (n // C == z)) | ((n >= 544) & (16 - (n // C - 16) == z)))
        )
    x = iota((304, 128), 0) % 16 - 4
    inside[...] = jnp.where(((x < 0) & ~has_below) | ((x >= 8) & ~has_above), 0.0, 1.0)
    for f in range(4):
        for ox in range(3):
            for b in range(3):
                shifted[f, ox, b, 0:16] = jnp.zeros((16, 256), BF16)

    for f in range(2):
        for move in row_moves[f]:
            move.wait_recv()
        filter_rows(f)
        band(f)
        band_back(f)

    for b, value in enumerate(take(0, 3, rows3[...], volume_moves)):
        blk[b] = value

    def first(r0):
        rows = pl.ds(r0, 16)
        here = inside[rows, :]
        for b in range(3):
            for v in range(2):
                lanes = slice(128 * v, 128 * v + 128)
                value = blk[b, rows, lanes]
                kept_here = jnp.where(value == GONE, 0.0, here)
                keep[b, rows, lanes] = kept_here
                put(0, b, v, r0, value * kept_here)

    tiles(19, first)
    conv(0, 0, 18, False)

    def second(r0):
        rows = pl.ds(r0, 16)
        parts = []
        for b in range(3):
            parts.append([])
            for v in range(2):
                lanes = slice(128 * v, 128 * v + 128)
                value, there = pre[b, rows, lanes], keep[b, rows, lanes]
                gate = logistic(value)
                slope[b, rows, lanes] = (gate + value * gate * (1.0 - gate)) * there
                parts[b].append(value * gate * there)
        put_all(1, r0, parts)

    tiles(18, second)
    conv(1, 1, 17, False)
    for b, value in enumerate(take(1, 1, rows1[...], cot_moves)):
        cot[b] = value
    x = iota((16, 128), 0) - 4
    own = [jnp.where((x >= 0) & (x < 8), 1.0, 0.0)]
    own.append(jnp.where(group == 0, own[0], 0.0))

    def third(r0, last=False):
        rows = pl.ds(r0, 16)
        parts = []
        for b in range(3):
            parts.append([])
            for v in range(2):
                lanes = slice(128 * v, 128 * v + 128)
                value, there = pre[b, rows, lanes], keep[b, rows, lanes]
                gate = logistic(value)
                grad = cot[b, rows, lanes] * there * (gate + value * gate * (1.0 - gate))
                parts[b].append(grad)
                if not last:
                    leaving[b, rows, lanes] = (value * gate * there).astype(BF16)
                    owned[1, b, rows, lanes] = (grad * own[b * v // 2]).astype(BF16)
        put_all(2, r0, parts)

    tiles(16, third, 2)
    third(256, True)
    conv(2, 3, 16, True)

    def fourth(r0):
        rows = pl.ds(r0, 16)
        for b in range(3):
            for v in range(2):
                lanes = slice(128 * v, 128 * v + 128)
                grad = pre[b, rows, lanes] * slope[b, rows, lanes]
                owned[0, b, rows, lanes] = (grad * own[b * v // 2]).astype(BF16)

    tiles(16, fourth, 2)
    pair_two = filter_gradient(1, 1)
    pair_one = filter_gradient(0, 0)
    grad_moves = give(2, 1, sel1[...], natural(owned[0]).astype(BF16))
    for f, move in ((1, pair_two), (0, pair_one)):
        move.wait_recv()
        for s in range(16):
            crossing[s, f] = pile[f, rz, s] + pair_in[f, s]
    xy_moves = [
        send(crossing.at[s], xy_in.at[xy], (xy_send, xy_recv), i, peer)
        for i, (s, peer) in enumerate(zip(xy_slots, xy_peers))
    ]
    xy_in[xy] = crossing[xy]

    outs = [depart(0, natural(leaving[...]), act_out)]
    for move in xy_moves:
        move.wait_recv()
    total = xy_in[0]
    for s in range(1, 16):
        total = total + xy_in[s]
    z_in[pz] = total
    z_moves = [
        send(z_in.at[pz], z_in.at[pz], (z_send, z_recv), i, peer) for i, peer in enumerate(z_peers)
    ]

    for b, value in enumerate(take(2, 1, rows1[...], grad_moves)):
        blk[b] = value

    def fifth(r0):
        rows = pl.ds(r0, 16)
        here = inside[rows, :]
        for b in range(3):
            for v in range(2):
                put(3, b, v, r0, blk[b, rows, 128 * v : 128 * v + 128] * here)

    tiles(17, fifth, 2)
    conv(3, 2, 16, True)

    def sixth(r0):
        rows = pl.ds(r0, 16)
        for b in range(3):
            leaving[b, rows, :] = (pre[b, rows, :] * keep[b, rows, :]).astype(BF16)

    tiles(16, sixth, 2)
    outs.append(depart(1, natural(leaving[...]), gin_out))

    for move in z_moves:
        move.wait_recv()
    total = z_in[0]
    for s in range(1, 8):
        total = total + z_in[s]
    xc_in[xc] = total * (1.0 / math.sqrt(4 * count * 2048))
    xc_moves = [
        send(xc_in.at[xc], xc_in.at[xc], (xc_send, xc_recv), i, peer) for i, peer in enumerate(xc_peers)
    ]
    for move in xc_moves:
        move.wait_recv()
    offset = lax.rem(4 - dp, 4) * 8
    for f, out in enumerate((grad_one_out, grad_two_out)):
        for j in range(4):
            for w in range(2):
                parts = []
                for g in range(4):
                    value = xc_in[4 * w + g, f]
                    parts.append(value if g == j else pltpu.roll(value, 32 * ((g - j) % 4), 1))
                final[8 * j : 8 * j + 8, 128 * w : 128 * w + 128] = pick(group, parts)
        out[...] = pltpu.roll(final[...], 256 - offset, 1)[:, :216]

    for copy in outs:
        copy.wait()
    for copy in started:
        copy.wait_send()


def on_device(volume, tissue_kept, filter_one, filter_two, cotangent):
    vmem, anywhere = pl.BlockSpec(memory_space=pltpu.VMEM), pl.BlockSpec(memory_space=pl.ANY)
    dma = pltpu.SemaphoreType.DMA
    field = jax.ShapeDtypeStruct(volume.shape, BF16)
    grad = jax.ShapeDtypeStruct((C, 216), F32)
    blocked = pltpu.VMEM((3, 304, 256), F32)
    act, gin, one, two = pl.pallas_call(
        kernel,
        out_shape=(field, field, grad, grad),
        in_specs=[pl.BlockSpec(memory_space=pltpu.SMEM), vmem, vmem, anywhere, anywhere],
        out_specs=(anywhere, anywhere, vmem, vmem),
        scratch_shapes=[
            pltpu.VMEM((C, 8, 256), BF16),
            pltpu.VMEM((C, 8, 256), BF16),
            pltpu.VMEM((2, C, 8, 256), BF16),
            pltpu.VMEM((256, 1024), F32),
            pltpu.VMEM((5, 128, 128), F32),
            pltpu.VMEM((3, 128, 512), BF16),
            pltpu.VMEM((3, 128, 128), BF16),
            pltpu.VMEM((3, 2, 48, 512), BF16),
            pltpu.VMEM((3, 2, 48, 128), BF16),
            pltpu.VMEM((3, 288, 512), BF16),
            pltpu.VMEM((3, 288, 128), BF16),
            blocked,
            blocked,
            blocked,
            blocked,
            blocked,
            pltpu.VMEM((4, 3, 3, 320, 256), BF16),
            pltpu.VMEM((4, 9, 256, 256), BF16),
            pltpu.VMEM((3, 256, 256), BF16),
            pltpu.VMEM((2, 3, 256, 256), BF16),
            pltpu.VMEM((256, 1024), BF16),
            pltpu.VMEM((2, 64, 128), BF16),
            pltpu.VMEM((2, 4, 64, 128), BF16),
            pltpu.VMEM((864, 128), F32),
            pltpu.VMEM((2, 27, C, 128), F32),
            pltpu.VMEM((9, 256, 256), F32),
            pltpu.VMEM((2, 27, 8, 128), F32),
            pltpu.VMEM((2, 2, 16, 8, 128), F32),
            pltpu.VMEM((2, 16, 8, 128), F32),
            pltpu.VMEM((16, 2, 8, 128), F32),
            pltpu.VMEM((16, 2, 8, 128), F32),
            pltpu.VMEM((8, 2, 8, 128), F32),
            pltpu.VMEM((8, 2, 8, 128), F32),
            pltpu.VMEM((C, 256), F32),
            pltpu.VMEM((256, 256), BF16),
            pltpu.VMEM((256, 1024), BF16),
            pltpu.VMEM((96, 128), BF16),
            pltpu.VMEM((32, 128), BF16),
            pltpu.VMEM((304, 288), BF16),
            pltpu.VMEM((304, 208), BF16),
            pltpu.VMEM((256, 256), BF16),
            pltpu.VMEM((384, 256), BF16),
            pltpu.VMEM((384, 256), BF16),
            pltpu.VMEM((128, 256), BF16),
            pltpu.VMEM((768, 640), BF16),
            pltpu.VMEM((304, 128), F32),
            dma((2,)), dma((2,)), dma((3, 11)), dma((3, 11)), dma((2, 3)), dma((2, 3)),
            dma((2,)), dma((2,)), dma((15,)), dma((15,)), dma((7,)), dma((7,)), dma((7,)), dma((7,)),
        ],
        compiler_params=pltpu.CompilerParams(
            collective_id=0, has_side_effects=True, vmem_limit_bytes=48 * 1024 * 1024
        ),
    )(tissue_kept, filter_one.T, filter_two.T, volume, cotangent)
    return act, gin, one.T, two.T


def solution(mesh):
    field, rows = P("dp", "space", None, None, None), P("dp", None)
    return jax.shard_map(
        on_device,
        mesh=mesh,
        in_specs=(field, P("dp", "space", None), rows, rows, field),
        out_specs=(field, field, rows, rows),
        check_vma=False,
    )
```

```python
import math

import jax
import jax.numpy as jnp
from jax import lax
from jax.experimental import pallas as pl
from jax.experimental.pallas import tpu as pltpu
from jax.sharding import PartitionSpec as P

MESH = pl.DeviceIdType.MESH
F32 = jnp.float32
BF16 = jnp.bfloat16
NN = (((1,), (0,)), ((), ()))
NT = (((1,), (1,)), ((), ()))
TN = (((0,), (0,)), ((), ()))

C = 32
GONE = 64.0
STARTS = (0, 6, 13, 20)


def dot(a, b, dims=NN):
    return lax.dot_general(a, b, dims, preferred_element_type=F32)


def iota(shape, axis):
    return lax.broadcasted_iota(jnp.int32, shape, axis)


def ones_at(cond):
    return jnp.where(cond, 1.0, 0.0).astype(BF16)


def pick(group, parts):
    value = None
    for g in range(len(parts) - 1, -1, -1):
        part = 0.0 if parts[g] is None else parts[g]
        if value is None:
            value = part
        elif not (parts[g] is None and isinstance(value, float)):
            value = jnp.where(group == g, part, value)
    return value


def logistic(v):
    return 1.0 / (1.0 + jnp.exp(-v))


def layout(h):
    yrows = 32 if h == 3 else 16
    low, high, beyond = 128, 128 + 16 * h, 128 + 32 * h
    return yrows, low, high, beyond, beyond + yrows, beyond + yrows + 16, beyond + yrows + 32


def kernel(
    flags, filter_one, filter_two, volume, cotangent,
    act_out, gin_out, grad_one_out, grad_two_out,
    kept, rows_in, vin, cin, spread, nat, nat_main, nat_z, face_main, face_z, stack_main, stack_z,
    blk, cot, keep, slope, pre, shifted, bands, leaving, owned, wide,
    wsend, wrecv, wrows, rep, product, tap_tile, pile, pair_in, crossing, xy_in, z_in, xc_in, final,
    turn, copies8, sel3, sel1, rows3, rows1, place0, place1, place2, pack, unplace, inside,
    local_sem, halo_send, halo_recv, filt_send, filt_recv,
    pair_send, pair_recv, xy_send, xy_recv, z_send, z_recv, xc_send, xc_recv,
):
    space = lax.axis_index("space")
    dp = lax.axis_index("dp")
    count = lax.axis_size("space")
    rx, ry, rz = space // 4, (space // 2) % 2, space % 2
    bx, pz = space // 16, (space // 2) % 8
    has_below, has_above = rx > 0, rx < count // 4 - 1
    started = []

    loads = [
        pltpu.make_async_copy(volume.at[0, 0], vin, local_sem.at[0]),
        pltpu.make_async_copy(flags.at[0], kept, local_sem.at[1]),
        pltpu.make_async_copy(filter_one, rows_in.at[0], local_sem.at[2]),
        pltpu.make_async_copy(filter_two, rows_in.at[1], local_sem.at[3]),
        pltpu.make_async_copy(cotangent.at[0, 0], cin, local_sem.at[4]),
    ]
    for load in loads:
        load.start()

    def send(src, dst, sems, at, peer):
        pltpu.make_async_remote_copy(
            src_ref=src, dst_ref=dst, send_sem=sems[0].at[at], recv_sem=sems[1].at[at],
            device_id=peer, device_id_type=MESH,
        ).start()

    def batch(ref, sems, at):
        copy = pltpu.make_async_remote_copy(
            src_ref=ref, dst_ref=ref, send_sem=sems[0].at[at], recv_sem=sems[1].at[at],
            device_id=dp_peers[0], device_id_type=MESH,
        )
        started.append(copy)
        return copy

    base = space - 2 * ry - rz
    column = (space, base + 2 * (1 - ry) + rz, base + 2 * ry + (1 - rz), base + 2 * (1 - ry) + (1 - rz))
    below = [lax.rem(d - 4 + count, count) for d in column]
    above = [lax.rem(d + 4, count) for d in column]
    xy = bx * 4 + dp
    xy_slots = [lax.rem(xy + k, 16) for k in range(1, 16)]
    xy_peers = [((s // 4) * 16 + lax.rem(space, 16), s % 4) for s in xy_slots]
    z_peers = [(bx * 16 + 2 * lax.rem(pz + k, 8) + rz, dp) for k in range(1, 8)]
    xc = rz * 4 + bx
    xc_slots = [lax.rem(xc + k, 8) for k in range(1, 8)]
    xc_peers = [((s % 4) * 16 + 2 * pz + s // 4, dp) for s in xc_slots]
    dp_peers = [(space, lax.rem(dp + k, 4)) for k in range(1, 4)]

    barrier = pltpu.get_barrier_semaphore()
    greeted = [(d, dp) for d in column[1:]] + [(d, dp) for d in below + above] + xy_peers + z_peers + xc_peers
    for peer in greeted:
        pl.semaphore_signal(barrier, inc=1, device_id=peer, device_id_type=MESH)

    group = iota((1, 128), 1) // C

    row, col = iota((256, 256), 0), iota((256, 256), 1)
    y, z = row % 16, row // 16
    turn[...] = ones_at(col == 16 * jnp.where(ry == 0, y, 15 - y) + jnp.where(rz == 0, z, 15 - z))
    row, col = iota((256, 128), 0), iota((256, 128), 1)
    for x in range(8):
        copies8[:, 128 * x : 128 * x + 128] = ones_at(row == 8 * (col % C) + x)

    def faces_of(h):
        row, col = iota((32 * h, 128), 0), iota((32 * h, 128), 1)
        y, x = col // 8, col % 8
        return ones_at(
            ((x < h) & (row == h * y + x)) | ((x >= 8 - h) & (row == 16 * h + h * y + x - (8 - h)))
        )

    sel3[...] = faces_of(3)

    cell = iota((1, 256), 1)
    tile = 2 * (cell // 128) + (cell % 16) // 8

    def turn_in(f, field):
        cells = dot(turn[...], field.astype(BF16), NT).astype(BF16)
        spread[...] = dot(cells, copies8[...])
        for x in range(8):
            for w in range(5):
                layers = [4 * w + g for g in range(4)] if w < 4 else [None, 15, 14, 13]
                parts = [None if l is None else spread[16 * l : 16 * l + 16, 128 * x : 128 * x + 128] for l in layers]
                nat[w, pl.ds(x, 16, stride=8), :] = pick(group, parts)
        return jnp.concatenate([nat[w] for w in range(5)], axis=1).astype(BF16)

    def give(f, h, sel, field):
        yrows, low, high, beyond, corner_low, corner_high, total = layout(h)
        main, last = field[:, :512], field[:, 512:]
        nat_main[f] = main
        nat_z[f] = last
        faces = dot(sel, field).astype(BF16)
        for side in range(2):
            face_main[f, side, 0 : 16 * h] = faces[16 * h * side : 16 * h * side + 16 * h, :512]
            face_z[f, side, 0 : 16 * h] = faces[16 * h * side : 16 * h * side + 16 * h, 512:]
        sems = (halo_send, halo_recv)

        def add(src, dst, d, kind):
            send(src, dst, sems, (f, kind), (d, dp))

        ends = ((1, low, corner_low, above), (0, high, corner_high, below))
        for side, at, _, to in ends:
            add(face_main.at[f, side, 0 : 16 * h], stack_main.at[f, at : at + 16 * h], to[0], 0)
        for side, at, corner, to in ends:
            add(face_z.at[f, side, 0 : 16 * h], stack_z.at[f, at : at + 16 * h], to[2], 1)
            add(face_main.at[f, side, 16 * h - 16 : 16 * h], stack_main.at[f, corner : corner + 16], to[1], 0)
            add(face_z.at[f, side, 16 * h - 16 : 16 * h], stack_z.at[f, corner : corner + 16], to[3], 1)
        add(nat_main.at[f, 128 - yrows : 128], stack_main.at[f, beyond : beyond + yrows], column[1], 0)
        add(nat_z.at[f, 128 - yrows : 128], stack_z.at[f, beyond : beyond + yrows], column[3], 1)
        add(nat_z.at[f], stack_z.at[f, 0:128], column[2], 1)
        stack_main[f, 0:128] = main
        return [batch(stack_main.at[f, 128:total], sems, (f, 0)), batch(stack_z.at[f, 0:total], sems, (f, 1))]

    def assemble(h):
        yrows, low, high, beyond, corner_low, corner_high, total = layout(h)
        row, col = iota((304, total), 0), iota((304, total), 1)
        y, x = row // 16, row % 16 - 4
        mid, lo, hi = (x >= 0) & (x < 8), (x < 0) & (x >= -h), (x >= 8) & (x < 8 + h)
        own, far = y < 16, (y >= 16) & (y < 16 + h)
        first, there = 16 - yrows // 8, 31 - y
        skip = 16 * h - 16
        at = jnp.where(own & mid, 8 * y + x, -1)
        at = jnp.where(own & lo, low + h * y + x + h, at)
        at = jnp.where(own & hi, high + h * y + x - 8, at)
        at = jnp.where(far & mid, beyond + 8 * (there - first) + x, at)
        at = jnp.where(far & lo, corner_low + h * there + x + h - skip, at)
        at = jnp.where(far & hi, corner_high + h * there + x - 8 - skip, at)
        return ones_at(at == col)

    def take(f, h, rows, moves):
        for move in moves:
            move.wait_recv()
        total = layout(h)[-1]
        pieces = jnp.concatenate([stack_main[f, 0:total], stack_z[f, 0:total]], axis=1)
        whole = dot(rows, pieces).astype(BF16)
        return (
            dot(whole[:, 0:256], place0[...]), dot(whole[:, 128:512], place1[...]), dot(whole[:, 256:640], place2[...])
        )

    def halves(value):
        return value[:, :128], value[:, 128:]

    def put(f, b, v, r0, value):
        lanes = slice(128 * v, 128 * v + 128)
        at = slice(r0 + 16, r0 + 32)
        shifted[f, 1, b, at, lanes] = value.astype(BF16)
        shifted[f, 0, b, at, lanes] = pltpu.roll(value, 1, 0).astype(BF16)
        shifted[f, 2, b, at, lanes] = pltpu.roll(value, 15, 0).astype(BF16)

    def put_all(f, r0, parts):
        for b in range(3):
            lo, hi = parts[b]
            lo = jnp.where(group == 0, pltpu.roll(parts[b - 1][1], 64, 1) if b > 0 else 0.0, lo)
            hi = jnp.where(group == 3, pltpu.roll(parts[b + 1][0], 64, 1) if b < 2 else 0.0, hi)
            put(f, b, 0, r0, lo)
            put(f, b, 1, r0, hi)

    def inputs_of(f, ox, oy, ny):
        return shifted[f, ox, :, 16 * oy : 16 * oy + 16 * ny].reshape(48 * ny, 256)

    def conv(f, slot, back, y0, ny):
        lhs = jnp.concatenate([inputs_of(f, ox, y0 + oy, ny) for ox in range(3) for oy in range(3)], axis=1)
        if back:
            rhs, dims = jnp.concatenate([bands[slot, t] for t in range(9)], axis=1), NT
        else:
            rhs, dims = bands[slot].reshape(9 * 256, 256), NN
        pre[slot, :, 16 * y0 : 16 * y0 + 16 * ny] = dot(lhs, rhs, dims).reshape(3, 16 * ny, 256)

    def send_rows(f, rows):
        square = ones_at(iota((216, 216), 0) == iota((216, 216), 1))
        four = jnp.concatenate([rows[...]] * 4, axis=0)
        full = jnp.concatenate([dot(square, four, NT), jnp.zeros((8, 128), F32)], axis=0)
        packed = pick(group, [full[56 * g : 56 * g + 56] for g in range(4)])
        packed = jnp.concatenate([packed, jnp.zeros((8, 128), F32)], axis=0).astype(BF16)
        wsend[f] = packed
        wrecv[f, dp] = packed

    def share_rows(f):
        sems = (filt_send, filt_recv)
        for peer in dp_peers:
            send(wsend.at[f], wrecv.at[f, dp], sems, f, peer)
        return [batch(wrecv.at[f, 0:3], sems, f)]

    def filter_rows(f):
        for g8 in range(108):
            src, rr = g8 // 27, g8 % 27
            g, r = rr // 7, rr % 7
            part = wrecv[f, src, 16 * (r // 2) : 16 * (r // 2) + 16].astype(F32)[8 * (r % 2) : 8 * (r % 2) + 8]
            wrows[8 * g8 : 8 * g8 + 8] = jnp.where(group == g, part, 0.0)
        again = ones_at(iota((128, 128), 0) % C == iota((128, 128), 1) % C)
        rep[f] = dot(wrows[...].astype(BF16), again).reshape(27, C, 128)

    def tap(ox, oy, oz):
        ty = oy if oy == 1 else jnp.where(ry == 0, oy, 2 - oy)
        tz = oz if oz == 1 else jnp.where(rz == 0, oz, 2 - oz)
        return 9 * ox + 3 * ty + tz

    def band(f):
        for ox in range(3):
            for oy in range(3):
                taps = [rep[f, tap(ox, oy, oz)] for oz in range(3)]
                for v in range(2):
                    for zi in range(8):
                        parts = []
                        for g in range(4):
                            zo = 4 * v + g
                            parts.append(taps[zi - zo + 1] if 1 <= zo <= 6 and abs(zi - zo) <= 1 else None)
                        if any(p is not None for p in parts):
                            value = pick(group, parts).astype(BF16)
                        else:
                            value = jnp.zeros((C, 128), BF16)
                        bands[f, 3 * ox + oy, C * zi : C * zi + C, 128 * v : 128 * v + 128] = value

    def band_back(f):
        for sx in range(3):
            for sy in range(3):
                taps = [rep[f, tap(2 - sx, 2 - sy, oz)] for oz in range(3)]
                for v in range(2):
                    for zo in range(8):
                        parts = []
                        for g in range(4):
                            zi = 4 * v + g
                            parts.append(taps[zo - zi + 1] if 1 <= zo <= 6 and abs(zi - zo) <= 1 else None)
                        if any(p is not None for p in parts):
                            value = pick(group, parts).astype(BF16)
                        else:
                            value = jnp.zeros((C, 128), BF16)
                        bands[2 + f, 3 * sx + sy, C * zo : C * zo + C, 128 * v : 128 * v + 128] = value

    def natural(blocked):
        rows = jnp.concatenate([dot(pack[...], blocked[b]) for b in range(3)], axis=1).astype(BF16)
        return dot(rows, unplace[...])

    def depart(field, out):
        for w in range(4):
            nat[w] = field[:, 128 * w : 128 * w + 128]
        for x in range(8):
            for w in range(4):
                value = nat[w, pl.ds(x, 16, stride=8), :]
                for g in range(4):
                    at = 16 * (4 * w + g)
                    wide[at : at + 16, 128 * x : 128 * x + 128] = jnp.where(group == g, value, 0.0).astype(BF16)
        cells = dot(copies8[...], wide[...], NT).astype(BF16)
        out[0, 0] = dot(cells, turn[...]).reshape(C, 8, 256).astype(BF16)

    def filter_gradient(f, r):
        gradient = owned[f].reshape(768, 256)
        odd, high = group % 2 == 1, group >= 2
        for t in range(9):
            product[f, t] = dot(gradient, inputs_of(r, t // 3, t % 3, 16), TN)
            for oz in range(3):
                a = []
                for j in range(4):
                    sides = []
                    for v in range(2):
                        parts = []
                        for g in range(4):
                            zo = 4 * v + g - (oz - 1)
                            at = zo * C + 8 * j
                            parts.append(product[f, t, at : at + 8, 128 * v : 128 * v + 128] if 1 <= zo <= 6 else None)
                        sides.append(pick(group, parts))
                    a.append(sides[0] + sides[1])
                pairs = [
                    jnp.where(odd, a[i + 1], a[i]) + pltpu.roll(jnp.where(odd, a[i], a[i + 1]), 32, 1) for i in (0, 2)
                ]
                tap_tile[f, tap(t // 3, t % 3, oz)] = jnp.where(high, pairs[1], pairs[0]) + pltpu.roll(
                    jnp.where(high, pairs[0], pairs[1]), 64, 1
                )
        for q in range(4):
            for k in range(8):
                source = STARTS[q] + k
                pile[f, k // 4, 4 * (k % 4) + q] = (
                    tap_tile[f, source] if source < 27 else jnp.zeros((8, 128), F32)
                )
        send(pile.at[f, 1 - rz], pair_in.at[f], (pair_send, pair_recv), f, (column[2], dp))
        return batch(pair_in.at[f], (pair_send, pair_recv), f)

    loads[0].wait()
    loads[1].wait()
    flag = kept[...].astype(F32)
    kept_cells = jnp.zeros((1, 256), F32)
    for b in range(4):
        kept_cells = jnp.where(tile == b, flag[:, b : b + 1], kept_cells)
    field = jnp.where(kept_cells > 0.5, vin[...].astype(F32).reshape(256, 256), GONE)
    field = turn_in(0, field)
    pl.semaphore_wait(barrier, len(greeted))
    volume_moves = give(0, 3, sel3[...], field)

    loads[2].wait()
    loads[3].wait()
    send_rows(0, rows_in.at[0])
    row_moves = [share_rows(0)]
    send_rows(1, rows_in.at[1])
    row_moves.append(share_rows(1))

    sel1[...] = faces_of(1)
    loads[4].wait()
    cot_moves = give(1, 1, sel1[...], turn_in(1, cin[...].astype(F32).reshape(256, 256)))

    rows3[...] = assemble(3)
    rows1[...] = assemble(1)
    k, n = iota((256, 256), 0), iota((256, 256), 1)
    place0[...] = ones_at(n - k == C)
    k, n = iota((384, 256), 0), iota((384, 256), 1)
    place1[...] = ones_at(k - n == C)
    place2[...] = ones_at(k - n == jnp.where(n < 160, 96, 128))
    row, col = iota((128, 256), 0), iota((128, 256), 1)
    pack[...] = ones_at(col == 16 * (row // 8) + row % 8 + 4)
    for b in range(3):
        k, n = iota((256, 640), 0), iota((256, 640), 1)
        zi, z = k // C, 6 * b + k // C - 1
        good = (zi >= 1) & (zi <= 6) & (z < 16) & (k % C == n % C)
        unplace[256 * b : 256 * b + 256] = ones_at(
            good & (((n < 512) & (n // C == z)) | ((n >= 544) & (16 - (n // C - 16) == z)))
        )
    x = iota((304, 128), 0) % 16 - 4
    inside[...] = jnp.where(((x < 0) & ~has_below) | ((x >= 8) & ~has_above), 0.0, 1.0)
    for f in range(4):
        for ox in range(3):
            for b in range(3):
                shifted[f, ox, b, 0:16] = jnp.zeros((16, 256), BF16)

    for f in range(2):
        for move in row_moves[f]:
            move.wait_recv()
        filter_rows(f)
        band(f)
        band_back(f)

    for b, value in enumerate(take(0, 3, rows3[...], volume_moves)):
        blk[b] = value

    def first(y):
        rows = slice(16 * y, 16 * y + 16)
        here = inside[rows, :]
        for b in range(3):
            for v in range(2):
                lanes = slice(128 * v, 128 * v + 128)
                value = blk[b, rows, lanes]
                kept_here = jnp.where(value == GONE, 0.0, here)
                keep[b, rows, lanes] = kept_here
                put(0, b, v, 16 * y, value * kept_here)

    def second(y):
        rows = slice(16 * y, 16 * y + 16)
        parts = []
        for b in range(3):
            value, there = pre[0, b, rows, :], keep[b, rows, :]
            gate = logistic(value)
            act = value * gate
            slope[b, rows, :] = (gate + act * (1.0 - gate)) * there
            parts.append(halves(act * there))
        put_all(1, 16 * y, parts)

    x = iota((16, 128), 0) - 4
    own = [jnp.where((x >= 0) & (x < 8), 1.0, 0.0)]
    own.append(jnp.where(group == 0, own[0], 0.0))
    own_lanes = [jnp.concatenate([own[0], own[b // 2]], axis=1) for b in range(3)]

    def third(y):
        rows = slice(16 * y, 16 * y + 16)
        parts = []
        for b in range(3):
            value, there = pre[1, b, rows, :], keep[b, rows, :]
            gate = logistic(value)
            act = value * gate
            grad = cot[b, rows, :] * there * (gate + act * (1.0 - gate))
            parts.append(halves(grad))
            if y < 16:
                leaving[b, rows, :] = (act * there).astype(BF16)
                owned[1, b, rows, :] = (grad * own_lanes[b]).astype(BF16)
        put_all(2, 16 * y, parts)

    def fourth(y):
        rows = slice(16 * y, 16 * y + 16)
        for b in range(3):
            owned[0, b, rows, :] = (pre[3, b, rows, :] * slope[b, rows, :] * own_lanes[b]).astype(BF16)

    def run(body, first_y, end):
        for y in range(first_y, end):
            body(y)

    run(first, 0, 8)
    conv(0, 0, False, 0, 6)
    run(first, 8, 14)
    conv(0, 0, False, 6, 6)
    run(second, 0, 6)
    run(first, 14, 19)
    conv(0, 0, False, 12, 6)
    run(second, 6, 12)
    conv(1, 1, False, 0, 6)
    run(second, 12, 18)
    conv(1, 1, False, 6, 6)
    for b, value in enumerate(take(1, 1, rows1[...], cot_moves)):
        cot[b] = value
    run(third, 0, 6)
    conv(1, 1, False, 12, 5)
    run(third, 6, 12)
    conv(2, 3, True, 0, 6)
    run(third, 12, 17)
    conv(2, 3, True, 6, 5)
    run(fourth, 0, 6)
    conv(2, 3, True, 11, 5)
    run(fourth, 6, 16)
    pair_one = filter_gradient(0, 0)
    pair_two = filter_gradient(1, 1)
    grad_moves = give(2, 1, sel1[...], natural(owned[0]).astype(BF16))
    for f, move in ((0, pair_one), (1, pair_two)):
        move.wait_recv()
        for s in range(16):
            crossing[s, f] = pile[f, rz, s] + pair_in[f, s]
    for s, peer in zip(xy_slots, xy_peers):
        send(crossing.at[s], xy_in.at[xy], (xy_send, xy_recv), 0, peer)
    xy_moves = [batch(xy_in.at[0:15], (xy_send, xy_recv), 0)]
    xy_in[xy] = crossing[xy]

    depart(natural(leaving[...]), act_out)
    for move in xy_moves:
        move.wait_recv()
    total = xy_in[0]
    for s in range(1, 16):
        total = total + xy_in[s]
    z_in[pz] = total
    for peer in z_peers:
        send(z_in.at[pz], z_in.at[pz], (z_send, z_recv), 0, peer)
    z_moves = [batch(z_in.at[0:7], (z_send, z_recv), 0)]

    for b, value in enumerate(take(2, 1, rows1[...], grad_moves)):
        blk[b] = value

    def fifth(y):
        rows = slice(16 * y, 16 * y + 16)
        here = inside[rows, :]
        for b in range(3):
            for v in range(2):
                put(3, b, v, 16 * y, blk[b, rows, 128 * v : 128 * v + 128] * here)

    def sixth(y):
        rows = slice(16 * y, 16 * y + 16)
        for b in range(3):
            leaving[b, rows, :] = (pre[2, b, rows, :] * keep[b, rows, :]).astype(BF16)

    run(fifth, 0, 8)
    conv(3, 2, True, 0, 6)
    run(fifth, 8, 17)
    conv(3, 2, True, 6, 5)
    run(sixth, 0, 6)
    conv(3, 2, True, 11, 5)
    run(sixth, 6, 16)
    depart(natural(leaving[...]), gin_out)

    for move in z_moves:
        move.wait_recv()
    total = z_in[0]
    for s in range(1, 8):
        total = total + z_in[s]
    xc_in[xc] = total * (1.0 / math.sqrt(4 * count * 2048))
    for peer in xc_peers:
        send(xc_in.at[xc], xc_in.at[xc], (xc_send, xc_recv), 0, peer)
    xc_moves = [batch(xc_in.at[0:7], (xc_send, xc_recv), 0)]
    for move in xc_moves:
        move.wait_recv()
    offset = lax.rem(4 - dp, 4) * 8
    for f, out in enumerate((grad_one_out, grad_two_out)):
        for j in range(4):
            for w in range(2):
                parts = []
                for g in range(4):
                    value = xc_in[4 * w + g, f]
                    parts.append(value if g == j else pltpu.roll(value, 32 * ((g - j) % 4), 1))
                final[8 * j : 8 * j + 8, 128 * w : 128 * w + 128] = pick(group, parts)
        out[...] = pltpu.roll(final[...], 256 - offset, 1)[:, :216]

    for copy in started:
        copy.wait_send()


def hand_over(*refs):
    copies = [pltpu.make_async_copy(refs[i], refs[4 + i], refs[8].at[i]) for i in range(4)]
    for copy in copies:
        copy.start()
    for copy in copies:
        copy.wait()


def on_device(volume, tissue_kept, filter_one, filter_two, cotangent):
    vmem, anywhere = pl.BlockSpec(memory_space=pltpu.VMEM), pl.BlockSpec(memory_space=pl.ANY)
    dma = pltpu.SemaphoreType.DMA
    field, grad = (volume.shape, BF16), ((C, 216), F32)
    results = (field, field, grad, grad)
    blocked = pltpu.VMEM((3, 304, 256), F32)
    held = pl.pallas_call(
        kernel,
        out_shape=tuple(pltpu.VMEM(*r) for r in results),
        in_specs=[anywhere] * 5,
        out_specs=(vmem,) * 4,
        scratch_shapes=[
            pltpu.VMEM((1, 4), jnp.int32),
            pltpu.VMEM((2, C, 216), BF16),
            pltpu.VMEM((C, 8, 256), BF16),
            pltpu.VMEM((C, 8, 256), BF16),
            pltpu.VMEM((256, 1024), F32),
            pltpu.VMEM((5, 128, 128), F32),
            pltpu.VMEM((3, 128, 512), BF16),
            pltpu.VMEM((3, 128, 128), BF16),
            pltpu.VMEM((3, 2, 48, 512), BF16),
            pltpu.VMEM((3, 2, 48, 128), BF16),
            pltpu.VMEM((3, 288, 512), BF16),
            pltpu.VMEM((3, 288, 128), BF16),
            blocked,
            blocked,
            blocked,
            blocked,
            pltpu.VMEM((4, 3, 288, 256), F32),
            pltpu.VMEM((4, 3, 3, 320, 256), BF16),
            pltpu.VMEM((4, 9, 256, 256), BF16),
            pltpu.VMEM((3, 256, 256), BF16),
            pltpu.VMEM((2, 3, 256, 256), BF16),
            pltpu.VMEM((256, 1024), BF16),
            pltpu.VMEM((2, 64, 128), BF16),
            pltpu.VMEM((2, 4, 64, 128), BF16),
            pltpu.VMEM((864, 128), F32),
            pltpu.VMEM((2, 27, C, 128), F32),
            pltpu.VMEM((2, 9, 256, 256), F32),
            pltpu.VMEM((2, 27, 8, 128), F32),
            pltpu.VMEM((2, 2, 16, 8, 128), F32),
            pltpu.VMEM((2, 16, 8, 128), F32),
            pltpu.VMEM((16, 2, 8, 128), F32),
            pltpu.VMEM((16, 2, 8, 128), F32),
            pltpu.VMEM((8, 2, 8, 128), F32),
            pltpu.VMEM((8, 2, 8, 128), F32),
            pltpu.VMEM((C, 256), F32),
            pltpu.VMEM((256, 256), BF16),
            pltpu.VMEM((256, 1024), BF16),
            pltpu.VMEM((96, 128), BF16),
            pltpu.VMEM((32, 128), BF16),
            pltpu.VMEM((304, 288), BF16),
            pltpu.VMEM((304, 208), BF16),
            pltpu.VMEM((256, 256), BF16),
            pltpu.VMEM((384, 256), BF16),
            pltpu.VMEM((384, 256), BF16),
            pltpu.VMEM((128, 256), BF16),
            pltpu.VMEM((768, 640), BF16),
            pltpu.VMEM((304, 128), F32),
            dma((5,)), dma((3, 2)), dma((3, 2)), dma((2,)), dma((2,)),
            dma((2,)), dma((2,)), dma((1,)), dma((1,)), dma((1,)), dma((1,)), dma((1,)), dma((1,)),
        ],
        compiler_params=pltpu.CompilerParams(
            collective_id=0, has_side_effects=True, vmem_limit_bytes=60 * 1024 * 1024
        ),
    )(tissue_kept, filter_one.T, filter_two.T, volume, cotangent)
    act, gin, one, two = pl.pallas_call(
        hand_over,
        out_shape=tuple(jax.ShapeDtypeStruct(*r) for r in results),
        in_specs=[anywhere] * 4,
        out_specs=(anywhere,) * 4,
        scratch_shapes=[dma((4,))],
    )(*(pltpu.with_memory_space_constraint(part, pltpu.VMEM) for part in held))
    return act, gin, one.T, two.T


def solution(mesh):
    field, rows = P("dp", "space", None, None, None), P("dp", None)
    return jax.shard_map(
        on_device,
        mesh=mesh,
        in_specs=(field, P("dp", "space", None), rows, rows, field),
        out_specs=(field, field, rows, rows),
        check_vma=False,
    )
```

```python
import math

import jax
import jax.numpy as jnp
from jax import lax
from jax.experimental import pallas as pl
from jax.experimental.pallas import tpu as pltpu
from jax.sharding import PartitionSpec as P

MESH = pl.DeviceIdType.MESH
F32 = jnp.float32
BF16 = jnp.bfloat16
NN = (((1,), (0,)), ((), ()))
NT = (((1,), (1,)), ((), ()))
TN = (((0,), (0,)), ((), ()))

C = 32
GONE = 64.0
STARTS = (0, 6, 13, 20)


def dot(a, b, dims=NN):
    return lax.dot_general(a, b, dims, preferred_element_type=F32)


def iota(shape, axis):
    return lax.broadcasted_iota(jnp.int32, shape, axis)


def ones_at(cond):
    return jnp.where(cond, 1.0, 0.0).astype(BF16)


def pick(group, parts):
    value = None
    for g in range(len(parts) - 1, -1, -1):
        part = 0.0 if parts[g] is None else parts[g]
        if value is None:
            value = part
        elif not (parts[g] is None and isinstance(value, float)):
            value = jnp.where(group == g, part, value)
    return value


def logistic(v):
    return 1.0 / (1.0 + jnp.exp(-v))


def layout(h):
    yrows = 32 if h == 3 else 16
    low, high, beyond = 128, 128 + 16 * h, 128 + 32 * h
    return yrows, low, high, beyond, beyond + yrows, beyond + yrows + 16, beyond + yrows + 32


def kernel(
    flags, filter_one, filter_two, volume, cotangent,
    act_out, gin_out, grad_one_out, grad_two_out,
    kept, rows_in, vin, cin, spread, nat, nat_main, nat_z, face_main, face_z, stack_main, stack_z,
    blk, cot, keep, slope, pre, shifted, bands, leaving, owned, wide,
    wsend, wrecv, wrows, rep, product, tap_tile, pile, pair_in, crossing, xy_in, z_in, xc_in, final,
    turn, copies8, sel3, sel1, near3, far3, near1, far1, place0, place1, place2, pack, unplace, inside,
    local_sem, halo_send, halo_recv, filt_send, filt_recv,
    pair_send, pair_recv, xy_send, xy_recv, z_send, z_recv, xc_send, xc_recv,
):
    space = lax.axis_index("space")
    dp = lax.axis_index("dp")
    count = lax.axis_size("space")
    rx, ry, rz = space // 4, (space // 2) % 2, space % 2
    bx, pz = space // 16, (space // 2) % 8
    has_below, has_above = rx > 0, rx < count // 4 - 1
    started = []

    loads = [
        pltpu.make_async_copy(volume.at[0, 0], vin, local_sem.at[0]),
        pltpu.make_async_copy(flags.at[0], kept, local_sem.at[1]),
        pltpu.make_async_copy(filter_one, rows_in.at[0], local_sem.at[2]),
        pltpu.make_async_copy(filter_two, rows_in.at[1], local_sem.at[3]),
        pltpu.make_async_copy(cotangent.at[0, 0], cin, local_sem.at[4]),
    ]
    for load in loads:
        load.start()

    def send(src, dst, sems, at, peer):
        pltpu.make_async_remote_copy(
            src_ref=src, dst_ref=dst, send_sem=sems[0].at[at], recv_sem=sems[1].at[at],
            device_id=peer, device_id_type=MESH,
        ).start()

    def batch(ref, sems, at):
        copy = pltpu.make_async_remote_copy(
            src_ref=ref, dst_ref=ref, send_sem=sems[0].at[at], recv_sem=sems[1].at[at],
            device_id=dp_peers[0], device_id_type=MESH,
        )
        started.append(copy)
        return copy

    base = space - 2 * ry - rz
    column = (space, base + 2 * (1 - ry) + rz, base + 2 * ry + (1 - rz), base + 2 * (1 - ry) + (1 - rz))
    below = [lax.rem(d - 4 + count, count) for d in column]
    above = [lax.rem(d + 4, count) for d in column]
    xy = bx * 4 + dp
    xy_slots = [lax.rem(xy + k, 16) for k in range(1, 16)]
    xy_peers = [((s // 4) * 16 + lax.rem(space, 16), s % 4) for s in xy_slots]
    z_peers = [(bx * 16 + 2 * lax.rem(pz + k, 8) + rz, dp) for k in range(1, 8)]
    xc = rz * 4 + bx
    xc_slots = [lax.rem(xc + k, 8) for k in range(1, 8)]
    xc_peers = [((s % 4) * 16 + 2 * pz + s // 4, dp) for s in xc_slots]
    dp_peers = [(space, lax.rem(dp + k, 4)) for k in range(1, 4)]

    barrier = pltpu.get_barrier_semaphore()
    greeted = [(d, dp) for d in column[1:]] + [(d, dp) for d in below + above] + xy_peers + z_peers + xc_peers
    for peer in greeted:
        pl.semaphore_signal(barrier, inc=1, device_id=peer, device_id_type=MESH)

    group = iota((1, 128), 1) // C

    row, col = iota((256, 256), 0), iota((256, 256), 1)
    y, z = row % 16, row // 16
    turn[...] = ones_at(col == 16 * jnp.where(ry == 0, y, 15 - y) + jnp.where(rz == 0, z, 15 - z))
    row, col = iota((256, 128), 0), iota((256, 128), 1)
    for x in range(8):
        copies8[:, 128 * x : 128 * x + 128] = ones_at(row == 8 * (col % C) + x)

    def faces_of(h):
        row, col = iota((32 * h, 128), 0), iota((32 * h, 128), 1)
        y, x = col // 8, col % 8
        return ones_at(
            ((x < h) & (row == h * y + x)) | ((x >= 8 - h) & (row == 16 * h + h * y + x - (8 - h)))
        )

    sel3[...] = faces_of(3)

    cell = iota((1, 256), 1)
    tile = 2 * (cell // 128) + (cell % 16) // 8

    def turn_in(f, field):
        cells = dot(turn[...], field.astype(BF16), NT).astype(BF16)
        spread[...] = dot(cells, copies8[...])
        for x in range(8):
            for w in range(5):
                layers = [4 * w + g for g in range(4)] if w < 4 else [None, 15, 14, 13]
                parts = [None if l is None else spread[16 * l : 16 * l + 16, 128 * x : 128 * x + 128] for l in layers]
                nat[w, pl.ds(x, 16, stride=8), :] = pick(group, parts)
        return jnp.concatenate([nat[w] for w in range(5)], axis=1).astype(BF16)

    def show(f, h, sel, field):
        main, last = field[:, :512], field[:, 512:]
        nat_main[f] = main
        nat_z[f] = last
        stack_main[f, 0:128] = main
        faces = dot(sel, field).astype(BF16)
        for side in range(2):
            face_main[f, side, 0 : 16 * h] = faces[16 * h * side : 16 * h * side + 16 * h, :512]
            face_z[f, side, 0 : 16 * h] = faces[16 * h * side : 16 * h * side + 16 * h, 512:]

    def give(f, h):
        yrows, low, high, beyond, corner_low, corner_high, total = layout(h)
        sems = (halo_send, halo_recv)

        def add(src, dst, d, kind):
            send(src, dst, sems, (f, kind), (d, dp))

        ends = ((1, low, corner_low, above), (0, high, corner_high, below))
        for side, at, _, to in ends:
            add(face_main.at[f, side, 0 : 16 * h], stack_main.at[f, at : at + 16 * h], to[0], 0)
        for side, at, _, to in ends:
            add(face_z.at[f, side, 0 : 16 * h], stack_z.at[f, at : at + 16 * h], to[2], 1)
        add(nat_z.at[f], stack_z.at[f, 0:128], column[2], 1)
        for side, _, corner, to in ends:
            add(face_main.at[f, side, 16 * h - 16 : 16 * h], stack_main.at[f, corner : corner + 16], to[1], 2)
            add(face_z.at[f, side, 16 * h - 16 : 16 * h], stack_z.at[f, corner : corner + 16], to[3], 3)
        add(nat_main.at[f, 128 - yrows : 128], stack_main.at[f, beyond : beyond + yrows], column[1], 2)
        add(nat_z.at[f, 128 - yrows : 128], stack_z.at[f, beyond : beyond + yrows], column[3], 3)
        near = [batch(stack_main.at[f, 128:beyond], sems, (f, 0)), batch(stack_z.at[f, 0:beyond], sems, (f, 1))]
        far = [
            batch(stack_main.at[f, beyond:total], sems, (f, 2)), batch(stack_z.at[f, beyond:total], sems, (f, 3))
        ]
        return near, far

    def assemble(h):
        yrows, low, high, beyond, corner_low, corner_high, total = layout(h)
        row, col = iota((256, beyond), 0), iota((256, beyond), 1)
        y, x = row // 16, row % 16 - 4
        at = jnp.where((x >= 0) & (x < 8), 8 * y + x, -1)
        at = jnp.where((x < 0) & (x >= -h), low + h * y + x + h, at)
        at = jnp.where((x >= 8) & (x < 8 + h), high + h * y + x - 8, at)
        near = ones_at(at == col)
        row, col = iota((48, total - beyond), 0), iota((48, total - beyond), 1)
        y, x = row // 16, row % 16 - 4
        there, skip = 15 - y, 16 * h - 16
        at = jnp.where((x >= 0) & (x < 8), 8 * (there - (16 - yrows // 8)) + x, -1)
        at = jnp.where((x < 0) & (x >= -h), yrows + h * there + x + h - skip, at)
        at = jnp.where((x >= 8) & (x < 8 + h), yrows + 16 + h * there + x - 8 - skip, at)
        return near, ones_at((at == col) & (y < h))

    def take(f, h, rows, part, moves, into):
        for move in moves:
            move.wait_recv()
        beyond, total = layout(h)[3], layout(h)[-1]
        start, end = ((0, beyond), (beyond, total))[part]
        pieces = jnp.concatenate([stack_main[f, start:end], stack_z[f, start:end]], axis=1)
        whole = dot(rows[...], pieces).astype(BF16)
        to = slice(256 * part, 256 + 48 * part)
        into[0, to] = dot(whole[:, 0:256], place0[...])
        into[1, to] = dot(whole[:, 128:512], place1[...])
        into[2, to] = dot(whole[:, 256:640], place2[...])

    def halves(value):
        return value[:, :128], value[:, 128:]

    def put(f, b, v, r0, value):
        lanes = slice(128 * v, 128 * v + 128)
        at = slice(r0 + 16, r0 + 32)
        shifted[f, 1, b, at, lanes] = value.astype(BF16)
        shifted[f, 0, b, at, lanes] = pltpu.roll(value, 1, 0).astype(BF16)
        shifted[f, 2, b, at, lanes] = pltpu.roll(value, 15, 0).astype(BF16)

    def put_all(f, r0, parts):
        for b in range(3):
            lo, hi = parts[b]
            lo = jnp.where(group == 0, pltpu.roll(parts[b - 1][1], 64, 1) if b > 0 else 0.0, lo)
            hi = jnp.where(group == 3, pltpu.roll(parts[b + 1][0], 64, 1) if b < 2 else 0.0, hi)
            put(f, b, 0, r0, lo)
            put(f, b, 1, r0, hi)

    def inputs_of(f, ox, oy, ny):
        return shifted[f, ox, :, 16 * oy : 16 * oy + 16 * ny].reshape(48 * ny, 256)

    def conv(f, slot, back, y0, ny):
        lhs = jnp.concatenate([inputs_of(f, ox, y0 + oy, ny) for ox in range(3) for oy in range(3)], axis=1)
        if back:
            rhs, dims = jnp.concatenate([bands[slot, t] for t in range(9)], axis=1), NT
        else:
            rhs, dims = bands[slot].reshape(9 * 256, 256), NN
        pre[slot, :, 16 * y0 : 16 * y0 + 16 * ny] = dot(lhs, rhs, dims).reshape(3, 16 * ny, 256)

    def send_rows(f, rows):
        square = ones_at(iota((216, 216), 0) == iota((216, 216), 1))
        four = jnp.concatenate([rows[...]] * 4, axis=0)
        full = jnp.concatenate([dot(square, four, NT), jnp.zeros((8, 128), F32)], axis=0)
        packed = pick(group, [full[56 * g : 56 * g + 56] for g in range(4)])
        packed = jnp.concatenate([packed, jnp.zeros((8, 128), F32)], axis=0).astype(BF16)
        wsend[f] = packed
        wrecv[f, dp] = packed

    def share_rows(f):
        sems = (filt_send, filt_recv)
        for peer in dp_peers:
            send(wsend.at[f], wrecv.at[f, dp], sems, f, peer)
        return [batch(wrecv.at[f, 0:3], sems, f)]

    def filter_rows(f):
        for g8 in range(108):
            src, rr = g8 // 27, g8 % 27
            g, r = rr // 7, rr % 7
            part = wrecv[f, src, 16 * (r // 2) : 16 * (r // 2) + 16].astype(F32)[8 * (r % 2) : 8 * (r % 2) + 8]
            wrows[8 * g8 : 8 * g8 + 8] = jnp.where(group == g, part, 0.0)
        again = ones_at(iota((128, 128), 0) % C == iota((128, 128), 1) % C)
        rep[f] = dot(wrows[...].astype(BF16), again).reshape(27, C, 128)

    def tap(ox, oy, oz):
        ty = oy if oy == 1 else jnp.where(ry == 0, oy, 2 - oy)
        tz = oz if oz == 1 else jnp.where(rz == 0, oz, 2 - oz)
        return 9 * ox + 3 * ty + tz

    def band(f):
        for ox in range(3):
            for oy in range(3):
                taps = [rep[f, tap(ox, oy, oz)] for oz in range(3)]
                for v in range(2):
                    for zi in range(8):
                        parts = []
                        for g in range(4):
                            zo = 4 * v + g
                            parts.append(taps[zi - zo + 1] if 1 <= zo <= 6 and abs(zi - zo) <= 1 else None)
                        if any(p is not None for p in parts):
                            value = pick(group, parts).astype(BF16)
                        else:
                            value = jnp.zeros((C, 128), BF16)
                        bands[f, 3 * ox + oy, C * zi : C * zi + C, 128 * v : 128 * v + 128] = value

    def band_back(f):
        for sx in range(3):
            for sy in range(3):
                taps = [rep[f, tap(2 - sx, 2 - sy, oz)] for oz in range(3)]
                for v in range(2):
                    for zo in range(8):
                        parts = []
                        for g in range(4):
                            zi = 4 * v + g
                            parts.append(taps[zo - zi + 1] if 1 <= zo <= 6 and abs(zi - zo) <= 1 else None)
                        if any(p is not None for p in parts):
                            value = pick(group, parts).astype(BF16)
                        else:
                            value = jnp.zeros((C, 128), BF16)
                        bands[2 + f, 3 * sx + sy, C * zo : C * zo + C, 128 * v : 128 * v + 128] = value

    def natural(blocked):
        rows = jnp.concatenate([dot(pack[...], blocked[b]) for b in range(3)], axis=1).astype(BF16)
        return dot(rows, unplace[...])

    def depart(field, out):
        for w in range(4):
            nat[w] = field[:, 128 * w : 128 * w + 128]
        for x in range(8):
            for w in range(4):
                value = nat[w, pl.ds(x, 16, stride=8), :]
                for g in range(4):
                    at = 16 * (4 * w + g)
                    wide[at : at + 16, 128 * x : 128 * x + 128] = jnp.where(group == g, value, 0.0).astype(BF16)
        cells = dot(copies8[...], wide[...], NT).astype(BF16)
        out[0, 0] = dot(cells, turn[...]).reshape(C, 8, 256).astype(BF16)

    def filter_gradient(f, r):
        gradient = owned[f].reshape(768, 256)
        odd, high = group % 2 == 1, group >= 2
        for t in range(9):
            product[f, t] = dot(gradient, inputs_of(r, t // 3, t % 3, 16), TN)
            for oz in range(3):
                a = []
                for j in range(4):
                    sides = []
                    for v in range(2):
                        parts = []
                        for g in range(4):
                            zo = 4 * v + g - (oz - 1)
                            at = zo * C + 8 * j
                            parts.append(product[f, t, at : at + 8, 128 * v : 128 * v + 128] if 1 <= zo <= 6 else None)
                        sides.append(pick(group, parts))
                    a.append(sides[0] + sides[1])
                pairs = [
                    jnp.where(odd, a[i + 1], a[i]) + pltpu.roll(jnp.where(odd, a[i], a[i + 1]), 32, 1) for i in (0, 2)
                ]
                tap_tile[f, tap(t // 3, t % 3, oz)] = jnp.where(high, pairs[1], pairs[0]) + pltpu.roll(
                    jnp.where(high, pairs[0], pairs[1]), 64, 1
                )
        for q in range(4):
            for k in range(8):
                source = STARTS[q] + k
                pile[f, k // 4, 4 * (k % 4) + q] = (
                    tap_tile[f, source] if source < 27 else jnp.zeros((8, 128), F32)
                )
        send(pile.at[f, 1 - rz], pair_in.at[f], (pair_send, pair_recv), f, (column[2], dp))
        return batch(pair_in.at[f], (pair_send, pair_recv), f)

    loads[0].wait()
    loads[1].wait()
    flag = kept[...].astype(F32)
    kept_cells = jnp.zeros((1, 256), F32)
    for b in range(4):
        kept_cells = jnp.where(tile == b, flag[:, b : b + 1], kept_cells)
    field = jnp.where(kept_cells > 0.5, vin[...].astype(F32).reshape(256, 256), GONE)
    field = turn_in(0, field)
    show(0, 3, sel3[...], field)
    loads[2].wait()
    loads[3].wait()
    send_rows(0, rows_in.at[0])
    send_rows(1, rows_in.at[1])
    pl.semaphore_wait(barrier, len(greeted))
    volume_near, volume_far = give(0, 3)
    row_moves = [share_rows(0), share_rows(1)]

    near3[...], far3[...] = assemble(3)
    k, n = iota((256, 256), 0), iota((256, 256), 1)
    place0[...] = ones_at(n - k == C)
    k, n = iota((384, 256), 0), iota((384, 256), 1)
    place1[...] = ones_at(k - n == C)
    place2[...] = ones_at(k - n == jnp.where(n < 160, 96, 128))
    sel1[...] = faces_of(1)
    loads[4].wait()
    show(1, 1, sel1[...], turn_in(1, cin[...].astype(F32).reshape(256, 256)))
    cot_near, cot_far = give(1, 1)
    near1[...], far1[...] = assemble(1)
    row, col = iota((128, 256), 0), iota((128, 256), 1)
    pack[...] = ones_at(col == 16 * (row // 8) + row % 8 + 4)
    for b in range(3):
        k, n = iota((256, 640), 0), iota((256, 640), 1)
        zi, z = k // C, 6 * b + k // C - 1
        good = (zi >= 1) & (zi <= 6) & (z < 16) & (k % C == n % C)
        unplace[256 * b : 256 * b + 256] = ones_at(
            good & (((n < 512) & (n // C == z)) | ((n >= 544) & (16 - (n // C - 16) == z)))
        )
    x = iota((304, 128), 0) % 16 - 4
    inside[...] = jnp.where(((x < 0) & ~has_below) | ((x >= 8) & ~has_above), 0.0, 1.0)
    for f in range(4):
        for ox in range(3):
            for b in range(3):
                shifted[f, ox, b, 0:16] = jnp.zeros((16, 256), BF16)

    for f in range(2):
        for move in row_moves[f]:
            move.wait_recv()
        filter_rows(f)
        band(f)
        band_back(f)

    take(0, 3, near3, 0, volume_near, blk)

    def first(y):
        rows = slice(16 * y, 16 * y + 16)
        here = inside[rows, :]
        for b in range(3):
            for v in range(2):
                lanes = slice(128 * v, 128 * v + 128)
                value = blk[b, rows, lanes]
                kept_here = jnp.where(value == GONE, 0.0, here)
                keep[b, rows, lanes] = kept_here
                put(0, b, v, 16 * y, value * kept_here)

    def second(y):
        rows = slice(16 * y, 16 * y + 16)
        parts = []
        for b in range(3):
            value, there = pre[0, b, rows, :], keep[b, rows, :]
            gate = logistic(value)
            act = value * gate
            slope[b, rows, :] = (gate + act * (1.0 - gate)) * there
            parts.append(halves(act * there))
        put_all(1, 16 * y, parts)

    x = iota((16, 128), 0) - 4
    own = [jnp.where((x >= 0) & (x < 8), 1.0, 0.0)]
    own.append(jnp.where(group == 0, own[0], 0.0))
    own_lanes = [jnp.concatenate([own[0], own[b // 2]], axis=1) for b in range(3)]

    def third(y):
        rows = slice(16 * y, 16 * y + 16)
        parts = []
        for b in range(3):
            value, there = pre[1, b, rows, :], keep[b, rows, :]
            gate = logistic(value)
            act = value * gate
            grad = cot[b, rows, :] * there * (gate + act * (1.0 - gate))
            parts.append(halves(grad))
            if y < 16:
                leaving[b, rows, :] = (act * there).astype(BF16)
                owned[1, b, rows, :] = (grad * own_lanes[b]).astype(BF16)
        put_all(2, 16 * y, parts)

    def fourth(y):
        rows = slice(16 * y, 16 * y + 16)
        for b in range(3):
            owned[0, b, rows, :] = (pre[3, b, rows, :] * slope[b, rows, :] * own_lanes[b]).astype(BF16)

    def run(body, first_y, end):
        for y in range(first_y, end):
            body(y)

    run(first, 0, 8)
    conv(0, 0, False, 0, 6)
    run(first, 8, 16)
    conv(0, 0, False, 6, 6)
    run(second, 0, 6)
    take(0, 3, far3, 1, volume_far, blk)
    run(first, 16, 19)
    conv(0, 0, False, 12, 6)
    run(second, 6, 12)
    conv(1, 1, False, 0, 6)
    run(second, 12, 18)
    conv(1, 1, False, 6, 6)
    take(1, 1, near1, 0, cot_near, cot)
    run(third, 0, 6)
    conv(1, 1, False, 12, 5)
    run(third, 6, 12)
    conv(2, 3, True, 0, 6)
    run(third, 12, 16)
    take(1, 1, far1, 1, cot_far, cot)
    run(third, 16, 17)
    conv(2, 3, True, 6, 5)
    run(fourth, 0, 6)
    conv(2, 3, True, 11, 5)
    run(fourth, 6, 16)
    pair_one = filter_gradient(0, 0)
    pair_two = filter_gradient(1, 1)
    show(2, 1, sel1[...], natural(owned[0]).astype(BF16))
    grad_near, grad_far = give(2, 1)
    for f, move in ((0, pair_one), (1, pair_two)):
        move.wait_recv()
        for s in range(16):
            crossing[s, f] = pile[f, rz, s] + pair_in[f, s]
    for s, peer in zip(xy_slots, xy_peers):
        send(crossing.at[s], xy_in.at[xy], (xy_send, xy_recv), 0, peer)
    xy_moves = [batch(xy_in.at[0:15], (xy_send, xy_recv), 0)]
    xy_in[xy] = crossing[xy]

    depart(natural(leaving[...]), act_out)
    for move in xy_moves:
        move.wait_recv()
    total = xy_in[0]
    for s in range(1, 16):
        total = total + xy_in[s]
    z_in[pz] = total.reshape(16, 128).astype(BF16)
    for peer in z_peers:
        send(z_in.at[pz], z_in.at[pz], (z_send, z_recv), 0, peer)
    z_moves = [batch(z_in.at[0:7], (z_send, z_recv), 0)]

    take(2, 1, near1, 0, grad_near, blk)

    def fifth(y):
        rows = slice(16 * y, 16 * y + 16)
        here = inside[rows, :]
        for b in range(3):
            for v in range(2):
                put(3, b, v, 16 * y, blk[b, rows, 128 * v : 128 * v + 128] * here)

    def sixth(y):
        rows = slice(16 * y, 16 * y + 16)
        for b in range(3):
            leaving[b, rows, :] = (pre[2, b, rows, :] * keep[b, rows, :]).astype(BF16)

    run(fifth, 0, 8)
    conv(3, 2, True, 0, 6)
    run(fifth, 8, 16)
    conv(3, 2, True, 6, 5)
    run(sixth, 0, 6)
    take(2, 1, far1, 1, grad_far, blk)
    run(fifth, 16, 17)
    conv(3, 2, True, 11, 5)
    run(sixth, 6, 16)
    depart(natural(leaving[...]), gin_out)

    for move in z_moves:
        move.wait_recv()
    total = z_in[0].astype(F32)
    for s in range(1, 8):
        total = total + z_in[s].astype(F32)
    xc_in[xc] = (total * (1.0 / math.sqrt(4 * count * 2048))).astype(BF16)
    for peer in xc_peers:
        send(xc_in.at[xc], xc_in.at[xc], (xc_send, xc_recv), 0, peer)
    xc_moves = [batch(xc_in.at[0:7], (xc_send, xc_recv), 0)]
    for move in xc_moves:
        move.wait_recv()
    offset = lax.rem(4 - dp, 4) * 8
    for f, out in enumerate((grad_one_out, grad_two_out)):
        for j in range(4):
            for w in range(2):
                parts = []
                for g in range(4):
                    value = xc_in[4 * w + g].astype(F32)[8 * f : 8 * f + 8]
                    parts.append(value if g == j else pltpu.roll(value, 32 * ((g - j) % 4), 1))
                final[8 * j : 8 * j + 8, 128 * w : 128 * w + 128] = pick(group, parts)
        out[...] = pltpu.roll(final[...], 256 - offset, 1)[:, :216]

    for copy in started:
        copy.wait_send()


def hand_over(*refs):
    copies = [pltpu.make_async_copy(refs[i], refs[4 + i], refs[8].at[i]) for i in range(4)]
    for copy in copies:
        copy.start()
    for copy in copies:
        copy.wait()


def on_device(volume, tissue_kept, filter_one, filter_two, cotangent):
    vmem, anywhere = pl.BlockSpec(memory_space=pltpu.VMEM), pl.BlockSpec(memory_space=pl.ANY)
    dma = pltpu.SemaphoreType.DMA
    field, grad = (volume.shape, BF16), ((C, 216), F32)
    results = (field, field, grad, grad)
    blocked = pltpu.VMEM((3, 304, 256), F32)
    held = pl.pallas_call(
        kernel,
        out_shape=tuple(pltpu.VMEM(*r) for r in results),
        in_specs=[anywhere] * 5,
        out_specs=(vmem,) * 4,
        scratch_shapes=[
            pltpu.VMEM((1, 4), jnp.int32),
            pltpu.VMEM((2, C, 216), BF16),
            pltpu.VMEM((C, 8, 256), BF16),
            pltpu.VMEM((C, 8, 256), BF16),
            pltpu.VMEM((256, 1024), F32),
            pltpu.VMEM((5, 128, 128), F32),
            pltpu.VMEM((3, 128, 512), BF16),
            pltpu.VMEM((3, 128, 128), BF16),
            pltpu.VMEM((3, 2, 48, 512), BF16),
            pltpu.VMEM((3, 2, 48, 128), BF16),
            pltpu.VMEM((3, 288, 512), BF16),
            pltpu.VMEM((3, 288, 128), BF16),
            blocked,
            blocked,
            blocked,
            blocked,
            pltpu.VMEM((4, 3, 288, 256), F32),
            pltpu.VMEM((4, 3, 3, 320, 256), BF16),
            pltpu.VMEM((4, 9, 256, 256), BF16),
            pltpu.VMEM((3, 256, 256), BF16),
            pltpu.VMEM((2, 3, 256, 256), BF16),
            pltpu.VMEM((256, 1024), BF16),
            pltpu.VMEM((2, 64, 128), BF16),
            pltpu.VMEM((2, 4, 64, 128), BF16),
            pltpu.VMEM((864, 128), F32),
            pltpu.VMEM((2, 27, C, 128), F32),
            pltpu.VMEM((2, 9, 256, 256), F32),
            pltpu.VMEM((2, 27, 8, 128), F32),
            pltpu.VMEM((2, 2, 16, 8, 128), F32),
            pltpu.VMEM((2, 16, 8, 128), F32),
            pltpu.VMEM((16, 2, 8, 128), F32),
            pltpu.VMEM((16, 2, 8, 128), F32),
            pltpu.VMEM((8, 16, 128), BF16),
            pltpu.VMEM((8, 16, 128), BF16),
            pltpu.VMEM((C, 256), F32),
            pltpu.VMEM((256, 256), BF16),
            pltpu.VMEM((256, 1024), BF16),
            pltpu.VMEM((96, 128), BF16),
            pltpu.VMEM((32, 128), BF16),
            pltpu.VMEM((256, 224), BF16),
            pltpu.VMEM((48, 64), BF16),
            pltpu.VMEM((256, 160), BF16),
            pltpu.VMEM((48, 48), BF16),
            pltpu.VMEM((256, 256), BF16),
            pltpu.VMEM((384, 256), BF16),
            pltpu.VMEM((384, 256), BF16),
            pltpu.VMEM((128, 256), BF16),
            pltpu.VMEM((768, 640), BF16),
            pltpu.VMEM((304, 128), F32),
            dma((5,)), dma((3, 4)), dma((3, 4)), dma((2,)), dma((2,)),
            dma((2,)), dma((2,)), dma((1,)), dma((1,)), dma((1,)), dma((1,)), dma((1,)), dma((1,)),
        ],
        compiler_params=pltpu.CompilerParams(
            collective_id=0, has_side_effects=True, vmem_limit_bytes=60 * 1024 * 1024
        ),
    )(tissue_kept, filter_one.T, filter_two.T, volume, cotangent)
    act, gin, one, two = pl.pallas_call(
        hand_over,
        out_shape=tuple(jax.ShapeDtypeStruct(*r) for r in results),
        in_specs=[anywhere] * 4,
        out_specs=(anywhere,) * 4,
        scratch_shapes=[dma((4,))],
    )(*(pltpu.with_memory_space_constraint(part, pltpu.VMEM) for part in held))
    return act, gin, one.T, two.T


def solution(mesh):
    field, rows = P("dp", "space", None, None, None), P("dp", None)
    return jax.shard_map(
        on_device,
        mesh=mesh,
        in_specs=(field, P("dp", "space", None), rows, rows, field),
        out_specs=(field, field, rows, rows),
        check_vma=False,
    )
```

```python
import math

import jax
import jax.numpy as jnp
from jax import lax
from jax.experimental import pallas as pl
from jax.experimental.pallas import tpu as pltpu
from jax.sharding import PartitionSpec as P

MESH = pl.DeviceIdType.MESH
F32 = jnp.float32
BF16 = jnp.bfloat16
NN = (((1,), (0,)), ((), ()))
NT = (((1,), (1,)), ((), ()))
TN = (((0,), (0,)), ((), ()))

C = 32
GONE = 64.0
STARTS = (0, 6, 13, 20)


def dot(a, b, dims=NN):
    return lax.dot_general(a, b, dims, preferred_element_type=F32)


def iota(shape, axis):
    return lax.broadcasted_iota(jnp.int32, shape, axis)


def ones_at(cond):
    return jnp.where(cond, 1.0, 0.0).astype(BF16)


def pick(group, parts):
    value = None
    for g in range(len(parts) - 1, -1, -1):
        part = 0.0 if parts[g] is None else parts[g]
        if value is None:
            value = part
        elif not (parts[g] is None and isinstance(value, float)):
            value = jnp.where(group == g, part, value)
    return value


def x_of(row):
    x = row % 16
    return jnp.where(x < 12, x, x - 16)


def logistic(v):
    return 1.0 / (1.0 + jnp.exp(-v))


def layout(h):
    yrows = 32 if h == 3 else 16
    low, high, beyond = 128, 128 + 16 * h, 128 + 32 * h
    return yrows, low, high, beyond, beyond + yrows, beyond + yrows + 16, beyond + yrows + 32


def kernel(
    flags, filter_one, filter_two, volume, cotangent,
    act_out, gin_out, grad_one_out, grad_two_out,
    kept, rows_in, vin, cin, spread, nat, nat_main, nat_z, face_main, face_z, stack_main, stack_z,
    blk, cot, keep, slope, pre, back, shifted, packed, bands, leaving, owned, wide,
    wsend, wrecv, wrows, rep, product, tap_tile, pile, pair_in, crossing, xy_in, z_in, xc_in, final,
    turn, copies8, sel3, sel1, near3, far3, near1, far1, place0, place1, place2, unplace, inside,
    local_sem, halo_send, halo_recv, filt_send, filt_recv,
    pair_send, pair_recv, xy_send, xy_recv, z_send, z_recv, xc_send, xc_recv,
):
    space = lax.axis_index("space")
    dp = lax.axis_index("dp")
    count = lax.axis_size("space")
    rx, ry, rz = space // 4, (space // 2) % 2, space % 2
    bx, pz = space // 16, (space // 2) % 8
    has_below, has_above = rx > 0, rx < count // 4 - 1
    started = []

    loads = [
        pltpu.make_async_copy(volume.at[0, 0], vin, local_sem.at[0]),
        pltpu.make_async_copy(flags.at[0], kept, local_sem.at[1]),
        pltpu.make_async_copy(filter_one, rows_in.at[0], local_sem.at[2]),
        pltpu.make_async_copy(filter_two, rows_in.at[1], local_sem.at[3]),
        pltpu.make_async_copy(cotangent.at[0, 0], cin, local_sem.at[4]),
    ]
    for load in loads:
        load.start()

    def send(src, dst, sems, at, peer):
        pltpu.make_async_remote_copy(
            src_ref=src, dst_ref=dst, send_sem=sems[0].at[at], recv_sem=sems[1].at[at],
            device_id=peer, device_id_type=MESH,
        ).start()

    def batch(ref, sems, at):
        copy = pltpu.make_async_remote_copy(
            src_ref=ref, dst_ref=ref, send_sem=sems[0].at[at], recv_sem=sems[1].at[at],
            device_id=dp_peers[0], device_id_type=MESH,
        )
        started.append(copy)
        return copy

    base = space - 2 * ry - rz
    column = (space, base + 2 * (1 - ry) + rz, base + 2 * ry + (1 - rz), base + 2 * (1 - ry) + (1 - rz))
    below = [lax.rem(d - 4 + count, count) for d in column]
    above = [lax.rem(d + 4, count) for d in column]
    xy = bx * 4 + dp
    hops = lambda d: min(d, 4 - d)
    steps = sorted([(i // 4, i % 4) for i in range(1, 16)], key=lambda d: -hops(d[0]) - hops(d[1]))
    xy_slots = [lax.rem(bx + i, 4) * 4 + lax.rem(dp + j, 4) for i, j in steps]
    xy_peers = [((s // 4) * 16 + lax.rem(space, 16), s % 4) for s in xy_slots]
    z_peers = [(bx * 16 + 2 * lax.rem(pz + k, 8) + rz, dp) for k in (4, 3, 5, 2, 6, 1, 7)]
    xc = rz * 4 + bx
    steps = ((1, 2), (0, 2), (1, 1), (1, 3), (0, 1), (0, 3), (1, 0))
    xc_slots = [lax.rem(rz + i, 2) * 4 + lax.rem(bx + j, 4) for i, j in steps]
    xc_peers = [((s % 4) * 16 + 2 * pz + s // 4, dp) for s in xc_slots]
    dp_peers = [(space, lax.rem(dp + k, 4)) for k in range(1, 4)]

    barrier = pltpu.get_barrier_semaphore()
    greeted = [(d, dp) for d in column[1:]] + [(d, dp) for d in below + above] + xy_peers + z_peers + xc_peers
    for peer in greeted:
        pl.semaphore_signal(barrier, inc=1, device_id=peer, device_id_type=MESH)

    group = iota((1, 128), 1) // C

    row, col = iota((256, 256), 0), iota((256, 256), 1)
    y, z = row % 16, row // 16
    turn[...] = ones_at(col == 16 * jnp.where(ry == 0, y, 15 - y) + jnp.where(rz == 0, z, 15 - z))
    row, col = iota((256, 128), 0), iota((256, 128), 1)
    for x in range(8):
        copies8[:, 128 * x : 128 * x + 128] = ones_at(row == 8 * (col % C) + x)

    def faces_of(h):
        row, col = iota((32 * h, 128), 0), iota((32 * h, 128), 1)
        y, x = col // 8, col % 8
        return ones_at(
            ((x < h) & (row == h * y + x)) | ((x >= 8 - h) & (row == 16 * h + h * y + x - (8 - h)))
        )

    sel3[...] = faces_of(3)

    cell = iota((1, 256), 1)
    tile = 2 * (cell // 128) + (cell % 16) // 8

    def turn_in(f, field):
        cells = dot(turn[...], field.astype(BF16), NT).astype(BF16)
        spread[...] = dot(cells, copies8[...])
        for x in range(8):
            for w in range(5):
                layers = [4 * w + g for g in range(4)] if w < 4 else [None, 15, 14, 13]
                parts = [None if l is None else spread[16 * l : 16 * l + 16, 128 * x : 128 * x + 128] for l in layers]
                nat[w, pl.ds(x, 16, stride=8), :] = pick(group, parts)
        return jnp.concatenate([nat[w] for w in range(5)], axis=1).astype(BF16)

    def show(f, h, sel, field):
        main, last = field[:, :512], field[:, 512:]
        nat_main[f] = main
        nat_z[f] = last
        stack_main[f, 0:128] = main
        faces = dot(sel, field).astype(BF16)
        for side in range(2):
            face_main[f, side, 0 : 16 * h] = faces[16 * h * side : 16 * h * side + 16 * h, :512]
            face_z[f, side, 0 : 16 * h] = faces[16 * h * side : 16 * h * side + 16 * h, 512:]

    def give(f, h):
        yrows, low, high, beyond, corner_low, corner_high, total = layout(h)
        sems = (halo_send, halo_recv)

        def add(src, dst, d, kind):
            send(src, dst, sems, (f, kind), (d, dp))

        ends = ((1, low, corner_low, above), (0, high, corner_high, below))
        for side, at, _, to in ends:
            add(face_z.at[f, side, 0 : 16 * h], stack_z.at[f, at : at + 16 * h], to[2], 1)
        for side, _, corner, to in ends:
            add(face_z.at[f, side, 16 * h - 16 : 16 * h], stack_z.at[f, corner : corner + 16], to[3], 3)
        for side, at, _, to in ends:
            add(face_main.at[f, side, 0 : 16 * h], stack_main.at[f, at : at + 16 * h], to[0], 0)
        for side, _, corner, to in ends:
            add(face_main.at[f, side, 16 * h - 16 : 16 * h], stack_main.at[f, corner : corner + 16], to[1], 2)
        add(nat_z.at[f], stack_z.at[f, 0:128], column[2], 1)
        add(nat_main.at[f, 128 - yrows : 128], stack_main.at[f, beyond : beyond + yrows], column[1], 2)
        add(nat_z.at[f, 128 - yrows : 128], stack_z.at[f, beyond : beyond + yrows], column[3], 3)
        near = [batch(stack_main.at[f, 128:beyond], sems, (f, 0)), batch(stack_z.at[f, 0:beyond], sems, (f, 1))]
        far = [
            batch(stack_main.at[f, beyond:total], sems, (f, 2)), batch(stack_z.at[f, beyond:total], sems, (f, 3))
        ]
        return near, far

    def assemble(h):
        yrows, low, high, beyond, corner_low, corner_high, total = layout(h)
        row, col = iota((256, beyond), 0), iota((256, beyond), 1)
        y, x = row // 16, x_of(row)
        at = jnp.where((x >= 0) & (x < 8), 8 * y + x, -1)
        at = jnp.where((x < 0) & (x >= -h), low + h * y + x + h, at)
        at = jnp.where((x >= 8) & (x < 8 + h), high + h * y + x - 8, at)
        near = ones_at(at == col)
        row, col = iota((48, total - beyond), 0), iota((48, total - beyond), 1)
        y, x = row // 16, x_of(row)
        there, skip = 15 - y, 16 * h - 16
        at = jnp.where((x >= 0) & (x < 8), 8 * (there - (16 - yrows // 8)) + x, -1)
        at = jnp.where((x < 0) & (x >= -h), yrows + h * there + x + h - skip, at)
        at = jnp.where((x >= 8) & (x < 8 + h), yrows + 16 + h * there + x - 8 - skip, at)
        return near, ones_at((at == col) & (y < h))

    def take(f, h, rows, part, moves, into):
        for move in moves:
            move.wait_recv()
        beyond, total = layout(h)[3], layout(h)[-1]
        start, end = ((0, beyond), (beyond, total))[part]
        pieces = jnp.concatenate([stack_main[f, start:end], stack_z[f, start:end]], axis=1)
        whole = dot(rows[...], pieces).astype(BF16)
        to = slice(256 * part, 256 + 48 * part)
        into[0, to] = dot(whole[:, 0:256], place0[...])
        into[1, to] = dot(whole[:, 128:512], place1[...])
        into[2, to] = dot(whole[:, 256:640], place2[...])

    def halves(value):
        return value[:, :128], value[:, 128:]

    last_own = {}

    def put(f, b, v, y, value):
        lanes = slice(128 * v, 128 * v + 128)
        for ox, moved in enumerate((pltpu.roll(value, 1, 0), value, pltpu.roll(value, 15, 0))):
            if f < 2:
                shifted[f, ox, b, 16 * y + 16 : 16 * y + 32, lanes] = moved.astype(BF16)
            if y <= 16:
                key = (f, ox, b, v)
                before = last_own[key] if y > 0 else jnp.zeros((8, 128), F32)
                last_own[key] = moved[0:8]
                at = 8 * (y - 1) if y % 2 == 1 else 128 + 8 * y
                packed[f, ox, b, at : at + 16, lanes] = jnp.concatenate([before, moved[0:8]], axis=0).astype(BF16)

    def put_all(f, y, parts):
        for b in range(3):
            lo, hi = parts[b]
            lo = jnp.where(group == 0, pltpu.roll(parts[b - 1][1], 64, 1) if b > 0 else 0.0, lo)
            hi = jnp.where(group == 3, pltpu.roll(parts[b + 1][0], 64, 1) if b < 2 else 0.0, hi)
            put(f, b, 0, y, lo)
            put(f, b, 1, y, hi)

    def own_inputs(f, ox, oy, y0, ny):
        at = 8 * y0 + (128 if oy == 0 else 0 if oy == 1 else 144)
        return packed[f, ox, :, at : at + 8 * ny].reshape(24 * ny, 256)

    def inputs_of(f, ox, oy, ny):
        return shifted[f, ox, :, 16 * oy : 16 * oy + 16 * ny].reshape(48 * ny, 256)

    def conv(f, y0, ny):
        lhs = jnp.concatenate([inputs_of(f, ox, y0 + oy, ny) for ox in range(3) for oy in range(3)], axis=1)
        pre[f, :, 16 * y0 : 16 * y0 + 16 * ny] = dot(lhs, bands[f].reshape(9 * 256, 256)).reshape(3, 16 * ny, 256)

    def conv_back(f, slot, y0, ny):
        lhs = jnp.concatenate([own_inputs(f, ox, oy, y0, ny) for ox in range(3) for oy in range(3)], axis=1)
        rhs = jnp.concatenate([bands[slot, t] for t in range(9)], axis=1)
        back[f - 2, :, 8 * y0 : 8 * y0 + 8 * ny] = dot(lhs, rhs, NT).reshape(3, 8 * ny, 256)

    def send_rows(f, rows):
        square = ones_at(iota((216, 216), 0) == iota((216, 216), 1))
        four = jnp.concatenate([rows[...]] * 4, axis=0)
        full = jnp.concatenate([dot(square, four, NT), jnp.zeros((8, 128), F32)], axis=0)
        lined = pick(group, [full[56 * g : 56 * g + 56] for g in range(4)])
        lined = jnp.concatenate([lined, jnp.zeros((8, 128), F32)], axis=0).astype(BF16)
        wsend[f] = lined
        wrecv[f, dp] = lined

    def share_rows(f):
        sems = (filt_send, filt_recv)
        for peer in dp_peers:
            send(wsend.at[f], wrecv.at[f, dp], sems, f, peer)
        return [batch(wrecv.at[f, 0:3], sems, f)]

    def filter_rows(f):
        for g8 in range(108):
            src, rr = g8 // 27, g8 % 27
            g, r = rr // 7, rr % 7
            part = wrecv[f, src, 16 * (r // 2) : 16 * (r // 2) + 16].astype(F32)[8 * (r % 2) : 8 * (r % 2) + 8]
            wrows[8 * g8 : 8 * g8 + 8] = jnp.where(group == g, part, 0.0)
        again = ones_at(iota((128, 128), 0) % C == iota((128, 128), 1) % C)
        rep[f] = dot(wrows[...].astype(BF16), again).reshape(27, C, 128)

    def tap(ox, oy, oz):
        ty = oy if oy == 1 else jnp.where(ry == 0, oy, 2 - oy)
        tz = oz if oz == 1 else jnp.where(rz == 0, oz, 2 - oz)
        return 9 * ox + 3 * ty + tz

    def band(f):
        for ox in range(3):
            for oy in range(3):
                taps = [rep[f, tap(ox, oy, oz)] for oz in range(3)]
                for v in range(2):
                    for zi in range(8):
                        parts = []
                        for g in range(4):
                            zo = 4 * v + g
                            parts.append(taps[zi - zo + 1] if 1 <= zo <= 6 and abs(zi - zo) <= 1 else None)
                        if any(p is not None for p in parts):
                            value = pick(group, parts).astype(BF16)
                        else:
                            value = jnp.zeros((C, 128), BF16)
                        bands[f, 3 * ox + oy, C * zi : C * zi + C, 128 * v : 128 * v + 128] = value

    def band_back(f):
        for sx in range(3):
            for sy in range(3):
                taps = [rep[f, tap(2 - sx, 2 - sy, oz)] for oz in range(3)]
                for v in range(2):
                    for zo in range(8):
                        parts = []
                        for g in range(4):
                            zi = 4 * v + g
                            parts.append(taps[zo - zi + 1] if 1 <= zo <= 6 and abs(zi - zo) <= 1 else None)
                        if any(p is not None for p in parts):
                            value = pick(group, parts).astype(BF16)
                        else:
                            value = jnp.zeros((C, 128), BF16)
                        bands[2 + f, 3 * sx + sy, C * zo : C * zo + C, 128 * v : 128 * v + 128] = value

    def natural(blocked):
        return dot(jnp.concatenate([blocked[b] for b in range(3)], axis=1), unplace[...])

    def depart(field, out):
        for w in range(4):
            nat[w] = field[:, 128 * w : 128 * w + 128]
        for x in range(8):
            for w in range(4):
                value = nat[w, pl.ds(x, 16, stride=8), :]
                for g in range(4):
                    at = 16 * (4 * w + g)
                    wide[at : at + 16, 128 * x : 128 * x + 128] = jnp.where(group == g, value, 0.0).astype(BF16)
        cells = dot(copies8[...], wide[...], NT).astype(BF16)
        out[0, 0] = dot(cells, turn[...]).reshape(C, 8, 256).astype(BF16)

    def filter_gradient(f, r):
        gradient = owned[f].reshape(384, 256)
        odd, high = group % 2 == 1, group >= 2
        for t in range(9):
            product[f, t] = dot(gradient, own_inputs(r, t // 3, t % 3, 0, 16), TN)
            for oz in range(3):
                a = []
                for j in range(4):
                    sides = []
                    for v in range(2):
                        parts = []
                        for g in range(4):
                            zo = 4 * v + g - (oz - 1)
                            at = zo * C + 8 * j
                            parts.append(product[f, t, at : at + 8, 128 * v : 128 * v + 128] if 1 <= zo <= 6 else None)
                        sides.append(pick(group, parts))
                    a.append(sides[0] + sides[1])
                pairs = [
                    jnp.where(odd, a[i + 1], a[i]) + pltpu.roll(jnp.where(odd, a[i], a[i + 1]), 32, 1) for i in (0, 2)
                ]
                tap_tile[f, tap(t // 3, t % 3, oz)] = jnp.where(high, pairs[1], pairs[0]) + pltpu.roll(
                    jnp.where(high, pairs[0], pairs[1]), 64, 1
                )
        for q in range(4):
            for k in range(8):
                source = STARTS[q] + k
                pile[f, k // 4, 4 * (k % 4) + q] = (
                    tap_tile[f, source] if source < 27 else jnp.zeros((8, 128), F32)
                )
        send(pile.at[f, 1 - rz], pair_in.at[f], (pair_send, pair_recv), f, (column[2], dp))
        return batch(pair_in.at[f], (pair_send, pair_recv), f)

    loads[0].wait()
    loads[1].wait()
    flag = kept[...].astype(F32)
    kept_cells = jnp.zeros((1, 256), F32)
    for b in range(4):
        kept_cells = jnp.where(tile == b, flag[:, b : b + 1], kept_cells)
    field = jnp.where(kept_cells > 0.5, vin[...].astype(F32).reshape(256, 256), GONE)
    field = turn_in(0, field)
    show(0, 3, sel3[...], field)
    pl.semaphore_wait(barrier, len(greeted))
    volume_near, volume_far = give(0, 3)
    loads[2].wait()
    loads[3].wait()
    send_rows(0, rows_in.at[0])
    row_moves = [share_rows(0)]
    send_rows(1, rows_in.at[1])
    row_moves.append(share_rows(1))

    near3[...], far3[...] = assemble(3)
    k, n = iota((256, 256), 0), iota((256, 256), 1)
    place0[...] = ones_at(n - k == C)
    k, n = iota((384, 256), 0), iota((384, 256), 1)
    place1[...] = ones_at(k - n == C)
    place2[...] = ones_at(k - n == jnp.where(n < 160, 96, 128))
    sel1[...] = faces_of(1)
    loads[4].wait()
    show(1, 1, sel1[...], turn_in(1, cin[...].astype(F32).reshape(256, 256)))
    cot_near, cot_far = give(1, 1)
    near1[...], far1[...] = assemble(1)
    for b in range(3):
        k, n = iota((256, 640), 0), iota((256, 640), 1)
        zi, z = k // C, 6 * b + k // C - 1
        good = (zi >= 1) & (zi <= 6) & (z < 16) & (k % C == n % C)
        unplace[256 * b : 256 * b + 256] = ones_at(
            good & (((n < 512) & (n // C == z)) | ((n >= 544) & (16 - (n // C - 16) == z)))
        )
    x = x_of(iota((304, 128), 0))
    inside[...] = jnp.where(((x < 0) & ~has_below) | ((x >= 8) & ~has_above), 0.0, 1.0)
    for f in range(2):
        for ox in range(3):
            for b in range(3):
                shifted[f, ox, b, 0:16] = jnp.zeros((16, 256), BF16)

    for f in range(2):
        for move in row_moves[f]:
            move.wait_recv()
        filter_rows(f)
        band(f)
        band_back(f)

    take(0, 3, near3, 0, volume_near, blk)

    def first(y):
        rows = slice(16 * y, 16 * y + 16)
        here = inside[rows, :]
        for b in range(3):
            for v in range(2):
                lanes = slice(128 * v, 128 * v + 128)
                value = blk[b, rows, lanes]
                kept_here = jnp.where(value == GONE, 0.0, here)
                keep[b, rows, lanes] = kept_here
                put(0, b, v, y, value * kept_here)

    def second(y):
        rows = slice(16 * y, 16 * y + 16)
        parts = []
        for b in range(3):
            value, there = pre[0, b, rows, :], keep[b, rows, :]
            gate = logistic(value)
            act = value * gate
            if y < 16:
                slope[b, 8 * y : 8 * y + 8, :] = ((gate + act * (1.0 - gate)) * there)[0:8]
            parts.append(halves(act * there))
        put_all(1, y, parts)

    own_lanes = [1.0, 1.0, jnp.where(iota((1, 256), 1) < 160, 1.0, 0.0)]

    def third(y):
        rows = slice(16 * y, 16 * y + 16)
        parts = []
        for b in range(3):
            value, there = pre[1, b, rows, :], keep[b, rows, :]
            gate = logistic(value)
            act = value * gate
            grad = cot[b, rows, :] * there * (gate + act * (1.0 - gate))
            parts.append(halves(grad))
            if y < 16:
                key, mine = ("own", b), ((act * there)[0:8], (grad * own_lanes[b])[0:8])
                if y % 2 == 1:
                    pair = [jnp.concatenate(p, axis=0).astype(BF16) for p in zip(last_own[key], mine)]
                    leaving[b, 8 * y - 8 : 8 * y + 8, :] = pair[0]
                    owned[1, b, 8 * y - 8 : 8 * y + 8, :] = pair[1]
                last_own[key] = mine
        put_all(2, y, parts)

    def fourth(y):
        rows = slice(8 * y, 8 * y + 16)
        for b in range(3):
            owned[0, b, rows, :] = (back[0, b, rows, :] * slope[b, rows, :] * own_lanes[b]).astype(BF16)

    def run(body, first_y, end, step=1):
        for y in range(first_y, end, step):
            body(y)

    run(first, 0, 8)
    conv(0, 0, 6)
    run(first, 8, 16)
    conv(0, 6, 6)
    run(second, 0, 6)
    take(0, 3, far3, 1, volume_far, blk)
    run(first, 16, 19)
    conv(0, 12, 6)
    run(second, 6, 12)
    conv(1, 0, 6)
    run(second, 12, 18)
    conv(1, 6, 6)
    take(1, 1, near1, 0, cot_near, cot)
    run(third, 0, 6)
    conv(1, 12, 5)
    run(third, 6, 12)
    run(third, 12, 16)
    conv_back(2, 3, 0, 8)
    take(1, 1, far1, 1, cot_far, cot)
    run(third, 16, 17)
    conv_back(2, 3, 8, 8)
    run(fourth, 0, 16, 2)
    pair_one = filter_gradient(0, 0)
    pair_two = filter_gradient(1, 1)
    show(2, 1, sel1[...], natural(owned[0]).astype(BF16))
    grad_near, grad_far = give(2, 1)
    for f, move in ((0, pair_one), (1, pair_two)):
        move.wait_recv()
        for s in range(16):
            crossing[s, f] = pile[f, rz, s] + pair_in[f, s]
    for s, peer in zip(xy_slots, xy_peers):
        send(crossing.at[s], xy_in.at[xy], (xy_send, xy_recv), 0, peer)
    xy_moves = [batch(xy_in.at[0:15], (xy_send, xy_recv), 0)]
    xy_in[xy] = crossing[xy]

    depart(natural(leaving[...]), act_out)
    for move in xy_moves:
        move.wait_recv()
    total = xy_in[0]
    for s in range(1, 16):
        total = total + xy_in[s]
    z_in[pz] = total.reshape(16, 128).astype(BF16)
    for peer in z_peers:
        send(z_in.at[pz], z_in.at[pz], (z_send, z_recv), 0, peer)
    z_moves = [batch(z_in.at[0:7], (z_send, z_recv), 0)]

    take(2, 1, near1, 0, grad_near, blk)

    def fifth(y):
        rows = slice(16 * y, 16 * y + 16)
        here = inside[rows, :]
        for b in range(3):
            for v in range(2):
                put(3, b, v, y, blk[b, rows, 128 * v : 128 * v + 128] * here)

    def sixth(y):
        rows = slice(8 * y, 8 * y + 16)
        for b in range(3):
            there = [keep[b, 16 * i : 16 * i + 8, :] for i in (y, y + 1)]
            leaving[b, rows, :] = (back[1, b, rows, :] * jnp.concatenate(there, axis=0)).astype(BF16)

    run(fifth, 0, 16)
    conv_back(3, 2, 0, 8)
    take(2, 1, far1, 1, grad_far, blk)
    run(fifth, 16, 17)
    conv_back(3, 2, 8, 8)
    run(sixth, 0, 16, 2)
    depart(natural(leaving[...]), gin_out)

    for move in z_moves:
        move.wait_recv()
    total = z_in[0].astype(F32)
    for s in range(1, 8):
        total = total + z_in[s].astype(F32)
    xc_in[xc] = (total * (1.0 / math.sqrt(4 * count * 2048))).astype(BF16)
    for peer in xc_peers:
        send(xc_in.at[xc], xc_in.at[xc], (xc_send, xc_recv), 0, peer)
    xc_moves = [batch(xc_in.at[0:7], (xc_send, xc_recv), 0)]
    for move in xc_moves:
        move.wait_recv()
    offset = lax.rem(4 - dp, 4) * 8
    for f, out in enumerate((grad_one_out, grad_two_out)):
        for j in range(4):
            for w in range(2):
                parts = []
                for g in range(4):
                    value = xc_in[4 * w + g].astype(F32)[8 * f : 8 * f + 8]
                    parts.append(value if g == j else pltpu.roll(value, 32 * ((g - j) % 4), 1))
                final[8 * j : 8 * j + 8, 128 * w : 128 * w + 128] = pick(group, parts)
        out[...] = pltpu.roll(final[...], 256 - offset, 1)[:, :216]

    for copy in started:
        copy.wait_send()


def hand_over(*refs):
    copies = [pltpu.make_async_copy(refs[i], refs[4 + i], refs[8].at[i]) for i in range(4)]
    for copy in copies:
        copy.start()
    for copy in copies:
        copy.wait()


def on_device(volume, tissue_kept, filter_one, filter_two, cotangent):
    vmem, anywhere = pl.BlockSpec(memory_space=pltpu.VMEM), pl.BlockSpec(memory_space=pl.ANY)
    dma = pltpu.SemaphoreType.DMA
    field, grad = (volume.shape, BF16), ((C, 216), F32)
    results = (field, field, grad, grad)
    blocked = pltpu.VMEM((3, 304, 256), F32)
    held = pl.pallas_call(
        kernel,
        out_shape=tuple(pltpu.VMEM(*r) for r in results),
        in_specs=[anywhere] * 5,
        out_specs=(vmem,) * 4,
        scratch_shapes=[
            pltpu.VMEM((1, 4), jnp.int32),
            pltpu.VMEM((2, C, 216), BF16),
            pltpu.VMEM((C, 8, 256), BF16),
            pltpu.VMEM((C, 8, 256), BF16),
            pltpu.VMEM((256, 1024), F32),
            pltpu.VMEM((5, 128, 128), F32),
            pltpu.VMEM((3, 128, 512), BF16),
            pltpu.VMEM((3, 128, 128), BF16),
            pltpu.VMEM((3, 2, 48, 512), BF16),
            pltpu.VMEM((3, 2, 48, 128), BF16),
            pltpu.VMEM((3, 288, 512), BF16),
            pltpu.VMEM((3, 288, 128), BF16),
            blocked,
            blocked,
            blocked,
            pltpu.VMEM((3, 128, 256), F32),
            pltpu.VMEM((2, 3, 288, 256), F32),
            pltpu.VMEM((2, 3, 128, 256), F32),
            pltpu.VMEM((2, 3, 3, 320, 256), BF16),
            pltpu.VMEM((4, 3, 3, 272, 256), BF16),
            pltpu.VMEM((4, 9, 256, 256), BF16),
            pltpu.VMEM((3, 128, 256), BF16),
            pltpu.VMEM((2, 3, 128, 256), BF16),
            pltpu.VMEM((256, 1024), BF16),
            pltpu.VMEM((2, 64, 128), BF16),
            pltpu.VMEM((2, 4, 64, 128), BF16),
            pltpu.VMEM((864, 128), F32),
            pltpu.VMEM((2, 27, C, 128), F32),
            pltpu.VMEM((2, 9, 256, 256), F32),
            pltpu.VMEM((2, 27, 8, 128), F32),
            pltpu.VMEM((2, 2, 16, 8, 128), F32),
            pltpu.VMEM((2, 16, 8, 128), F32),
            pltpu.VMEM((16, 2, 8, 128), F32),
            pltpu.VMEM((16, 2, 8, 128), F32),
            pltpu.VMEM((8, 16, 128), BF16),
            pltpu.VMEM((8, 16, 128), BF16),
            pltpu.VMEM((C, 256), F32),
            pltpu.VMEM((256, 256), BF16),
            pltpu.VMEM((256, 1024), BF16),
            pltpu.VMEM((96, 128), BF16),
            pltpu.VMEM((32, 128), BF16),
            pltpu.VMEM((256, 224), BF16),
            pltpu.VMEM((48, 64), BF16),
            pltpu.VMEM((256, 160), BF16),
            pltpu.VMEM((48, 48), BF16),
            pltpu.VMEM((256, 256), BF16),
            pltpu.VMEM((384, 256), BF16),
            pltpu.VMEM((384, 256), BF16),
            pltpu.VMEM((768, 640), BF16),
            pltpu.VMEM((304, 128), F32),
            dma((5,)), dma((3, 4)), dma((3, 4)), dma((2,)), dma((2,)),
            dma((2,)), dma((2,)), dma((1,)), dma((1,)), dma((1,)), dma((1,)), dma((1,)), dma((1,)),
        ],
        compiler_params=pltpu.CompilerParams(
            collective_id=0, has_side_effects=True, vmem_limit_bytes=60 * 1024 * 1024
        ),
    )(tissue_kept, filter_one.T, filter_two.T, volume, cotangent)
    act, gin, one, two = pl.pallas_call(
        hand_over,
        out_shape=tuple(jax.ShapeDtypeStruct(*r) for r in results),
        in_specs=[anywhere] * 4,
        out_specs=(anywhere,) * 4,
        scratch_shapes=[dma((4,))],
    )(*(pltpu.with_memory_space_constraint(part, pltpu.VMEM) for part in held))
    return act, gin, one.T, two.T


def solution(mesh):
    field, rows = P("dp", "space", None, None, None), P("dp", None)
    return jax.shard_map(
        on_device,
        mesh=mesh,
        in_specs=(field, P("dp", "space", None), rows, rows, field),
        out_specs=(field, field, rows, rows),
        check_vma=False,
    )
```

```python
import math

import jax
import jax.numpy as jnp
from jax import lax
from jax.experimental import pallas as pl
from jax.experimental.pallas import tpu as pltpu
from jax.sharding import PartitionSpec as P

MESH = pl.DeviceIdType.MESH
F32 = jnp.float32
BF16 = jnp.bfloat16
NN = (((1,), (0,)), ((), ()))
NT = (((1,), (1,)), ((), ()))
TN = (((0,), (0,)), ((), ()))

C = 32
GONE = 64.0
STARTS = (0, 6, 13, 20)


def dot(a, b, dims=NN):
    return lax.dot_general(a, b, dims, preferred_element_type=F32)


def iota(shape, axis):
    return lax.broadcasted_iota(jnp.int32, shape, axis)


def ones_at(cond):
    return jnp.where(cond, 1.0, 0.0).astype(BF16)


def pick(group, parts):
    value = None
    for g in range(len(parts) - 1, -1, -1):
        part = 0.0 if parts[g] is None else parts[g]
        if value is None:
            value = part
        elif not (parts[g] is None and isinstance(value, float)):
            value = jnp.where(group == g, part, value)
    return value


def x_of(row):
    x = row % 16
    return jnp.where(x < 12, x, x - 16)


def logistic(v):
    return 1.0 / (1.0 + jnp.exp(-v))


def layout(h):
    yrows = 32 if h == 3 else 16
    low, high, beyond = 128, 128 + 16 * h, 128 + 32 * h
    return yrows, low, high, beyond, beyond + yrows, beyond + yrows + 16, beyond + yrows + 32


def kernel(
    flags, filter_one, filter_two, volume, cotangent,
    act_out, gin_out, grad_one_out, grad_two_out,
    kept, rows_in, vin, cin, spread, nat, nat_main, nat_z, face_main, face_z, stack_main, stack_z,
    blk, cot, keep, slope, pre, back, shifted, packed, bands, leaving, owned, wide,
    wsend, wrecv, wrows, rep, product, tap_tile, pair_in, crossing, xy_in, z_in, xc_in, final,
    turn, copies8, sel3, sel1, near3, far3, near1, far1, place0, place1, place2, unplace, inside,
    local_sem, halo_send, halo_recv, filt_send, filt_recv,
    pair_send, pair_recv, xy_send, xy_recv, z_send, z_recv, xc_send, xc_recv,
):
    space = lax.axis_index("space")
    dp = lax.axis_index("dp")
    count = lax.axis_size("space")
    rx, ry, rz = space // 4, (space // 2) % 2, space % 2
    bx, pz = space // 16, (space // 2) % 8
    has_below, has_above = rx > 0, rx < count // 4 - 1
    started = []

    loads = [
        pltpu.make_async_copy(volume.at[0, 0], vin, local_sem.at[0]),
        pltpu.make_async_copy(flags.at[0], kept, local_sem.at[1]),
        pltpu.make_async_copy(filter_one, rows_in.at[0], local_sem.at[2]),
        pltpu.make_async_copy(filter_two, rows_in.at[1], local_sem.at[3]),
        pltpu.make_async_copy(cotangent.at[0, 0], cin, local_sem.at[4]),
    ]
    for load in loads:
        load.start()

    def send(src, dst, sems, at, peer):
        pltpu.make_async_remote_copy(
            src_ref=src, dst_ref=dst, send_sem=sems[0].at[at], recv_sem=sems[1].at[at],
            device_id=peer, device_id_type=MESH,
        ).start()

    def batch(ref, sems, at):
        copy = pltpu.make_async_remote_copy(
            src_ref=ref, dst_ref=ref, send_sem=sems[0].at[at], recv_sem=sems[1].at[at],
            device_id=dp_peers[0], device_id_type=MESH,
        )
        started.append(copy)
        return copy

    base = space - 2 * ry - rz
    column = (space, base + 2 * (1 - ry) + rz, base + 2 * ry + (1 - rz), base + 2 * (1 - ry) + (1 - rz))
    below = [lax.rem(d - 4 + count, count) for d in column]
    above = [lax.rem(d + 4, count) for d in column]
    xy = bx * 4 + dp
    hops = lambda d: min(d, 4 - d)
    steps = sorted([(i // 4, i % 4) for i in range(1, 16)], key=lambda d: -hops(d[0]) - hops(d[1]))
    xy_slots = [lax.rem(bx + i, 4) * 4 + lax.rem(dp + j, 4) for i, j in steps]
    xy_peers = [((s // 4) * 16 + lax.rem(space, 16), s % 4) for s in xy_slots]
    z_peers = [(bx * 16 + 2 * lax.rem(pz + k, 8) + rz, dp) for k in (4, 3, 5, 2, 6, 1, 7)]
    xc = rz * 4 + bx
    steps = ((1, 2), (0, 2), (1, 1), (1, 3), (0, 1), (0, 3), (1, 0))
    xc_slots = [lax.rem(rz + i, 2) * 4 + lax.rem(bx + j, 4) for i, j in steps]
    xc_peers = [((s % 4) * 16 + 2 * pz + s // 4, dp) for s in xc_slots]
    dp_peers = [(space, lax.rem(dp + k, 4)) for k in range(1, 4)]

    barrier = pltpu.get_barrier_semaphore()
    greeted = [(d, dp) for d in column[1:]] + [(d, dp) for d in below + above] + xy_peers + z_peers + xc_peers
    for peer in greeted:
        pl.semaphore_signal(barrier, inc=1, device_id=peer, device_id_type=MESH)

    group = iota((1, 128), 1) // C

    row, col = iota((256, 256), 0), iota((256, 256), 1)
    y, z = row % 16, row // 16
    turn[...] = ones_at(col == 16 * jnp.where(ry == 0, y, 15 - y) + jnp.where(rz == 0, z, 15 - z))
    row, col = iota((256, 128), 0), iota((256, 128), 1)
    for x in range(8):
        copies8[:, 128 * x : 128 * x + 128] = ones_at(row == 8 * (col % C) + x)

    def faces_of(h):
        row, col = iota((32 * h, 128), 0), iota((32 * h, 128), 1)
        y, x = col // 8, col % 8
        return ones_at(
            ((x < h) & (row == h * y + x)) | ((x >= 8 - h) & (row == 16 * h + h * y + x - (8 - h)))
        )

    sel3[...] = faces_of(3)

    cell = iota((1, 256), 1)
    tile = 2 * (cell // 128) + (cell % 16) // 8

    def turn_in(f, field):
        cells = dot(turn[...], field.astype(BF16), NT).astype(BF16)
        spread[...] = dot(cells, copies8[...])
        for x in range(8):
            for w in range(5):
                layers = [4 * w + g for g in range(4)] if w < 4 else [None, 15, 14, 13]
                parts = [None if l is None else spread[16 * l : 16 * l + 16, 128 * x : 128 * x + 128] for l in layers]
                nat[w, pl.ds(x, 16, stride=8), :] = pick(group, parts)
        return jnp.concatenate([nat[w] for w in range(5)], axis=1).astype(BF16)

    def show(f, h, sel, field):
        main, last = field[:, :512], field[:, 512:]
        nat_main[f] = main
        nat_z[f] = last
        stack_main[f, 0:128] = main
        faces = dot(sel, field).astype(BF16)
        for side in range(2):
            face_main[f, side, 0 : 16 * h] = faces[16 * h * side : 16 * h * side + 16 * h, :512]
            face_z[f, side, 0 : 16 * h] = faces[16 * h * side : 16 * h * side + 16 * h, 512:]

    def give(f, h):
        yrows, low, high, beyond, corner_low, corner_high, total = layout(h)
        sems = (halo_send, halo_recv)

        def add(src, dst, d, kind):
            send(src, dst, sems, (f, kind), (d, dp))

        ends = ((1, low, corner_low, above), (0, high, corner_high, below))
        for side, at, _, to in ends:
            add(face_z.at[f, side, 0 : 16 * h], stack_z.at[f, at : at + 16 * h], to[2], 1)
        for side, _, corner, to in ends:
            add(face_z.at[f, side, 16 * h - 16 : 16 * h], stack_z.at[f, corner : corner + 16], to[3], 3)
        for side, at, _, to in ends:
            add(face_main.at[f, side, 0 : 16 * h], stack_main.at[f, at : at + 16 * h], to[0], 0)
        for side, _, corner, to in ends:
            add(face_main.at[f, side, 16 * h - 16 : 16 * h], stack_main.at[f, corner : corner + 16], to[1], 2)
        add(nat_z.at[f], stack_z.at[f, 0:128], column[2], 1)
        add(nat_main.at[f, 128 - yrows : 128], stack_main.at[f, beyond : beyond + yrows], column[1], 2)
        add(nat_z.at[f, 128 - yrows : 128], stack_z.at[f, beyond : beyond + yrows], column[3], 3)
        near = [batch(stack_main.at[f, 128:beyond], sems, (f, 0)), batch(stack_z.at[f, 0:beyond], sems, (f, 1))]
        far = [
            batch(stack_main.at[f, beyond:total], sems, (f, 2)), batch(stack_z.at[f, beyond:total], sems, (f, 3))
        ]
        return near, far

    def assemble(h):
        yrows, low, high, beyond, corner_low, corner_high, total = layout(h)
        row, col = iota((256, beyond), 0), iota((256, beyond), 1)
        y, x = row // 16, x_of(row)
        at = jnp.where((x >= 0) & (x < 8), 8 * y + x, -1)
        at = jnp.where((x < 0) & (x >= -h), low + h * y + x + h, at)
        at = jnp.where((x >= 8) & (x < 8 + h), high + h * y + x - 8, at)
        near = ones_at(at == col)
        row, col = iota((48, total - beyond), 0), iota((48, total - beyond), 1)
        y, x = row // 16, x_of(row)
        there, skip = 15 - y, 16 * h - 16
        at = jnp.where((x >= 0) & (x < 8), 8 * (there - (16 - yrows // 8)) + x, -1)
        at = jnp.where((x < 0) & (x >= -h), yrows + h * there + x + h - skip, at)
        at = jnp.where((x >= 8) & (x < 8 + h), yrows + 16 + h * there + x - 8 - skip, at)
        return near, ones_at((at == col) & (y < h))

    def take(f, h, rows, part, moves, into):
        for move in moves:
            move.wait_recv()
        beyond, total = layout(h)[3], layout(h)[-1]
        start, end = ((0, beyond), (beyond, total))[part]
        pieces = jnp.concatenate([stack_main[f, start:end], stack_z[f, start:end]], axis=1)
        whole = dot(rows[...], pieces).astype(BF16)
        to = slice(256 * part, 256 + 48 * part)
        into[0, to] = dot(whole[:, 0:256], place0[...])
        into[1, to] = dot(whole[:, 128:512], place1[...])
        into[2, to] = dot(whole[:, 256:640], place2[...])

    def halves(value):
        return value[:, :128], value[:, 128:]

    last_own = {}

    def put(f, b, v, y, value):
        lanes = slice(128 * v, 128 * v + 128)
        for ox, moved in enumerate((pltpu.roll(value, 1, 0), value, pltpu.roll(value, 15, 0))):
            if f < 2:
                shifted[f, ox, b, 16 * y + 16 : 16 * y + 32, lanes] = moved.astype(BF16)
            if y <= 16:
                key = (f, ox, b, v)
                before = last_own[key] if y > 0 else jnp.zeros((8, 128), F32)
                last_own[key] = moved[0:8]
                at = 8 * (y - 1) if y % 2 == 1 else 128 + 8 * y
                packed[f, ox, b, at : at + 16, lanes] = jnp.concatenate([before, moved[0:8]], axis=0).astype(BF16)

    def put_all(f, y, parts):
        for b in range(3):
            lo, hi = parts[b]
            lo = jnp.where(group == 0, pltpu.roll(parts[b - 1][1], 64, 1) if b > 0 else 0.0, lo)
            hi = jnp.where(group == 3, pltpu.roll(parts[b + 1][0], 64, 1) if b < 2 else 0.0, hi)
            put(f, b, 0, y, lo)
            put(f, b, 1, y, hi)

    def own_inputs(f, ox, oy, y0, ny):
        at = 8 * y0 + (128 if oy == 0 else 0 if oy == 1 else 144)
        return packed[f, ox, :, at : at + 8 * ny].reshape(24 * ny, 256)

    def inputs_of(f, ox, oy, ny):
        return shifted[f, ox, :, 16 * oy : 16 * oy + 16 * ny].reshape(48 * ny, 256)

    def conv(f, y0, ny):
        lhs = jnp.concatenate([inputs_of(f, ox, y0 + oy, ny) for ox in range(3) for oy in range(3)], axis=1)
        pre[f, :, 16 * y0 : 16 * y0 + 16 * ny] = dot(lhs, bands[f].reshape(9 * 256, 256)).reshape(3, 16 * ny, 256)

    def conv_back(f, slot, y0, ny):
        lhs = jnp.concatenate([own_inputs(f, ox, oy, y0, ny) for ox in range(3) for oy in range(3)], axis=1)
        rhs = jnp.concatenate([bands[slot, t] for t in range(9)], axis=1)
        back[f - 2, :, 8 * y0 : 8 * y0 + 8 * ny] = dot(lhs, rhs, NT).reshape(3, 8 * ny, 256)

    def send_rows(f, rows):
        square = ones_at(iota((216, 216), 0) == iota((216, 216), 1))
        four = jnp.concatenate([rows[...]] * 4, axis=0)
        full = jnp.concatenate([dot(square, four, NT), jnp.zeros((8, 128), F32)], axis=0)
        lined = pick(group, [full[56 * g : 56 * g + 56] for g in range(4)])
        lined = jnp.concatenate([lined, jnp.zeros((8, 128), F32)], axis=0).astype(BF16)
        wsend[f] = lined
        wrecv[f, dp] = lined

    def share_rows(f):
        sems = (filt_send, filt_recv)
        for peer in dp_peers:
            send(wsend.at[f], wrecv.at[f, dp], sems, f, peer)
        return [batch(wrecv.at[f, 0:3], sems, f)]

    def filter_rows(f):
        for g8 in range(108):
            src, rr = g8 // 27, g8 % 27
            g, r = rr // 7, rr % 7
            part = wrecv[f, src, 16 * (r // 2) : 16 * (r // 2) + 16].astype(F32)[8 * (r % 2) : 8 * (r % 2) + 8]
            wrows[8 * g8 : 8 * g8 + 8] = jnp.where(group == g, part, 0.0)
        again = ones_at(iota((128, 128), 0) % C == iota((128, 128), 1) % C)
        rep[f] = dot(wrows[...].astype(BF16), again).reshape(27, C, 128)

    def tap(ox, oy, oz):
        ty = oy if oy == 1 else jnp.where(ry == 0, oy, 2 - oy)
        tz = oz if oz == 1 else jnp.where(rz == 0, oz, 2 - oz)
        return 9 * ox + 3 * ty + tz

    def band(f):
        for ox in range(3):
            for oy in range(3):
                taps = [rep[f, tap(ox, oy, oz)] for oz in range(3)]
                for v in range(2):
                    for zi in range(8):
                        parts = []
                        for g in range(4):
                            zo = 4 * v + g
                            parts.append(taps[zi - zo + 1] if 1 <= zo <= 6 and abs(zi - zo) <= 1 else None)
                        if any(p is not None for p in parts):
                            value = pick(group, parts).astype(BF16)
                        else:
                            value = jnp.zeros((C, 128), BF16)
                        bands[f, 3 * ox + oy, C * zi : C * zi + C, 128 * v : 128 * v + 128] = value

    def band_back(f):
        for sx in range(3):
            for sy in range(3):
                taps = [rep[f, tap(2 - sx, 2 - sy, oz)] for oz in range(3)]
                for v in range(2):
                    for zo in range(8):
                        parts = []
                        for g in range(4):
                            zi = 4 * v + g
                            parts.append(taps[zo - zi + 1] if 1 <= zo <= 6 and abs(zi - zo) <= 1 else None)
                        if any(p is not None for p in parts):
                            value = pick(group, parts).astype(BF16)
                        else:
                            value = jnp.zeros((C, 128), BF16)
                        bands[2 + f, 3 * sx + sy, C * zo : C * zo + C, 128 * v : 128 * v + 128] = value

    def natural(blocked):
        return dot(jnp.concatenate([blocked[b] for b in range(3)], axis=1), unplace[...])

    def depart(field, out):
        for w in range(4):
            nat[w] = field[:, 128 * w : 128 * w + 128]
        for x in range(8):
            for w in range(4):
                value = nat[w, pl.ds(x, 16, stride=8), :]
                for g in range(4):
                    at = 16 * (4 * w + g)
                    wide[at : at + 16, 128 * x : 128 * x + 128] = jnp.where(group == g, value, 0.0).astype(BF16)
        cells = dot(copies8[...], wide[...], NT).astype(BF16)
        out[0, 0] = dot(cells, turn[...]).reshape(C, 8, 256).astype(BF16)

    def filter_gradient(slot, f):
        gradient = owned[f].reshape(384, 256)
        odd, high = group % 2 == 1, group >= 2
        for t in range(9):
            product[slot, t] = dot(gradient, own_inputs(f, t // 3, t % 3, 0, 16), TN)
            for oz in range(3):
                a = []
                for j in range(4):
                    sides = []
                    for v in range(2):
                        parts = []
                        for g in range(4):
                            zo = 4 * v + g - (oz - 1)
                            at = zo * C + 8 * j
                            parts.append(product[slot, t, at : at + 8, 128 * v : 128 * v + 128] if 1 <= zo <= 6 else None)
                        sides.append(pick(group, parts))
                    a.append(sides[0] + sides[1])
                pairs = [
                    jnp.where(odd, a[i + 1], a[i]) + pltpu.roll(jnp.where(odd, a[i], a[i + 1]), 32, 1) for i in (0, 2)
                ]
                tap_tile[slot, tap(t // 3, t % 3, oz)] = jnp.where(high, pairs[1], pairs[0]) + pltpu.roll(
                    jnp.where(high, pairs[0], pairs[1]), 64, 1
                )

    loads[0].wait()
    loads[1].wait()
    flag = kept[...].astype(F32)
    kept_cells = jnp.zeros((1, 256), F32)
    for b in range(4):
        kept_cells = jnp.where(tile == b, flag[:, b : b + 1], kept_cells)
    field = jnp.where(kept_cells > 0.5, vin[...].astype(F32).reshape(256, 256), GONE)
    field = turn_in(0, field)
    show(0, 3, sel3[...], field)
    pl.semaphore_wait(barrier, len(greeted))
    volume_near, volume_far = give(0, 3)
    loads[2].wait()
    loads[3].wait()
    send_rows(0, rows_in.at[0])
    row_moves = [share_rows(0)]
    send_rows(1, rows_in.at[1])
    row_moves.append(share_rows(1))

    near3[...], far3[...] = assemble(3)
    k, n = iota((256, 256), 0), iota((256, 256), 1)
    place0[...] = ones_at(n - k == C)
    k, n = iota((384, 256), 0), iota((384, 256), 1)
    place1[...] = ones_at(k - n == C)
    place2[...] = ones_at(k - n == jnp.where(n < 160, 96, 128))
    sel1[...] = faces_of(1)
    loads[4].wait()
    show(1, 1, sel1[...], turn_in(1, cin[...].astype(F32).reshape(256, 256)))
    cot_near, cot_far = give(1, 1)
    near1[...], far1[...] = assemble(1)
    for b in range(3):
        k, n = iota((256, 640), 0), iota((256, 640), 1)
        zi, z = k // C, 6 * b + k // C - 1
        good = (zi >= 1) & (zi <= 6) & (z < 16) & (k % C == n % C)
        unplace[256 * b : 256 * b + 256] = ones_at(
            good & (((n < 512) & (n // C == z)) | ((n >= 544) & (16 - (n // C - 16) == z)))
        )
    x = x_of(iota((304, 128), 0))
    inside[...] = jnp.where(((x < 0) & ~has_below) | ((x >= 8) & ~has_above), 0.0, 1.0)
    for f in range(2):
        for ox in range(3):
            for b in range(3):
                shifted[f, ox, b, 0:16] = jnp.zeros((16, 256), BF16)

    for f in range(2):
        for move in row_moves[f]:
            move.wait_recv()
        filter_rows(f)
        band(f)
        band_back(f)

    take(0, 3, near3, 0, volume_near, blk)

    def first(y):
        rows = slice(16 * y, 16 * y + 16)
        here = inside[rows, :]
        for b in range(3):
            for v in range(2):
                lanes = slice(128 * v, 128 * v + 128)
                value = blk[b, rows, lanes]
                kept_here = jnp.where(value == GONE, 0.0, here)
                keep[b, rows, lanes] = kept_here
                put(0, b, v, y, value * kept_here)

    def second(y):
        rows = slice(16 * y, 16 * y + 16)
        parts = []
        for b in range(3):
            value, there = pre[0, b, rows, :], keep[b, rows, :]
            gate = logistic(value)
            act = value * gate
            if y < 16:
                slope[b, 8 * y : 8 * y + 8, :] = ((gate + act * (1.0 - gate)) * there)[0:8]
            parts.append(halves(act * there))
        put_all(1, y, parts)

    own_lanes = [1.0, 1.0, jnp.where(iota((1, 256), 1) < 160, 1.0, 0.0)]

    def third(y):
        rows = slice(16 * y, 16 * y + 16)
        parts = []
        for b in range(3):
            value, there = pre[1, b, rows, :], keep[b, rows, :]
            gate = logistic(value)
            act = value * gate
            grad = cot[b, rows, :] * there * (gate + act * (1.0 - gate))
            parts.append(halves(grad))
            if y < 16:
                key, mine = ("own", b), ((act * there)[0:8], (grad * own_lanes[b])[0:8])
                if y % 2 == 1:
                    pair = [jnp.concatenate(p, axis=0).astype(BF16) for p in zip(last_own[key], mine)]
                    leaving[b, 8 * y - 8 : 8 * y + 8, :] = pair[0]
                    owned[1, b, 8 * y - 8 : 8 * y + 8, :] = pair[1]
                last_own[key] = mine
        put_all(2, y, parts)

    def fourth(y):
        rows = slice(8 * y, 8 * y + 16)
        for b in range(3):
            owned[0, b, rows, :] = (back[0, b, rows, :] * slope[b, rows, :] * own_lanes[b]).astype(BF16)

    def run(body, first_y, end, step=1):
        for y in range(first_y, end, step):
            body(y)

    run(first, 0, 8)
    conv(0, 0, 6)
    run(first, 8, 16)
    conv(0, 6, 6)
    run(second, 0, 6)
    take(0, 3, far3, 1, volume_far, blk)
    run(first, 16, 19)
    conv(0, 12, 6)
    run(second, 6, 12)
    conv(1, 0, 6)
    run(second, 12, 18)
    conv(1, 6, 6)
    take(1, 1, near1, 0, cot_near, cot)
    run(third, 0, 6)
    conv(1, 12, 5)
    run(third, 6, 12)
    run(third, 12, 16)
    conv_back(2, 3, 0, 8)
    take(1, 1, far1, 1, cot_far, cot)
    run(third, 16, 17)
    conv_back(2, 3, 8, 8)
    run(fourth, 0, 16, 2)
    filter_gradient(0, 1 - rz)
    send(tap_tile.at[0], pair_in, (pair_send, pair_recv), 0, (column[2], dp))
    pair = batch(pair_in, (pair_send, pair_recv), 0)
    filter_gradient(1, rz)
    show(2, 1, sel1[...], natural(owned[0]).astype(BF16))
    grad_near, grad_far = give(2, 1)
    pair.wait_recv()
    for s in range(16):
        for j in range(2):
            source = STARTS[s % 4] + 2 * (s // 4) + j
            crossing[s, j] = tap_tile[1, source] + pair_in[source] if source < 27 else jnp.zeros((8, 128), F32)
    for s, peer in zip(xy_slots, xy_peers):
        send(crossing.at[s], xy_in.at[xy], (xy_send, xy_recv), 0, peer)
    xy_moves = [batch(xy_in.at[0:15], (xy_send, xy_recv), 0)]
    xy_in[xy] = crossing[xy]

    depart(natural(leaving[...]), act_out)
    for move in xy_moves:
        move.wait_recv()
    total = xy_in[0]
    for s in range(1, 16):
        total = total + xy_in[s]
    z_in[pz] = total.reshape(16, 128).astype(BF16)
    for peer in z_peers:
        send(z_in.at[pz], z_in.at[pz], (z_send, z_recv), 0, peer)
    z_moves = [batch(z_in.at[0:7], (z_send, z_recv), 0)]

    take(2, 1, near1, 0, grad_near, blk)

    def fifth(y):
        rows = slice(16 * y, 16 * y + 16)
        here = inside[rows, :]
        for b in range(3):
            for v in range(2):
                put(3, b, v, y, blk[b, rows, 128 * v : 128 * v + 128] * here)

    def sixth(y):
        rows = slice(8 * y, 8 * y + 16)
        for b in range(3):
            there = [keep[b, 16 * i : 16 * i + 8, :] for i in (y, y + 1)]
            leaving[b, rows, :] = (back[1, b, rows, :] * jnp.concatenate(there, axis=0)).astype(BF16)

    run(fifth, 0, 16)
    conv_back(3, 2, 0, 8)
    take(2, 1, far1, 1, grad_far, blk)
    run(fifth, 16, 17)
    conv_back(3, 2, 8, 8)
    run(sixth, 0, 16, 2)
    depart(natural(leaving[...]), gin_out)

    for move in z_moves:
        move.wait_recv()
    total = z_in[0].astype(F32)
    for s in range(1, 8):
        total = total + z_in[s].astype(F32)
    xc_in[xc] = (total * (1.0 / math.sqrt(4 * count * 2048))).astype(BF16)
    for peer in xc_peers:
        send(xc_in.at[xc], xc_in.at[xc], (xc_send, xc_recv), 0, peer)
    xc_moves = [batch(xc_in.at[0:7], (xc_send, xc_recv), 0)]
    for move in xc_moves:
        move.wait_recv()
    offset = lax.rem(4 - dp, 4) * 8
    for f, out in enumerate((grad_one_out, grad_two_out)):
        for j in range(4):
            for w in range(2):
                parts = []
                for g in range(4):
                    value = xc_in[4 * f + 2 * w + g // 2].astype(F32)[8 * (g % 2) : 8 * (g % 2) + 8]
                    parts.append(value if g == j else pltpu.roll(value, 32 * ((g - j) % 4), 1))
                final[8 * j : 8 * j + 8, 128 * w : 128 * w + 128] = pick(group, parts)
        out[...] = pltpu.roll(final[...], 256 - offset, 1)[:, :216]

    for copy in started:
        copy.wait_send()


def hand_over(*refs):
    copies = [pltpu.make_async_copy(refs[i], refs[4 + i], refs[8].at[i]) for i in range(4)]
    for copy in copies:
        copy.start()
    for copy in copies:
        copy.wait()


def on_device(volume, tissue_kept, filter_one, filter_two, cotangent):
    vmem, anywhere = pl.BlockSpec(memory_space=pltpu.VMEM), pl.BlockSpec(memory_space=pl.ANY)
    dma = pltpu.SemaphoreType.DMA
    field, grad = (volume.shape, BF16), ((C, 216), F32)
    results = (field, field, grad, grad)
    blocked = pltpu.VMEM((3, 304, 256), F32)
    held = pl.pallas_call(
        kernel,
        out_shape=tuple(pltpu.VMEM(*r) for r in results),
        in_specs=[anywhere] * 5,
        out_specs=(vmem,) * 4,
        scratch_shapes=[
            pltpu.VMEM((1, 4), jnp.int32),
            pltpu.VMEM((2, C, 216), BF16),
            pltpu.VMEM((C, 8, 256), BF16),
            pltpu.VMEM((C, 8, 256), BF16),
            pltpu.VMEM((256, 1024), F32),
            pltpu.VMEM((5, 128, 128), F32),
            pltpu.VMEM((3, 128, 512), BF16),
            pltpu.VMEM((3, 128, 128), BF16),
            pltpu.VMEM((3, 2, 48, 512), BF16),
            pltpu.VMEM((3, 2, 48, 128), BF16),
            pltpu.VMEM((3, 288, 512), BF16),
            pltpu.VMEM((3, 288, 128), BF16),
            blocked,
            blocked,
            blocked,
            pltpu.VMEM((3, 128, 256), F32),
            pltpu.VMEM((2, 3, 288, 256), F32),
            pltpu.VMEM((2, 3, 128, 256), F32),
            pltpu.VMEM((2, 3, 3, 320, 256), BF16),
            pltpu.VMEM((4, 3, 3, 272, 256), BF16),
            pltpu.VMEM((4, 9, 256, 256), BF16),
            pltpu.VMEM((3, 128, 256), BF16),
            pltpu.VMEM((2, 3, 128, 256), BF16),
            pltpu.VMEM((256, 1024), BF16),
            pltpu.VMEM((2, 64, 128), BF16),
            pltpu.VMEM((2, 4, 64, 128), BF16),
            pltpu.VMEM((864, 128), F32),
            pltpu.VMEM((2, 27, C, 128), F32),
            pltpu.VMEM((2, 9, 256, 256), F32),
            pltpu.VMEM((2, 27, 8, 128), F32),
            pltpu.VMEM((27, 8, 128), F32),
            pltpu.VMEM((16, 2, 8, 128), F32),
            pltpu.VMEM((16, 2, 8, 128), F32),
            pltpu.VMEM((8, 16, 128), BF16),
            pltpu.VMEM((8, 16, 128), BF16),
            pltpu.VMEM((C, 256), F32),
            pltpu.VMEM((256, 256), BF16),
            pltpu.VMEM((256, 1024), BF16),
            pltpu.VMEM((96, 128), BF16),
            pltpu.VMEM((32, 128), BF16),
            pltpu.VMEM((256, 224), BF16),
            pltpu.VMEM((48, 64), BF16),
            pltpu.VMEM((256, 160), BF16),
            pltpu.VMEM((48, 48), BF16),
            pltpu.VMEM((256, 256), BF16),
            pltpu.VMEM((384, 256), BF16),
            pltpu.VMEM((384, 256), BF16),
            pltpu.VMEM((768, 640), BF16),
            pltpu.VMEM((304, 128), F32),
            dma((5,)), dma((3, 4)), dma((3, 4)), dma((2,)), dma((2,)),
            dma((1,)), dma((1,)), dma((1,)), dma((1,)), dma((1,)), dma((1,)), dma((1,)), dma((1,)),
        ],
        compiler_params=pltpu.CompilerParams(
            collective_id=0, has_side_effects=True, vmem_limit_bytes=60 * 1024 * 1024
        ),
    )(tissue_kept, filter_one.T, filter_two.T, volume, cotangent)
    act, gin, one, two = pl.pallas_call(
        hand_over,
        out_shape=tuple(jax.ShapeDtypeStruct(*r) for r in results),
        in_specs=[anywhere] * 4,
        out_specs=(anywhere,) * 4,
        scratch_shapes=[dma((4,))],
    )(*(pltpu.with_memory_space_constraint(part, pltpu.VMEM) for part in held))
    return act, gin, one.T, two.T


def solution(mesh):
    field, rows = P("dp", "space", None, None, None), P("dp", None)
    return jax.shard_map(
        on_device,
        mesh=mesh,
        in_specs=(field, P("dp", "space", None), rows, rows, field),
        out_specs=(field, field, rows, rows),
        check_vma=False,
    )
```

```python
import math

import jax
import jax.numpy as jnp
from jax import lax
from jax.experimental import pallas as pl
from jax.experimental.pallas import tpu as pltpu
from jax.sharding import PartitionSpec as P

MESH = pl.DeviceIdType.MESH
F32 = jnp.float32
BF16 = jnp.bfloat16
NN = (((1,), (0,)), ((), ()))
NT = (((1,), (1,)), ((), ()))
TN = (((0,), (0,)), ((), ()))

C = 32
GONE = 64.0
STARTS = (0, 6, 13, 20)


def dot(a, b, dims=NN):
    return lax.dot_general(a, b, dims, preferred_element_type=F32)


def iota(shape, axis):
    return lax.broadcasted_iota(jnp.int32, shape, axis)


def ones_at(cond):
    return jnp.where(cond, 1.0, 0.0).astype(BF16)


def pick(group, parts):
    value = None
    for g in range(len(parts) - 1, -1, -1):
        part = 0.0 if parts[g] is None else parts[g]
        if value is None:
            value = part
        elif not (parts[g] is None and isinstance(value, float)):
            value = jnp.where(group == g, part, value)
    return value


def x_of(row):
    x = row % 16
    return jnp.where(x < 12, x, x - 16)


def logistic(v):
    return 1.0 / (1.0 + jnp.exp(-v))


def layout(h):
    yrows = 32 if h == 3 else 16
    low, high, beyond = 128, 128 + 16 * h, 128 + 32 * h
    return yrows, low, high, beyond, beyond + yrows, beyond + yrows + 16, beyond + yrows + 32


def kernel(
    flags, filter_one, filter_two, volume, cotangent,
    act_out, gin_out, grad_one_out, grad_two_out,
    kept, rows_in, vin, cin, spread, nat, nat_main, nat_z, face_main, face_z, stack_main, stack_z,
    blk, cot, keep, slope, pre, back, shifted, packed, bands, leaving, owned, wide,
    wsend, wrecv, wrows, rep, product, tap_tile, pair_in, crossing, xy_in, z_in, xc_in, final,
    turn, copies8, sel3, sel1, near3, far3, near1, far1, place0, place1, place2, unplace, inside,
    local_sem, halo_send, halo_recv, filt_send, filt_recv,
    pair_send, pair_recv, xy_send, xy_recv, z_send, z_recv, xc_send, xc_recv,
):
    space = lax.axis_index("space")
    dp = lax.axis_index("dp")
    count = lax.axis_size("space")
    rx, ry, rz = space // 4, (space // 2) % 2, space % 2
    bx, pz = space // 16, (space // 2) % 8
    has_below, has_above = rx > 0, rx < count // 4 - 1
    started = []

    loads = [
        pltpu.make_async_copy(volume.at[0, 0], vin, local_sem.at[0]),
        pltpu.make_async_copy(flags.at[0], kept, local_sem.at[1]),
        pltpu.make_async_copy(filter_one, rows_in.at[0], local_sem.at[2]),
        pltpu.make_async_copy(filter_two, rows_in.at[1], local_sem.at[3]),
        pltpu.make_async_copy(cotangent.at[0, 0], cin, local_sem.at[4]),
    ]
    for load in loads:
        load.start()

    def send(src, dst, sems, at, peer):
        pltpu.make_async_remote_copy(
            src_ref=src, dst_ref=dst, send_sem=sems[0].at[at], recv_sem=sems[1].at[at],
            device_id=peer, device_id_type=MESH,
        ).start()

    def batch(ref, sems, at):
        copy = pltpu.make_async_remote_copy(
            src_ref=ref, dst_ref=ref, send_sem=sems[0].at[at], recv_sem=sems[1].at[at],
            device_id=dp_peers[0], device_id_type=MESH,
        )
        started.append(copy)
        return copy

    base = space - 2 * ry - rz
    column = (space, base + 2 * (1 - ry) + rz, base + 2 * ry + (1 - rz), base + 2 * (1 - ry) + (1 - rz))
    below = [lax.rem(d - 4 + count, count) for d in column]
    above = [lax.rem(d + 4, count) for d in column]
    xy = bx * 4 + dp
    hops = lambda d: min(d, 4 - d)
    steps = sorted([(i // 4, i % 4) for i in range(1, 16)], key=lambda d: -hops(d[0]) - hops(d[1]))
    xy_slots = [lax.rem(bx + i, 4) * 4 + lax.rem(dp + j, 4) for i, j in steps]
    xy_peers = [((s // 4) * 16 + lax.rem(space, 16), s % 4) for s in xy_slots]
    z_peers = [(bx * 16 + 2 * lax.rem(pz + k, 8) + rz, dp) for k in (4, 3, 5, 2, 6, 1, 7)]
    xc = rz * 4 + bx
    steps = ((1, 2), (0, 2), (1, 1), (1, 3), (0, 1), (0, 3), (1, 0))
    xc_slots = [lax.rem(rz + i, 2) * 4 + lax.rem(bx + j, 4) for i, j in steps]
    xc_peers = [((s % 4) * 16 + 2 * pz + s // 4, dp) for s in xc_slots]
    dp_peers = [(space, lax.rem(dp + k, 4)) for k in range(1, 4)]

    barrier = pltpu.get_barrier_semaphore()
    greeted = [(column[3], dp)] + [(d, dp) for d in below + above] + xy_peers + z_peers + xc_peers
    for peer in greeted:
        pl.semaphore_signal(barrier, inc=1, device_id=peer, device_id_type=MESH)

    group = iota((1, 128), 1) // C

    row, col = iota((256, 256), 0), iota((256, 256), 1)
    y, z = row % 16, row // 16
    turn[...] = ones_at(col == 16 * jnp.where(ry == 0, y, 15 - y) + jnp.where(rz == 0, z, 15 - z))
    row, col = iota((256, 128), 0), iota((256, 128), 1)
    for x in range(8):
        copies8[:, 128 * x : 128 * x + 128] = ones_at(row == 8 * (col % C) + x)

    def faces_of(h):
        row, col = iota((32 * h, 128), 0), iota((32 * h, 128), 1)
        y, x = col // 8, col % 8
        return ones_at(
            ((x < h) & (row == h * y + x)) | ((x >= 8 - h) & (row == 16 * h + h * y + x - (8 - h)))
        )

    sel3[...] = faces_of(3)

    cell = iota((1, 256), 1)
    tile = 2 * (cell // 128) + (cell % 16) // 8

    def turn_in(f, field):
        cells = dot(turn[...], field.astype(BF16), NT).astype(BF16)
        spread[...] = dot(cells, copies8[...])
        for x in range(8):
            for w in range(5):
                layers = [4 * w + g for g in range(4)] if w < 4 else [None, 15, 14, 13]
                parts = [None if l is None else spread[16 * l : 16 * l + 16, 128 * x : 128 * x + 128] for l in layers]
                nat[w, pl.ds(x, 16, stride=8), :] = pick(group, parts)
        return jnp.concatenate([nat[w] for w in range(5)], axis=1).astype(BF16)

    def show(f, h, sel, field):
        main, last = field[:, :512], field[:, 512:]
        nat_main[f] = main
        nat_z[f] = last
        stack_main[f, 0:128] = main
        faces = dot(sel, field).astype(BF16)
        for side in range(2):
            face_main[f, side, 0 : 16 * h] = faces[16 * h * side : 16 * h * side + 16 * h, :512]
            face_z[f, side, 0 : 16 * h] = faces[16 * h * side : 16 * h * side + 16 * h, 512:]

    def give(f, h):
        yrows, low, high, beyond, corner_low, corner_high, total = layout(h)
        sems = (halo_send, halo_recv)

        def add(src, dst, d, kind):
            send(src, dst, sems, (f, kind), (d, dp))

        ends = ((1, low, corner_low, above), (0, high, corner_high, below))
        for side, at, _, to in ends:
            add(face_z.at[f, side, 0 : 16 * h], stack_z.at[f, at : at + 16 * h], to[2], 1)
        for side, _, corner, to in ends:
            add(face_z.at[f, side, 16 * h - 16 : 16 * h], stack_z.at[f, corner : corner + 16], to[3], 3)
        for side, at, _, to in ends:
            add(face_main.at[f, side, 0 : 16 * h], stack_main.at[f, at : at + 16 * h], to[0], 0)
        for side, _, corner, to in ends:
            add(face_main.at[f, side, 16 * h - 16 : 16 * h], stack_main.at[f, corner : corner + 16], to[1], 2)
        add(nat_z.at[f], stack_z.at[f, 0:128], column[2], 1)
        add(nat_main.at[f, 128 - yrows : 128], stack_main.at[f, beyond : beyond + yrows], column[1], 2)
        add(nat_z.at[f, 128 - yrows : 128], stack_z.at[f, beyond : beyond + yrows], column[3], 3)
        near = [batch(stack_main.at[f, 128:beyond], sems, (f, 0)), batch(stack_z.at[f, 0:beyond], sems, (f, 1))]
        far = [
            batch(stack_main.at[f, beyond:total], sems, (f, 2)), batch(stack_z.at[f, beyond:total], sems, (f, 3))
        ]
        return near, far

    def assemble(h):
        yrows, low, high, beyond, corner_low, corner_high, total = layout(h)
        row, col = iota((256, beyond), 0), iota((256, beyond), 1)
        y, x = row // 16, x_of(row)
        at = jnp.where((x >= 0) & (x < 8), 8 * y + x, -1)
        at = jnp.where((x < 0) & (x >= -h), low + h * y + x + h, at)
        at = jnp.where((x >= 8) & (x < 8 + h), high + h * y + x - 8, at)
        near = ones_at(at == col)
        row, col = iota((48, total - beyond), 0), iota((48, total - beyond), 1)
        y, x = row // 16, x_of(row)
        there, skip = 15 - y, 16 * h - 16
        at = jnp.where((x >= 0) & (x < 8), 8 * (there - (16 - yrows // 8)) + x, -1)
        at = jnp.where((x < 0) & (x >= -h), yrows + h * there + x + h - skip, at)
        at = jnp.where((x >= 8) & (x < 8 + h), yrows + 16 + h * there + x - 8 - skip, at)
        return near, ones_at((at == col) & (y < h))

    def take(f, h, rows, part, moves, into):
        for move in moves:
            move.wait_recv()
        beyond, total = layout(h)[3], layout(h)[-1]
        start, end = ((0, beyond), (beyond, total))[part]
        pieces = jnp.concatenate([stack_main[f, start:end], stack_z[f, start:end]], axis=1)
        whole = dot(rows[...], pieces).astype(BF16)
        to = slice(256 * part, 256 + 48 * part)
        into[0, to] = dot(whole[:, 0:256], place0[...])
        into[1, to] = dot(whole[:, 128:512], place1[...])
        into[2, to] = dot(whole[:, 256:640], place2[...])

    def halves(value):
        return value[:, :128], value[:, 128:]

    last_own = {}

    def put(f, b, v, y, value):
        lanes = slice(128 * v, 128 * v + 128)
        for ox, moved in enumerate((pltpu.roll(value, 1, 0), value, pltpu.roll(value, 15, 0))):
            if f < 2:
                shifted[f, ox, b, 16 * y + 16 : 16 * y + 32, lanes] = moved.astype(BF16)
            if y <= 16:
                key = (f, ox, b, v)
                before = last_own[key] if y > 0 else jnp.zeros((8, 128), F32)
                last_own[key] = moved[0:8]
                at = 8 * (y - 1) if y % 2 == 1 else 128 + 8 * y
                packed[f, ox, b, at : at + 16, lanes] = jnp.concatenate([before, moved[0:8]], axis=0).astype(BF16)

    def put_all(f, y, parts):
        for b in range(3):
            lo, hi = parts[b]
            lo = jnp.where(group == 0, pltpu.roll(parts[b - 1][1], 64, 1) if b > 0 else 0.0, lo)
            hi = jnp.where(group == 3, pltpu.roll(parts[b + 1][0], 64, 1) if b < 2 else 0.0, hi)
            put(f, b, 0, y, lo)
            put(f, b, 1, y, hi)

    def own_inputs(f, ox, oy, y0, ny):
        at = 8 * y0 + (128 if oy == 0 else 0 if oy == 1 else 144)
        return packed[f, ox, :, at : at + 8 * ny].reshape(24 * ny, 256)

    def inputs_of(f, ox, oy, ny):
        return shifted[f, ox, :, 16 * oy : 16 * oy + 16 * ny].reshape(48 * ny, 256)

    def conv(f, y0, ny):
        lhs = jnp.concatenate([inputs_of(f, ox, y0 + oy, ny) for ox in range(3) for oy in range(3)], axis=1)
        pre[f, :, 16 * y0 : 16 * y0 + 16 * ny] = dot(lhs, bands[f].reshape(9 * 256, 256)).reshape(3, 16 * ny, 256)

    def conv_back(f, slot, y0, ny):
        lhs = jnp.concatenate([own_inputs(f, ox, oy, y0, ny) for ox in range(3) for oy in range(3)], axis=1)
        rhs = jnp.concatenate([bands[slot, t] for t in range(9)], axis=1)
        back[f - 2, :, 8 * y0 : 8 * y0 + 8 * ny] = dot(lhs, rhs, NT).reshape(3, 8 * ny, 256)

    def send_rows(f, rows):
        square = ones_at(iota((216, 216), 0) == iota((216, 216), 1))
        four = jnp.concatenate([rows[...]] * 4, axis=0)
        full = jnp.concatenate([dot(square, four, NT), jnp.zeros((8, 128), F32)], axis=0)
        lined = pick(group, [full[56 * g : 56 * g + 56] for g in range(4)])
        lined = jnp.concatenate([lined, jnp.zeros((8, 128), F32)], axis=0).astype(BF16)
        wsend[f] = lined
        wrecv[f, dp] = lined

    def share_rows(f):
        sems = (filt_send, filt_recv)
        for peer in dp_peers:
            send(wsend.at[f], wrecv.at[f, dp], sems, f, peer)
        return [batch(wrecv.at[f, 0:3], sems, f)]

    def filter_rows(f):
        for g8 in range(108):
            src, rr = g8 // 27, g8 % 27
            g, r = rr // 7, rr % 7
            part = wrecv[f, src, 16 * (r // 2) : 16 * (r // 2) + 16].astype(F32)[8 * (r % 2) : 8 * (r % 2) + 8]
            wrows[8 * g8 : 8 * g8 + 8] = jnp.where(group == g, part, 0.0)
        again = ones_at(iota((128, 128), 0) % C == iota((128, 128), 1) % C)
        rep[f] = dot(wrows[...].astype(BF16), again).reshape(27, C, 128)

    def tap(ox, oy, oz):
        ty = oy if oy == 1 else jnp.where(ry == 0, oy, 2 - oy)
        tz = oz if oz == 1 else jnp.where(rz == 0, oz, 2 - oz)
        return 9 * ox + 3 * ty + tz

    def band(f):
        for ox in range(3):
            for oy in range(3):
                taps = [rep[f, tap(ox, oy, oz)] for oz in range(3)]
                for v in range(2):
                    for zi in range(8):
                        parts = []
                        for g in range(4):
                            zo = 4 * v + g
                            parts.append(taps[zi - zo + 1] if 1 <= zo <= 6 and abs(zi - zo) <= 1 else None)
                        if any(p is not None for p in parts):
                            value = pick(group, parts).astype(BF16)
                        else:
                            value = jnp.zeros((C, 128), BF16)
                        bands[f, 3 * ox + oy, C * zi : C * zi + C, 128 * v : 128 * v + 128] = value

    def band_back(f):
        for sx in range(3):
            for sy in range(3):
                taps = [rep[f, tap(2 - sx, 2 - sy, oz)] for oz in range(3)]
                for v in range(2):
                    for zo in range(8):
                        parts = []
                        for g in range(4):
                            zi = 4 * v + g
                            parts.append(taps[zo - zi + 1] if 1 <= zo <= 6 and abs(zi - zo) <= 1 else None)
                        if any(p is not None for p in parts):
                            value = pick(group, parts).astype(BF16)
                        else:
                            value = jnp.zeros((C, 128), BF16)
                        bands[2 + f, 3 * sx + sy, C * zo : C * zo + C, 128 * v : 128 * v + 128] = value

    def natural(blocked):
        return dot(jnp.concatenate([blocked[b] for b in range(3)], axis=1), unplace[...])

    def depart(field, out):
        for w in range(4):
            nat[w] = field[:, 128 * w : 128 * w + 128]
        for x in range(8):
            for w in range(4):
                value = nat[w, pl.ds(x, 16, stride=8), :]
                for g in range(4):
                    at = 16 * (4 * w + g)
                    wide[at : at + 16, 128 * x : 128 * x + 128] = jnp.where(group == g, value, 0.0).astype(BF16)
        cells = dot(copies8[...], wide[...], NT).astype(BF16)
        out[0, 0] = dot(cells, turn[...]).reshape(C, 8, 256).astype(BF16)

    def filter_gradient(slot, f):
        gradient = owned[f].reshape(384, 256)
        odd, high = group % 2 == 1, group >= 2
        for t in range(9):
            product[slot, t] = dot(gradient, own_inputs(f, t // 3, t % 3, 0, 16), TN)
            for oz in range(3):
                a = []
                for j in range(4):
                    sides = []
                    for v in range(2):
                        parts = []
                        for g in range(4):
                            zo = 4 * v + g - (oz - 1)
                            at = zo * C + 8 * j
                            parts.append(product[slot, t, at : at + 8, 128 * v : 128 * v + 128] if 1 <= zo <= 6 else None)
                        sides.append(pick(group, parts))
                    a.append(sides[0] + sides[1])
                pairs = [
                    jnp.where(odd, a[i + 1], a[i]) + pltpu.roll(jnp.where(odd, a[i], a[i + 1]), 32, 1) for i in (0, 2)
                ]
                tap_tile[slot, tap(t // 3, t % 3, oz)] = jnp.where(high, pairs[1], pairs[0]) + pltpu.roll(
                    jnp.where(high, pairs[0], pairs[1]), 64, 1
                )

    loads[0].wait()
    loads[1].wait()
    flag = kept[...].astype(F32)
    kept_cells = jnp.zeros((1, 256), F32)
    for b in range(4):
        kept_cells = jnp.where(tile == b, flag[:, b : b + 1], kept_cells)
    field = jnp.where(kept_cells > 0.5, vin[...].astype(F32).reshape(256, 256), GONE)
    field = turn_in(0, field)
    show(0, 3, sel3[...], field)
    pl.semaphore_wait(barrier, len(greeted))
    volume_near, volume_far = give(0, 3)
    loads[2].wait()
    loads[3].wait()
    send_rows(0, rows_in.at[0])
    row_moves = [share_rows(0)]
    send_rows(1, rows_in.at[1])
    row_moves.append(share_rows(1))

    near3[...], far3[...] = assemble(3)
    k, n = iota((256, 256), 0), iota((256, 256), 1)
    place0[...] = ones_at(n - k == C)
    k, n = iota((384, 256), 0), iota((384, 256), 1)
    place1[...] = ones_at(k - n == C)
    place2[...] = ones_at(k - n == jnp.where(n < 160, 96, 128))
    near1[...], far1[...] = assemble(1)
    for b in range(3):
        k, n = iota((256, 640), 0), iota((256, 640), 1)
        zi, z = k // C, 6 * b + k // C - 1
        good = (zi >= 1) & (zi <= 6) & (z < 16) & (k % C == n % C)
        unplace[256 * b : 256 * b + 256] = ones_at(
            good & (((n < 512) & (n // C == z)) | ((n >= 544) & (16 - (n // C - 16) == z)))
        )
    x = x_of(iota((304, 128), 0))
    inside[...] = jnp.where(((x < 0) & ~has_below) | ((x >= 8) & ~has_above), 0.0, 1.0)
    for f in range(2):
        for ox in range(3):
            for b in range(3):
                shifted[f, ox, b, 0:16] = jnp.zeros((16, 256), BF16)

    sel1[...] = faces_of(1)
    loads[4].wait()
    show(1, 1, sel1[...], turn_in(1, cin[...].astype(F32).reshape(256, 256)))
    cot_near, cot_far = give(1, 1)
    for f in range(2):
        for move in row_moves[f]:
            move.wait_recv()
        filter_rows(f)
        band(f)
        band_back(f)

    take(0, 3, near3, 0, volume_near, blk)

    def first(y):
        rows = slice(16 * y, 16 * y + 16)
        here = inside[rows, :]
        for b in range(3):
            for v in range(2):
                lanes = slice(128 * v, 128 * v + 128)
                value = blk[b, rows, lanes]
                kept_here = jnp.where(value == GONE, 0.0, here)
                keep[b, rows, lanes] = kept_here
                put(0, b, v, y, value * kept_here)

    def second(y):
        rows = slice(16 * y, 16 * y + 16)
        parts = []
        for b in range(3):
            value, there = pre[0, b, rows, :], keep[b, rows, :]
            gate = logistic(value)
            act = value * gate
            if y < 16:
                slope[b, 8 * y : 8 * y + 8, :] = ((gate + act * (1.0 - gate)) * there)[0:8]
            parts.append(halves(act * there))
        put_all(1, y, parts)

    own_lanes = [1.0, 1.0, jnp.where(iota((1, 256), 1) < 160, 1.0, 0.0)]

    def third(y):
        rows = slice(16 * y, 16 * y + 16)
        parts = []
        for b in range(3):
            value, there = pre[1, b, rows, :], keep[b, rows, :]
            gate = logistic(value)
            act = value * gate
            grad = cot[b, rows, :] * there * (gate + act * (1.0 - gate))
            parts.append(halves(grad))
            if y < 16:
                key, mine = ("own", b), ((act * there)[0:8], (grad * own_lanes[b])[0:8])
                if y % 2 == 1:
                    pair = [jnp.concatenate(p, axis=0).astype(BF16) for p in zip(last_own[key], mine)]
                    leaving[b, 8 * y - 8 : 8 * y + 8, :] = pair[0]
                    owned[1, b, 8 * y - 8 : 8 * y + 8, :] = pair[1]
                last_own[key] = mine
        put_all(2, y, parts)

    def fourth(y):
        rows = slice(8 * y, 8 * y + 16)
        for b in range(3):
            owned[0, b, rows, :] = (back[0, b, rows, :] * slope[b, rows, :] * own_lanes[b]).astype(BF16)

    def run(body, first_y, end, step=1):
        for y in range(first_y, end, step):
            body(y)

    run(first, 0, 8)
    conv(0, 0, 6)
    run(first, 8, 16)
    conv(0, 6, 6)
    run(second, 0, 6)
    take(0, 3, far3, 1, volume_far, blk)
    run(first, 16, 19)
    conv(0, 12, 6)
    run(second, 6, 12)
    conv(1, 0, 6)
    run(second, 12, 18)
    conv(1, 6, 6)
    take(1, 1, near1, 0, cot_near, cot)
    run(third, 0, 6)
    conv(1, 12, 5)
    run(third, 6, 12)
    run(third, 12, 16)
    conv_back(2, 3, 0, 8)
    take(1, 1, far1, 1, cot_far, cot)
    run(third, 16, 17)
    conv_back(2, 3, 8, 8)
    run(fourth, 0, 16, 2)
    filter_gradient(0, 1 - rz)
    send(tap_tile.at[0], pair_in, (pair_send, pair_recv), 0, (column[2], dp))
    pair = batch(pair_in, (pair_send, pair_recv), 0)
    filter_gradient(1, rz)
    show(2, 1, sel1[...], natural(owned[0]).astype(BF16))
    grad_near, grad_far = give(2, 1)
    pair.wait_recv()
    for s in range(16):
        for j in range(2):
            source = STARTS[s % 4] + 2 * (s // 4) + j
            crossing[s, j] = tap_tile[1, source] + pair_in[source] if source < 27 else jnp.zeros((8, 128), F32)
    for s, peer in zip(xy_slots, xy_peers):
        send(crossing.at[s], xy_in.at[xy], (xy_send, xy_recv), 0, peer)
    xy_moves = [batch(xy_in.at[0:15], (xy_send, xy_recv), 0)]
    xy_in[xy] = crossing[xy]

    depart(natural(leaving[...]), act_out)
    for move in xy_moves:
        move.wait_recv()
    total = xy_in[0]
    for s in range(1, 16):
        total = total + xy_in[s]
    z_in[pz] = total.reshape(16, 128).astype(BF16)
    for peer in z_peers:
        send(z_in.at[pz], z_in.at[pz], (z_send, z_recv), 0, peer)
    z_moves = [batch(z_in.at[0:7], (z_send, z_recv), 0)]

    take(2, 1, near1, 0, grad_near, blk)

    def fifth(y):
        rows = slice(16 * y, 16 * y + 16)
        here = inside[rows, :]
        for b in range(3):
            for v in range(2):
                put(3, b, v, y, blk[b, rows, 128 * v : 128 * v + 128] * here)

    def sixth(y):
        rows = slice(8 * y, 8 * y + 16)
        for b in range(3):
            there = [keep[b, 16 * i : 16 * i + 8, :] for i in (y, y + 1)]
            leaving[b, rows, :] = (back[1, b, rows, :] * jnp.concatenate(there, axis=0)).astype(BF16)

    run(fifth, 0, 16)
    conv_back(3, 2, 0, 8)
    take(2, 1, far1, 1, grad_far, blk)
    run(fifth, 16, 17)
    conv_back(3, 2, 8, 8)
    run(sixth, 0, 16, 2)
    depart(natural(leaving[...]), gin_out)

    for move in z_moves:
        move.wait_recv()
    total = z_in[0].astype(F32)
    for s in range(1, 8):
        total = total + z_in[s].astype(F32)
    xc_in[xc] = (total * (1.0 / math.sqrt(4 * count * 2048))).astype(BF16)
    for peer in xc_peers:
        send(xc_in.at[xc], xc_in.at[xc], (xc_send, xc_recv), 0, peer)
    xc_moves = [batch(xc_in.at[0:7], (xc_send, xc_recv), 0)]
    for move in xc_moves:
        move.wait_recv()
    offset = lax.rem(4 - dp, 4) * 8
    for f, out in enumerate((grad_one_out, grad_two_out)):
        for j in range(4):
            for w in range(2):
                parts = []
                for g in range(4):
                    value = xc_in[4 * f + 2 * w + g // 2].astype(F32)[8 * (g % 2) : 8 * (g % 2) + 8]
                    parts.append(value if g == j else pltpu.roll(value, 32 * ((g - j) % 4), 1))
                final[8 * j : 8 * j + 8, 128 * w : 128 * w + 128] = pick(group, parts)
        out[...] = pltpu.roll(final[...], 256 - offset, 1)[:, :216]

    for copy in started:
        copy.wait_send()


def hand_over(*refs):
    copies = [pltpu.make_async_copy(refs[i], refs[4 + i], refs[8].at[i]) for i in range(4)]
    for copy in copies:
        copy.start()
    for copy in copies:
        copy.wait()


def on_device(volume, tissue_kept, filter_one, filter_two, cotangent):
    vmem, anywhere = pl.BlockSpec(memory_space=pltpu.VMEM), pl.BlockSpec(memory_space=pl.ANY)
    dma = pltpu.SemaphoreType.DMA
    field, grad = (volume.shape, BF16), ((C, 216), F32)
    results = (field, field, grad, grad)
    blocked = pltpu.VMEM((3, 304, 256), F32)
    held = pl.pallas_call(
        kernel,
        out_shape=tuple(pltpu.VMEM(*r) for r in results),
        in_specs=[anywhere] * 5,
        out_specs=(vmem,) * 4,
        scratch_shapes=[
            pltpu.VMEM((1, 4), jnp.int32),
            pltpu.VMEM((2, C, 216), BF16),
            pltpu.VMEM((C, 8, 256), BF16),
            pltpu.VMEM((C, 8, 256), BF16),
            pltpu.VMEM((256, 1024), F32),
            pltpu.VMEM((5, 128, 128), F32),
            pltpu.VMEM((3, 128, 512), BF16),
            pltpu.VMEM((3, 128, 128), BF16),
            pltpu.VMEM((3, 2, 48, 512), BF16),
            pltpu.VMEM((3, 2, 48, 128), BF16),
            pltpu.VMEM((3, 288, 512), BF16),
            pltpu.VMEM((3, 288, 128), BF16),
            blocked,
            blocked,
            blocked,
            pltpu.VMEM((3, 128, 256), F32),
            pltpu.VMEM((2, 3, 288, 256), F32),
            pltpu.VMEM((2, 3, 128, 256), F32),
            pltpu.VMEM((2, 3, 3, 320, 256), BF16),
            pltpu.VMEM((4, 3, 3, 272, 256), BF16),
            pltpu.VMEM((4, 9, 256, 256), BF16),
            pltpu.VMEM((3, 128, 256), BF16),
            pltpu.VMEM((2, 3, 128, 256), BF16),
            pltpu.VMEM((256, 1024), BF16),
            pltpu.VMEM((2, 64, 128), BF16),
            pltpu.VMEM((2, 4, 64, 128), BF16),
            pltpu.VMEM((864, 128), F32),
            pltpu.VMEM((2, 27, C, 128), F32),
            pltpu.VMEM((2, 9, 256, 256), F32),
            pltpu.VMEM((2, 27, 8, 128), F32),
            pltpu.VMEM((27, 8, 128), F32),
            pltpu.VMEM((16, 2, 8, 128), F32),
            pltpu.VMEM((16, 2, 8, 128), F32),
            pltpu.VMEM((8, 16, 128), BF16),
            pltpu.VMEM((8, 16, 128), BF16),
            pltpu.VMEM((C, 256), F32),
            pltpu.VMEM((256, 256), BF16),
            pltpu.VMEM((256, 1024), BF16),
            pltpu.VMEM((96, 128), BF16),
            pltpu.VMEM((32, 128), BF16),
            pltpu.VMEM((256, 224), BF16),
            pltpu.VMEM((48, 64), BF16),
            pltpu.VMEM((256, 160), BF16),
            pltpu.VMEM((48, 48), BF16),
            pltpu.VMEM((256, 256), BF16),
            pltpu.VMEM((384, 256), BF16),
            pltpu.VMEM((384, 256), BF16),
            pltpu.VMEM((768, 640), BF16),
            pltpu.VMEM((304, 128), F32),
            dma((5,)), dma((3, 4)), dma((3, 4)), dma((2,)), dma((2,)),
            dma((1,)), dma((1,)), dma((1,)), dma((1,)), dma((1,)), dma((1,)), dma((1,)), dma((1,)),
        ],
        compiler_params=pltpu.CompilerParams(
            collective_id=0, has_side_effects=True, vmem_limit_bytes=60 * 1024 * 1024
        ),
    )(tissue_kept, filter_one.T, filter_two.T, volume, cotangent)
    act, gin, one, two = pl.pallas_call(
        hand_over,
        out_shape=tuple(jax.ShapeDtypeStruct(*r) for r in results),
        in_specs=[anywhere] * 4,
        out_specs=(anywhere,) * 4,
        scratch_shapes=[dma((4,))],
    )(*(pltpu.with_memory_space_constraint(part, pltpu.VMEM) for part in held))
    return act, gin, one.T, two.T


def solution(mesh):
    field, rows = P("dp", "space", None, None, None), P("dp", None)
    return jax.shard_map(
        on_device,
        mesh=mesh,
        in_specs=(field, P("dp", "space", None), rows, rows, field),
        out_specs=(field, field, rows, rows),
        check_vma=False,
    )
```
